32 devices in a mesh: blk: 8 (over y, x, core), grp: 4 (over z).
Axes of the slice: x: 2, y: 2, z: 4, core: 2. Of those that a mesh axis runs over, the one named last changes fastest.
Arguments:
- source_embed: bfloat16 [16384, 768], P(('blk', 'grp')), may hold values from -60 to 60
- target_embed: bfloat16 [1024, 768], P('blk'), may hold values from -18 to 18
- target_init: float32 [1024], P('blk'), may hold values from -6 to 6
- source_logw: float32 [16384], P(('blk', 'grp')), may hold values from -2 to 2
- target_logw: float32 [1024], P('blk'), may hold values from -2 to 2
Outputs:
- row_pot: float32 [16384], P(('blk', 'grp'))
- column_pot: float32 [1024], P('blk')
The draws below stay inside these ranges and needn't reach their ends.
All inputs are finite; a program needn't handle non-finite values.
Results may differ from the reference program's by a relative error of at most 0.0003.
Values may be sent and summed in bfloat16 or wider, within the bound.
No kernel may reach another device: no remote copies, remote signals or barrier semaphores. Data moves between devices by JAX's collectives and lax.ppermute only.
A program may use at most 128 MiB of HBM per device.

```python
import math
import jax
import jax.numpy as jnp
from jax import lax

D = 768
S_DEV = 512
ITERS = 2
S = 16384
NT = 1024


def target_base(key):
    values = jnp.clip(jax.random.normal(jax.random.fold_in(key, 11), (NT, D), jnp.float32), -6.0, 6.0)
    return values


def draw_target_embed(key, part):
    return target_base(key).astype(jnp.bfloat16)


def draw_source_embed(key, part):
    values = jnp.clip(jax.random.normal(jax.random.fold_in(key, 21), (S, D), jnp.float32), -6.0, 6.0)
    return values.astype(jnp.bfloat16)


def steps_of(own_key, dims, pieces, smallest, high):
    level = 1.0
    for axis_at, shards_of in pieces:
        draws = jax.random.uniform(jax.random.fold_in(jax.random.fold_in(own_key, 6), axis_at), (shards_of,), jnp.float32, smallest / len(pieces), high / len(pieces))
        level = level * jnp.repeat(jnp.exp(draws), dims[axis_at] // shards_of).reshape((-1,) + (1,) * (len(dims) - 1 - axis_at))
    return level


def normal_values(rng, dims, width, bound, shards=(), kind=jnp.bfloat16):
    loudness = steps_of(rng, dims, shards, -0.22, 0.18) if shards else 1.0
    values = jax.random.normal(rng, dims, jnp.float32) * width * loudness
    return jnp.minimum(jnp.maximum(values, -bound), bound).astype(kind)


def setup_inputs(seed: int = 0) -> dict:
    key_of = jax.random.split(jax.random.key(seed), 6)
    return {
        "source_embed": draw_source_embed(jax.random.fold_in(key_of[5], 71), 0),
        "target_embed": draw_target_embed(jax.random.fold_in(key_of[5], 71), 0),
        "target_init": normal_values(key_of[2], (NT,), 1.0, 6.0, ((0, 8),), jnp.float32),
        "source_logw": jnp.clip(jax.random.uniform(key_of[3], (S,), jnp.float32, -2.0, 2.0) * steps_of(key_of[3], (S,), ((0, 32),), -0.4, 0.0), -2.0, 2.0),
        "target_logw": jnp.clip(jax.random.uniform(key_of[4], (NT,), jnp.float32, -2.0, 2.0) * steps_of(key_of[4], (NT,), ((0, 8),), -0.4, 0.0), -2.0, 2.0),
    }


epsilon = 0.1
inverse_eps = 10.0

def row_update(cost_matrix, column_pot, row_logw):
    scores = (column_pot[None, :] - cost_matrix) * inverse_eps
    row_top = lax.optimization_barrier(jnp.max(scores, axis=1))
    row_sum = lax.optimization_barrier(jnp.sum(jnp.exp(scores - row_top[:, None]), axis=1))
    return epsilon * row_logw - epsilon * (row_top + jnp.log(row_sum))

def column_partial(cost_matrix, row_pot):
    scores = (row_pot[:, None] - cost_matrix) * inverse_eps
    col_top = lax.optimization_barrier(jnp.max(scores, axis=0))
    col_sum = lax.optimization_barrier(jnp.sum(jnp.exp(scores - col_top[None, :]), axis=0))
    return (col_top, col_sum)

def reference(source_embed, target_embed, target_init, source_logw, target_logw):
    factor = -1.0 / math.sqrt(D)
    slabs = source_embed.reshape(S // S_DEV, S_DEV, D)
    weights = source_logw.reshape(S // S_DEV, S_DEV)

    def half_sweep(column_pot):

        def one_slab(slab_pair):
            slab_rows, slab_logw = slab_pair
            cost_matrix = lax.dot_general(slab_rows, target_embed, (((1,), (1,)), ((), ())), preferred_element_type=jnp.float32) * factor
            row_pot = row_update(cost_matrix, column_pot, slab_logw)
            col_top, col_sum = column_partial(cost_matrix, row_pot)
            return (row_pot, col_top, col_sum)
        row_pot, tops, sums = lax.map(one_slab, (slabs, weights))
        col_peak = lax.optimization_barrier(jnp.max(tops, axis=0))
        col_total = lax.optimization_barrier(jnp.sum(sums * jnp.exp(tops - col_peak[None, :]), axis=0))
        new_column = epsilon * target_logw - epsilon * (col_peak + jnp.log(col_total))
        return (row_pot.reshape(S), new_column)
    column_pot = target_init
    row_pot = jnp.zeros((S,), jnp.float32)
    for iteration in range(ITERS):
        row_pot, column_pot = half_sweep(column_pot)
    return (row_pot, column_pot)
```

```python
import math

import jax
import jax.numpy as jnp
from jax import lax
from jax.sharding import PartitionSpec as P

ITERS = 2
epsilon = 0.1
inverse_eps = 10.0


def partner(index, step, size):
    return index ^ step if size & (size - 1) == 0 else (index + step) % size


def moved(position, step, size):
    return position ^ step if size & (size - 1) == 0 else (position - step) % size


def fetch(array, axis, step, size):
    return lax.ppermute(array, axis, [(partner(i, step, size), i) for i in range(size)])


def gather_positions(array, axis, size):
    if size % 2 or size & (size - 1):
        return [array] + [fetch(array, axis, step, size) for step in range(1, size)]
    even = {0: array}
    for step in range(2, size, 2):
        even[step] = fetch(array, axis, step, size)
    odd = {step + 1: fetch(block, axis, 1, size) for step, block in even.items()}
    return [block for _, block in sorted({**even, **odd}.items())]


def lse(values):
    top = jnp.max(values, axis=0)
    return top + jnp.log(jnp.sum(jnp.exp(values - top[None, :]), axis=0))


def solution(mesh):
    blk, grp = mesh.shape["blk"], mesh.shape["grp"]

    def shards(source_embed, target_embed, target_init, source_logw, target_logw):
        width = target_embed.shape[0]
        factor = -1.0 / math.sqrt(source_embed.shape[1])
        small = jnp.stack([target_init, target_logw])
        smalls = [small] + [fetch(small, "blk", step, blk) for step in range(1, blk)]
        smalls = jnp.concatenate(smalls, axis=1)
        init_all, logw_all = smalls[0], smalls[1]
        targets = jnp.concatenate(gather_positions(target_embed, "blk", blk), axis=0)
        cost = (
            lax.dot_general(
                source_embed, targets, (((1,), (1,)), ((), ())), preferred_element_type=jnp.float32
            )
            * factor
        )

        def column_lse(row_pot):
            scores = (row_pot[:, None] - cost) * inverse_eps
            return lse(scores)

        def over_grp(part):
            return lse(jnp.stack([part] + [fetch(part, "grp", s, grp) for s in range(1, grp)]))

        column_pot = init_all
        for iteration in range(ITERS):
            scores = (column_pot[None, :] - cost) * inverse_eps
            row_top = jnp.max(scores, axis=1)
            row_sum = jnp.sum(jnp.exp(scores - row_top[:, None]), axis=1)
            row_pot = epsilon * source_logw - epsilon * (row_top + jnp.log(row_sum))
            part = column_lse(row_pot)
            if iteration < ITERS - 1:
                blocks = part.reshape(blk, width)
                parts = [part]
                for step in range(1, blk):
                    got = fetch(part, "blk", step, blk).reshape(blk, width)
                    parts.append(
                        jnp.concatenate([got[moved(p, step, blk)] for p in range(blk)])
                    )
                total = over_grp(lse(jnp.stack(parts)))
                column_pot = epsilon * logw_all - epsilon * total
            else:
                blocks = part.reshape(blk, width)
                parts = [blocks[0]]
                for step in range(1, blk):
                    parts.append(fetch(blocks[moved(0, step, blk)], "blk", step, blk))
                total = over_grp(lse(jnp.stack(parts)))
                own_column = epsilon * target_logw - epsilon * total
        return row_pot, own_column

    in_specs = (P(("blk", "grp"), None), P("blk", None), P("blk"), P(("blk", "grp")), P("blk"))
    out_specs = (P(("blk", "grp")), P("blk"))
    return jax.shard_map(shards, mesh=mesh, in_specs=in_specs, out_specs=out_specs, check_vma=False)
```

```python
import math

import jax
import jax.numpy as jnp
from jax import lax
from jax.sharding import PartitionSpec as P

ITERS = 2
epsilon = 0.1
inverse_eps = 10.0


def pieces(value):
    high = lax.reduce_precision(value, 8, 7)
    rest = value - high
    middle = lax.reduce_precision(rest, 8, 7)
    low = rest - middle
    return jnp.stack([high, middle, low]).astype(jnp.bfloat16)


def gather_doubling(array, axis, size):
    step = 1
    order = []
    while step < size:
        order.append(step)
        step *= 2
    blocks = {0: array}
    for step in reversed(order):
        held = sorted(blocks)
        message = jnp.stack([blocks[p] for p in held])
        got = lax.ppermute(message, axis, [(i ^ step, i) for i in range(size)])
        for k, p in enumerate(held):
            blocks[p ^ step] = got[k]
    return [blocks[p] for p in range(size)]


def lse(values):
    top = jnp.max(values, axis=0)
    return top + jnp.log(jnp.sum(jnp.exp(values - top[None]), axis=0))


def solution(mesh):
    blk, grp = mesh.shape["blk"], mesh.shape["grp"]
    everyone = ("blk", "grp")

    def shards(source_embed, target_embed, target_init, source_logw, target_logw):
        width, depth = target_embed.shape
        factor = -1.0 / math.sqrt(depth)
        small = jnp.concatenate([pieces(target_init), pieces(target_logw)]).reshape(-1)
        rows = -(-small.shape[0] // (8 * depth)) * 8
        small = jnp.pad(small, (0, rows * depth - small.shape[0])).reshape(rows, depth)
        message = jnp.concatenate([target_embed, small])
        blocks = gather_doubling(message, "blk", blk)
        targets = jnp.concatenate([block[:width] for block in blocks])
        smalls = jnp.stack([block[width:].reshape(-1)[: 6 * width].reshape(6, width) for block in blocks])
        smalls = smalls.astype(jnp.float32)
        init_all = ((smalls[:, 0] + smalls[:, 1]) + smalls[:, 2]).reshape(-1)
        logw_all = ((smalls[:, 3] + smalls[:, 4]) + smalls[:, 5]).reshape(-1)
        cost = (
            lax.dot_general(
                source_embed, targets, (((1,), (1,)), ((), ())), preferred_element_type=jnp.float32
            )
            * factor
        )
        me = lax.axis_index("blk")

        def to_absolute(values):
            parts = values.reshape(blk, width)
            step = 1
            while step < blk:
                pairs = parts.reshape(blk // (2 * step), 2, step, width)
                pairs = jnp.where(me & step, pairs[:, ::-1], pairs)
                parts = pairs.reshape(blk, width)
                step *= 2
            return parts

        column_pot = init_all
        for iteration in range(ITERS):
            scores = (column_pot[None, :] - cost) * inverse_eps
            row_top = jnp.max(scores, axis=1)
            row_sum = jnp.sum(jnp.exp(scores - row_top[:, None]), axis=1)
            row_pot = epsilon * source_logw - epsilon * (row_top + jnp.log(row_sum))
            part = to_absolute(lse((row_pot[:, None] - cost) * inverse_eps))
            if iteration < ITERS - 1:
                copies = jnp.broadcast_to(part[None], (blk * grp, blk, width))
                got = lax.all_to_all(copies, everyone, 0, 0)
                total = to_absolute(lse(got)).reshape(-1)
                column_pot = epsilon * logw_all - epsilon * total
            else:
                copies = jnp.broadcast_to(part[:, None], (blk, grp, width)).reshape(blk * grp, width)
                got = lax.all_to_all(copies, everyone, 0, 0)
                own_column = epsilon * target_logw - epsilon * lse(got)
        return row_pot, own_column

    in_specs = (P(("blk", "grp"), None), P("blk", None), P("blk"), P(("blk", "grp")), P("blk"))
    out_specs = (P(("blk", "grp")), P("blk"))
    return jax.shard_map(shards, mesh=mesh, in_specs=in_specs, out_specs=out_specs, check_vma=False)
```

```python
import math

import jax
import jax.numpy as jnp
from jax import lax
from jax.sharding import Mesh, PartitionSpec as P

ITERS = 2
epsilon = 0.1
inverse_eps = 10.0


def fetch(array, axis, step, size):
    return lax.ppermute(array, axis, [(i ^ step, i) for i in range(size)])


def gather_relative(array, axis, size):
    blocks = {0: array}
    step = size // 2
    while step >= 4:
        held = sorted(blocks)
        got = fetch(jnp.concatenate([blocks[p] for p in held]), axis, step, size)
        for p, part in zip(held, jnp.split(got, len(held))):
            blocks[p ^ step] = part
        step //= 2
    held = sorted(blocks)
    message = jnp.concatenate([blocks[p] for p in held]) if len(held) > 1 else array
    found = {0: message}
    if size >= 2:
        found[1] = fetch(message, axis, 1, size)
    if size >= 4:
        found[2] = fetch(message, axis, 2, size)
        half = message.shape[0] // 2
        found[3] = jnp.concatenate(
            [fetch(found[1][:half], axis, 2, size), fetch(found[2][half:], axis, 1, size)]
        )
    for q, got in found.items():
        for p, part in zip(held, jnp.split(got, len(held))):
            blocks[p ^ q] = part
    return [blocks[p] for p in range(size)]


def gather_direct(array, axis, size):
    return [array] + [fetch(array, axis, step, size) for step in range(1, size)]


def lse(values):
    top = jnp.max(values, axis=0)
    return top + jnp.log(jnp.sum(jnp.exp(values - top[None]), axis=0))


def solution(mesh):
    grp = mesh.shape["grp"]
    chips = mesh.shape["blk"] // 2
    mesh = Mesh(mesh.devices.reshape(chips, 2, grp), ("chip", "core", "grp"))
    everyone = ("chip", "grp")

    def shards(source_embed, target_embed, target_init, source_logw, target_logw):
        rows, depth = source_embed.shape
        width = target_embed.shape[0]
        factor = -1.0 / math.sqrt(depth)
        me = lax.axis_index("chip")

        def swap_order(values):
            parts = values.reshape(chips, width)
            step = 1
            while step < chips:
                pairs = parts.reshape(chips // (2 * step), 2, step, width)
                pairs = jnp.where(me & step, pairs[:, ::-1], pairs)
                parts = pairs.reshape(chips, width)
                step *= 2
            return parts

        sources = jnp.concatenate([source_embed, fetch(source_embed, "core", 1, 2)])
        targets = jnp.concatenate(gather_relative(target_embed, "chip", chips))
        small = jnp.stack([target_init, target_logw])
        if chips <= 4:
            small = jnp.stack(gather_direct(small, "chip", chips), axis=1)
        else:
            small = jnp.stack(gather_relative(small[None], "chip", chips), axis=2)[0]
        init_all, logw_all = small[0].reshape(-1), small[1].reshape(-1)
        cost = (
            lax.dot_general(
                sources, targets, (((1,), (1,)), ((), ())), preferred_element_type=jnp.float32
            )
            * factor
        )
        column_pot = init_all
        for iteration in range(ITERS):
            part = lse(((column_pot[None, :] - cost) * inverse_eps).T)
            if iteration == 0:
                other = fetch(jnp.concatenate([part, source_logw]), "core", 1, 2)
                row_logw = jnp.concatenate([source_logw, other[2 * rows :]])
            else:
                other = fetch(part, "core", 1, 2)
            other = jnp.concatenate([other[rows : 2 * rows], other[:rows]])
            row_pot = epsilon * row_logw - epsilon * lse(jnp.stack([part, other]))
            part = swap_order(lse((row_pot[:, None] - cost) * inverse_eps))
            if iteration < ITERS - 1:
                copies = jnp.broadcast_to(part[None], (chips * grp, chips, width))
                got = lax.all_to_all(copies, everyone, 0, 0)
                total = swap_order(lse(got)).reshape(-1)
                column_pot = epsilon * logw_all - epsilon * total
            else:
                copies = jnp.broadcast_to(part[:, None], (chips, grp, width))
                got = lax.all_to_all(copies.reshape(chips * grp, width), everyone, 0, 0)
                own_column = epsilon * target_logw - epsilon * lse(got)
        return row_pot[:rows], own_column

    rows_spec, blk_spec = P(("chip", "core", "grp")), P(("chip", "core"))
    in_specs = (rows_spec, blk_spec, blk_spec, rows_spec, blk_spec)
    out_specs = (rows_spec, blk_spec)
    return jax.shard_map(shards, mesh=mesh, in_specs=in_specs, out_specs=out_specs, check_vma=False)
```

```python
import math

import jax
import jax.numpy as jnp
from jax import lax
from jax.sharding import Mesh, PartitionSpec as P

ITERS = 2
epsilon = 0.1
inverse_eps = 10.0


def fetch(array, axis, step, size):
    return lax.ppermute(array, axis, [(i ^ step, i) for i in range(size)])


def after(value, *others):
    return lax.optimization_barrier((value, *others))[0]


def gather_blocks(array, small, chips):
    near = {(0, 0): array, (0, 1): fetch(array, "core", 1, 2)}
    small = after(small, near[0, 1])
    smalls = {(0, 0): small, (0, 1): fetch(small, "core", 1, 2)}

    def take_over(step, held):
        got = {p: fetch(near[p, 0], "chip", step, chips) for p in held}
        for p in held:
            near[p ^ step, 0] = got[p]
            near[p ^ step, 1] = fetch(got[p], "core", 1, 2)

    if chips <= 4:
        pair = jnp.concatenate([smalls[0, 0], smalls[0, 1]])
        for step in range(1, chips):
            got = fetch(pair, "chip", step, chips)
            smalls[step, 0], smalls[step, 1] = jnp.split(got, 2)
        smalls = [smalls[p, c] for p in range(chips) for c in range(2)]
    else:
        pair = jnp.stack([smalls[0, 0], smalls[0, 1]])[None]
        step = 1
        while step < chips:
            pair = jnp.concatenate([pair, fetch(pair, "chip", step, chips)])
            step *= 2
        smalls = [pair[p, c] for p in range(chips) for c in range(2)]

    if chips == 4:
        take_over(1, [0])
        take_over(2, [0])
        half = array.shape[0] // 2
        halves = (
            fetch(near[1, 0][:half], "chip", 2, chips),
            fetch(near[2, 0][half:], "chip", 1, chips),
        )
        near[3, 0] = jnp.concatenate(halves)
        near[3, 1] = jnp.concatenate([fetch(part, "core", 1, 2) for part in halves])
    else:
        pair = jnp.stack([near[0, 0], near[0, 1]])[None]
        step = 1
        while step < chips:
            pair = jnp.concatenate([pair, fetch(pair, "chip", step, chips)])
            step *= 2
        near = {(p, c): pair[p, c] for p in range(chips) for c in range(2)}
    return [near[p, c] for p in range(chips) for c in range(2)], smalls


def lse(values):
    top = jnp.max(values, axis=0)
    return top + jnp.log(jnp.sum(jnp.exp(values - top[None]), axis=0))


def solution(mesh):
    blk, grp = mesh.shape["blk"], mesh.shape["grp"]
    chips = blk // 2
    mesh = Mesh(mesh.devices.reshape(chips, 2, grp), ("chip", "core", "grp"))
    everyone = ("chip", "core", "grp")

    def shards(source_embed, target_embed, target_init, source_logw, target_logw):
        width, depth = target_embed.shape
        factor = -1.0 / math.sqrt(depth)
        me = lax.axis_index("chip") * 2 + lax.axis_index("core")

        def swap_order(values):
            parts = values.reshape(blk, width)
            step = 1
            while step < blk:
                pairs = parts.reshape(blk // (2 * step), 2, step, width)
                pairs = jnp.where(me & step, pairs[:, ::-1], pairs)
                parts = pairs.reshape(blk, width)
                step *= 2
            return parts

        small = jnp.stack([target_init, target_logw])
        blocks, smalls = gather_blocks(target_embed, small, chips)
        targets = jnp.concatenate(blocks)
        init_all = jnp.concatenate([part[0] for part in smalls])
        logw_all = jnp.concatenate([part[1] for part in smalls])
        cost = (
            lax.dot_general(
                source_embed, targets, (((1,), (1,)), ((), ())), preferred_element_type=jnp.float32
            )
            * factor
        )
        column_pot = init_all
        for iteration in range(ITERS):
            scores = (column_pot[None, :] - cost) * inverse_eps
            row_top = jnp.max(scores, axis=1)
            row_sum = jnp.sum(jnp.exp(scores - row_top[:, None]), axis=1)
            row_pot = epsilon * source_logw - epsilon * (row_top + jnp.log(row_sum))
            part = swap_order(lse((row_pot[:, None] - cost) * inverse_eps))
            if iteration < ITERS - 1:
                copies = jnp.broadcast_to(part[None], (blk * grp, blk, width))
                got = lax.all_to_all(copies, everyone, 0, 0)
                total = swap_order(lse(got)).reshape(-1)
                column_pot = epsilon * logw_all - epsilon * total
            else:
                copies = jnp.broadcast_to(part[:, None], (blk, grp, width)).reshape(blk * grp, width)
                got = lax.all_to_all(copies, everyone, 0, 0)
                own_column = epsilon * target_logw - epsilon * lse(got)
        return row_pot, own_column

    rows_spec, blk_spec = P(("chip", "core", "grp")), P(("chip", "core"))
    in_specs = (rows_spec, blk_spec, blk_spec, rows_spec, blk_spec)
    out_specs = (rows_spec, blk_spec)
    return jax.shard_map(shards, mesh=mesh, in_specs=in_specs, out_specs=out_specs, check_vma=False)
```

```python
import math

import jax
import jax.numpy as jnp
from jax import lax
from jax.sharding import Mesh, PartitionSpec as P

ITERS = 2
epsilon = 0.1
inverse_eps = 10.0


def fetch(array, axis, step, size):
    return lax.ppermute(array, axis, [(i ^ step, i) for i in range(size)])


def after(value, *others):
    return lax.optimization_barrier((value, *others))[0]


def gather_blocks(array, small, chips):
    near = {(0, 0): array, (0, 1): fetch(array, "core", 1, 2)}
    small = after(small, near[0, 1])

    def take_over(step, held):
        got = {p: fetch(near[p, 0], "chip", step, chips) for p in held}
        for p in held:
            near[p ^ step, 0] = got[p]
            near[p ^ step, 1] = fetch(got[p], "core", 1, 2)

    if chips <= 4:
        smalls = [small] + [fetch(small, "chip", step, chips) for step in range(1, chips)]
        smalls = jnp.stack(smalls)
    else:
        smalls = small[None]
        step = 1
        while step < chips:
            smalls = jnp.concatenate([smalls, fetch(smalls, "chip", step, chips)])
            step *= 2
    smalls = jnp.stack([smalls, fetch(smalls, "core", 1, 2)], axis=1)
    smalls = [smalls[p, c] for p in range(chips) for c in range(2)]

    if chips == 4:
        take_over(1, [0])
        take_over(2, [0])
        half = array.shape[0] // 2
        halves = (
            fetch(near[1, 0][:half], "chip", 2, chips),
            fetch(near[2, 0][half:], "chip", 1, chips),
        )
        near[3, 0] = jnp.concatenate(halves)
        near[3, 1] = jnp.concatenate([fetch(part, "core", 1, 2) for part in halves])
    else:
        pair = jnp.stack([near[0, 0], near[0, 1]])[None]
        step = 1
        while step < chips:
            pair = jnp.concatenate([pair, fetch(pair, "chip", step, chips)])
            step *= 2
        near = {(p, c): pair[p, c] for p in range(chips) for c in range(2)}
    return [near[p, c] for p in range(chips) for c in range(2)], smalls


def lse(values):
    top = jnp.max(values, axis=0)
    return top + jnp.log(jnp.sum(jnp.exp(values - top[None]), axis=0))


def solution(mesh):
    blk, grp = mesh.shape["blk"], mesh.shape["grp"]
    chips = blk // 2
    mesh = Mesh(mesh.devices.reshape(chips, 2, grp), ("chip", "core", "grp"))
    everyone = ("chip", "core", "grp")

    def shards(source_embed, target_embed, target_init, source_logw, target_logw):
        width, depth = target_embed.shape
        factor = -1.0 / math.sqrt(depth)
        me = lax.axis_index("chip") * 2 + lax.axis_index("core")

        def swap_order(values):
            parts = values.reshape(blk, width)
            step = 1
            while step < blk:
                pairs = parts.reshape(blk // (2 * step), 2, step, width)
                pairs = jnp.where(me & step, pairs[:, ::-1], pairs)
                parts = pairs.reshape(blk, width)
                step *= 2
            return parts

        small = jnp.stack([target_init, target_logw])
        blocks, smalls = gather_blocks(target_embed, small, chips)
        targets = jnp.concatenate(blocks)
        init_all = jnp.concatenate([part[0] for part in smalls])
        logw_all = jnp.concatenate([part[1] for part in smalls])
        cost = (
            lax.dot_general(
                source_embed, targets, (((1,), (1,)), ((), ())), preferred_element_type=jnp.float32
            )
            * factor
        )
        column_pot = init_all
        for iteration in range(ITERS):
            scores = (column_pot[None, :] - cost) * inverse_eps
            row_top = jnp.max(scores, axis=1)
            row_sum = jnp.sum(jnp.exp(scores - row_top[:, None]), axis=1)
            row_pot = epsilon * source_logw - epsilon * (row_top + jnp.log(row_sum))
            part = swap_order(lse((row_pot[:, None] - cost) * inverse_eps))
            if iteration < ITERS - 1:
                copies = jnp.broadcast_to(part[None], (blk * grp, blk, width))
                got = lax.all_to_all(copies, everyone, 0, 0)
                total = swap_order(lse(got)).reshape(-1)
                column_pot = epsilon * logw_all - epsilon * total
            else:
                copies = jnp.broadcast_to(part[:, None], (blk, grp, width)).reshape(blk * grp, width)
                got = lax.all_to_all(copies, everyone, 0, 0)
                own_column = epsilon * target_logw - epsilon * lse(got)
        return row_pot, own_column

    rows_spec, blk_spec = P(("chip", "core", "grp")), P(("chip", "core"))
    in_specs = (rows_spec, blk_spec, blk_spec, rows_spec, blk_spec)
    out_specs = (rows_spec, blk_spec)
    return jax.shard_map(shards, mesh=mesh, in_specs=in_specs, out_specs=out_specs, check_vma=False)
```

```python
import math

import jax
import jax.numpy as jnp
from jax import lax
from jax.sharding import Mesh, PartitionSpec as P

ITERS = 2
epsilon = 0.1
inverse_eps = 10.0


def fetch(array, axis, step, size):
    return lax.ppermute(array, axis, [(i ^ step, i) for i in range(size)])


def after(value, *others):
    return lax.optimization_barrier((value, *others))[0]


def doubled(held, step, chips):
    return jnp.concatenate([held, fetch(held, "chip", step, chips)])


def gather_blocks(array, small, chips):
    near = {(0, 0): array, (0, 1): fetch(array, "core", 1, 2)}
    small = after(small, near[0, 1])
    smalls = jnp.stack([small, fetch(small, "core", 1, 2)])[None]
    if chips == 4:
        near[1, 0] = fetch(array, "chip", 1, chips)
        near[2, 0] = fetch(array, "chip", 2, chips)
        smalls = doubled(smalls, 1, chips)
        half = array.shape[0] // 2
        halves = (
            fetch(after(near[1, 0][:half], smalls), "chip", 2, chips),
            fetch(near[2, 0][half:], "chip", 1, chips),
        )
        near[1, 1] = fetch(near[1, 0], "core", 1, 2)
        near[2, 1] = fetch(near[2, 0], "core", 1, 2)
        smalls = doubled(after(smalls, near[1, 1]), 2, chips)
        halves = (after(halves[0], smalls), halves[1])
        near[3, 0] = jnp.concatenate(halves)
        near[3, 1] = jnp.concatenate([fetch(part, "core", 1, 2) for part in halves])
    else:
        pair = jnp.stack([near[0, 0], near[0, 1]])[None]
        step = 1
        while step < chips:
            pair = doubled(pair, step, chips)
            smalls = doubled(smalls, step, chips)
            step *= 2
        near = {(p, c): pair[p, c] for p in range(chips) for c in range(2)}
    order = [(p, c) for p in range(chips) for c in range(2)]
    return [near[at] for at in order], [smalls[at] for at in order]


def lse(values):
    top = jnp.max(values, axis=0)
    return top + jnp.log(jnp.sum(jnp.exp(values - top[None]), axis=0))


def solution(mesh):
    blk, grp = mesh.shape["blk"], mesh.shape["grp"]
    chips = blk // 2
    mesh = Mesh(mesh.devices.reshape(chips, 2, grp), ("chip", "core", "grp"))

    def shards(source_embed, target_embed, target_init, source_logw, target_logw):
        width, depth = target_embed.shape
        factor = -1.0 / math.sqrt(depth)
        me = lax.axis_index("chip") * 2 + lax.axis_index("core")

        def swap_order(values):
            parts = values.reshape(blk, width)
            step = 1
            while step < blk:
                pairs = parts.reshape(blk // (2 * step), 2, step, width)
                pairs = jnp.where(me & step, pairs[:, ::-1], pairs)
                parts = pairs.reshape(blk, width)
                step *= 2
            return parts

        small = jnp.stack([target_init, target_logw])
        blocks, smalls = gather_blocks(target_embed, small, chips)
        targets = jnp.concatenate(blocks)
        init_all = jnp.concatenate([part[0] for part in smalls])
        logw_all = jnp.concatenate([part[1] for part in smalls])
        cost = (
            lax.dot_general(
                source_embed, targets, (((1,), (1,)), ((), ())), preferred_element_type=jnp.float32
            )
            * factor
        )
        column_pot = init_all
        for iteration in range(ITERS):
            scores = (column_pot[None, :] - cost) * inverse_eps
            row_top = jnp.max(scores, axis=1)
            row_sum = jnp.sum(jnp.exp(scores - row_top[:, None]), axis=1)
            row_pot = epsilon * source_logw - epsilon * (row_top + jnp.log(row_sum))
            part = swap_order(lse((row_pot[:, None] - cost) * inverse_eps))
            if iteration < ITERS - 1:
                part = jnp.broadcast_to(part[None], (blk, blk, width))
            part = lse(lax.all_to_all(part, ("chip", "core"), 0, 0))
            part = lax.all_to_all(jnp.broadcast_to(part[None], (grp, *part.shape)), "grp", 0, 0)
            total = lse(part)
            if iteration < ITERS - 1:
                column_pot = epsilon * logw_all - epsilon * swap_order(total).reshape(-1)
            else:
                own_column = epsilon * target_logw - epsilon * total
        return row_pot, own_column

    rows_spec, blk_spec = P(("chip", "core", "grp")), P(("chip", "core"))
    in_specs = (rows_spec, blk_spec, blk_spec, rows_spec, blk_spec)
    out_specs = (rows_spec, blk_spec)
    return jax.shard_map(shards, mesh=mesh, in_specs=in_specs, out_specs=out_specs, check_vma=False)
```

```python
import functools
import math

import jax
import jax.numpy as jnp
from jax import lax
from jax.experimental import pallas as pl
from jax.experimental.pallas import tpu as pltpu
from jax.sharding import Mesh, PartitionSpec as P

ITERS = 2
epsilon = 0.1
inverse_eps = 10.0
LOG2E = math.log2(math.e)
LN2 = math.log(2.0)
LANES = 128
SUBLANES = 8
SPARE = 16


def fetch(array, axis, step, size):
    return lax.ppermute(array, axis, [(i ^ step, i) for i in range(size)])


def after(value, other):
    return lax.optimization_barrier((value, other))[0]


def encode(smalls, depth):
    high = lax.reduce_precision(smalls, 8, 7)
    rest = smalls - high
    middle = lax.reduce_precision(rest, 8, 7)
    parts = jnp.stack([high, middle, rest - middle]).astype(jnp.bfloat16).reshape(-1)
    return jnp.pad(parts, (0, SPARE * depth - parts.shape[0])).reshape(SPARE, depth)


def decode(rows, shape):
    count = 3 * math.prod(shape)
    parts = rows.reshape(-1)[:count].reshape(3, *shape).astype(jnp.float32)
    return (parts[0] + parts[1]) + parts[2]


def doubled(held, step, chips):
    return jnp.concatenate([held, fetch(held, "chip", step, chips)])


def gather_any(array, small, chips):
    pair = jnp.stack([array, fetch(array, "core", 1, 2)])[None]
    smalls = jnp.stack([small, fetch(small, "core", 1, 2)])[None]
    step = 1
    while step < chips:
        pair = doubled(pair, step, chips)
        smalls = doubled(smalls, step, chips)
        step *= 2
    return pair.reshape(-1, array.shape[1]), smalls.reshape(-1, *small.shape)


def gather_square(array, small):
    width, depth = array.shape
    half = width // 2
    sibling = fetch(array, "core", 1, 2)
    over_x = fetch(array, "chip", 1, 4)
    over_y = fetch(array, "chip", 2, 4)
    small_x = fetch(after(small, sibling), "chip", 1, 4)
    rows = encode(jnp.stack([small, small_x]), depth)
    tie = (small_x[0, 0] * 0.0).astype(array.dtype)
    far_a = fetch(jnp.concatenate([over_x[:half], rows]), "chip", 2, 4)
    far_b = fetch(over_y[half:] + tie, "chip", 1, 4)
    sibling_x = fetch(jnp.concatenate([over_x, rows]), "core", 1, 2)
    sibling_y = fetch(over_y, "core", 1, 2)
    sibling_far_a = fetch(far_a, "core", 1, 2)
    sibling_far_b = fetch(far_b, "core", 1, 2)
    pair = (2, 2, width)
    smalls = jnp.stack(
        [
            jnp.concatenate([jnp.stack([small, small_x]), decode(far_a[half:], (2, *small.shape))]),
            jnp.concatenate(
                [
                    decode(sibling_x[width:], (2, *small.shape)),
                    decode(sibling_far_a[half:], (2, *small.shape)),
                ]
            ),
        ],
        axis=1,
    )
    pieces = [
        array,
        sibling,
        over_x,
        sibling_x,
        over_y,
        sibling_y,
        far_a,
        far_b,
        sibling_far_a,
        sibling_far_b,
    ]
    places = [(k * width, width) for k in range(6)]
    places += [(6 * width + k * half, half) for k in range(4)]
    return pieces, places, smalls.reshape(-1, *small.shape)


def as_column(row):
    size = row.shape[1]
    here = lax.broadcasted_iota(jnp.int32, (LANES, LANES), 0)
    there = lax.broadcasted_iota(jnp.int32, (LANES, LANES), 1)
    parts = []
    for start in range(0, size, LANES):
        wide = jnp.broadcast_to(row[:, start : start + LANES], (LANES, LANES))
        parts.append(jnp.sum(jnp.where(here == there, wide, 0.0), axis=1, keepdims=True))
    return jnp.concatenate(parts, axis=0)


def as_row(column):
    size = column.shape[0]
    here = lax.broadcasted_iota(jnp.int32, (LANES, LANES), 0)
    there = lax.broadcasted_iota(jnp.int32, (LANES, LANES), 1)
    parts = []
    for start in range(0, size, LANES):
        wide = jnp.broadcast_to(column[start : start + LANES], (LANES, LANES))
        parts.append(jnp.sum(jnp.where(here == there, wide, 0.0), axis=0, keepdims=True))
    return jnp.concatenate(parts, axis=1)


def half_sweep(scaled, columns, logw, row_pot_of, partial_of):
    rows, width = scaled.shape
    blocks = width // LANES
    chunk = 64
    for start in range(0, rows, chunk):
        at = pl.ds(start, chunk)
        top = None
        for p in range(blocks):
            score = scaled[at, p * LANES : (p + 1) * LANES] + columns[p]
            top = score if top is None else jnp.maximum(top, score)
        top = jnp.max(top, axis=1, keepdims=True)
        total = None
        for p in range(blocks):
            score = scaled[at, p * LANES : (p + 1) * LANES] + columns[p]
            term = jnp.exp2(score - top)
            total = term if total is None else total + term
        total = jnp.sum(total, axis=1, keepdims=True)
        row_pot_of[at, :] = jnp.broadcast_to(
            logw[start : start + chunk] - (top + jnp.log2(total)), (chunk, LANES)
        )
    for p in range(blocks):
        lanes = slice(p * LANES, (p + 1) * LANES)
        top = None
        for start in range(0, rows, chunk):
            at = pl.ds(start, chunk)
            score = scaled[at, lanes] + row_pot_of[at, :]
            score = jnp.max(score.reshape(chunk // SUBLANES, SUBLANES, LANES), axis=0)
            top = score if top is None else jnp.maximum(top, score)
        top = jnp.max(top, axis=0, keepdims=True)
        total = None
        for start in range(0, rows, chunk):
            at = pl.ds(start, chunk)
            term = jnp.exp2(scaled[at, lanes] + row_pot_of[at, :] - top)
            term = jnp.sum(term.reshape(chunk // SUBLANES, SUBLANES, LANES), axis=0)
            total = term if total is None else total + term
        total = jnp.sum(total, axis=0, keepdims=True)
        partial_of(p, top + jnp.log2(total))


def first_kernel(places, factor, *refs):
    count = len(places)
    source, pieces = refs[0], refs[1 : count + 1]
    init, logw, scaled, message, targets, row_pot, ordered = refs[count + 1 :]
    me = lax.axis_index("chip") * 2 + lax.axis_index("core")
    width = targets.shape[0]
    group = 2 * LANES
    for piece, (start, size) in zip(pieces, places):
        targets[start : start + size, :] = piece[0:size, :]
    for start in range(0, width, group):
        product = lax.dot_general(
            source[...],
            targets[start : start + group, :],
            (((1,), (1,)), ((), ())),
            preferred_element_type=jnp.float32,
        )
        scaled[:, start : start + group] = product * factor
    columns = [init[p : p + 1, :] * (inverse_eps * LOG2E) for p in range(width // LANES)]
    logw = as_column(logw[...] * LOG2E)

    def partial_of(p, value):
        ordered[pl.ds(jnp.bitwise_xor(me, p), 1), :] = value

    half_sweep(scaled, columns, logw, row_pot, partial_of)
    message[...] = jnp.broadcast_to(ordered[...][None], message.shape)


def second_kernel(scaled, got, target_logw, logw, row_out, message, row_pot, ordered):
    me = lax.axis_index("chip") * 2 + lax.axis_index("core")
    blocks = scaled.shape[1] // LANES
    copies = message.shape[0] // blocks
    values = got[...]
    top = jnp.max(values, axis=0)
    ordered[...] = top + jnp.log2(jnp.sum(jnp.exp2(values - top[None]), axis=0))
    columns = []
    for p in range(blocks):
        total = ordered[pl.ds(jnp.bitwise_xor(me, p), 1), :]
        columns.append(target_logw[p : p + 1, :] * LOG2E - total)

    def partial_of(p, value):
        at = pl.ds(jnp.bitwise_xor(me, p) * copies, copies)
        message[at, :] = jnp.broadcast_to(value, (copies, LANES))

    half_sweep(scaled, columns, as_column(logw[...] * LOG2E), row_pot, partial_of)
    row_out[...] = as_row(row_pot[:, 0:1]) * (epsilon * LN2)


def lse(values):
    top = jnp.max(values, axis=0)
    return top + jnp.log(jnp.sum(jnp.exp(values - top[None]), axis=0))


def solution(mesh):
    blk, grp = mesh.shape["blk"], mesh.shape["grp"]
    chips = blk // 2
    mesh = Mesh(mesh.devices.reshape(chips, 2, grp), ("chip", "core", "grp"))
    everyone = ("chip", "core", "grp")

    def shards_square(source_embed, target_embed, target_init, source_logw, target_logw):
        rows, depth = source_embed.shape
        width = target_embed.shape[0]
        small = jnp.stack([target_init, target_logw])
        pieces, places, smalls = gather_square(target_embed, small)
        vmem = pl.BlockSpec(memory_space=pltpu.VMEM)
        params = pltpu.CompilerParams(vmem_limit_bytes=24 * 1024 * 1024)
        logw = source_logw.reshape(1, rows)
        scaled, message = pl.pallas_call(
            functools.partial(first_kernel, places, inverse_eps * LOG2E / math.sqrt(depth)),
            out_shape=(
                jax.ShapeDtypeStruct((rows, blk * width), jnp.float32),
                jax.ShapeDtypeStruct((blk * grp, blk, width), jnp.float32),
            ),
            in_specs=[vmem] * (len(pieces) + 3),
            out_specs=(vmem, vmem),
            scratch_shapes=[
                pltpu.VMEM((blk * width, depth), target_embed.dtype),
                pltpu.VMEM((rows, LANES), jnp.float32),
                pltpu.VMEM((blk, width), jnp.float32),
            ],
            compiler_params=params,
        )(source_embed, *pieces, smalls[:, 0], logw)
        got = lax.all_to_all(message, everyone, 0, 0)
        row_pot, message = pl.pallas_call(
            second_kernel,
            out_shape=(
                jax.ShapeDtypeStruct((1, rows), jnp.float32),
                jax.ShapeDtypeStruct((blk * grp, width), jnp.float32),
            ),
            in_specs=[vmem] * 4,
            out_specs=(vmem, vmem),
            scratch_shapes=[
                pltpu.VMEM((rows, LANES), jnp.float32),
                pltpu.VMEM((blk, width), jnp.float32),
            ],
            compiler_params=params,
        )(scaled, got, smalls[:, 1], logw)
        got = lax.all_to_all(message, everyone, 0, 0)
        top = jnp.max(got, axis=0)
        total = top + jnp.log2(jnp.sum(jnp.exp2(got - top[None]), axis=0))
        return row_pot.reshape(rows), epsilon * target_logw - (epsilon * LN2) * total

    def shards_any(source_embed, target_embed, target_init, source_logw, target_logw):
        width, depth = target_embed.shape
        factor = -1.0 / math.sqrt(depth)
        me = lax.axis_index("chip") * 2 + lax.axis_index("core")

        def swap_order(values):
            parts = values.reshape(blk, width)
            step = 1
            while step < blk:
                pairs = parts.reshape(blk // (2 * step), 2, step, width)
                pairs = jnp.where(me & step, pairs[:, ::-1], pairs)
                parts = pairs.reshape(blk, width)
                step *= 2
            return parts

        small = jnp.stack([target_init, target_logw])
        targets, smalls = gather_any(target_embed, small, chips)
        cost = (
            lax.dot_general(
                source_embed, targets, (((1,), (1,)), ((), ())), preferred_element_type=jnp.float32
            )
            * factor
        )
        column_pot, logw_all = smalls[:, 0].reshape(-1), smalls[:, 1].reshape(-1)
        for iteration in range(ITERS):
            scores = (column_pot[None, :] - cost) * inverse_eps
            row_top = jnp.max(scores, axis=1)
            row_sum = jnp.sum(jnp.exp(scores - row_top[:, None]), axis=1)
            row_pot = epsilon * source_logw - epsilon * (row_top + jnp.log(row_sum))
            part = swap_order(lse((row_pot[:, None] - cost) * inverse_eps))
            if iteration < ITERS - 1:
                copies = jnp.broadcast_to(part[None], (blk * grp, blk, width))
                got = lax.all_to_all(copies, everyone, 0, 0)
                total = swap_order(lse(got)).reshape(-1)
                column_pot = epsilon * logw_all - epsilon * total
            else:
                copies = jnp.broadcast_to(part[:, None], (blk, grp, width)).reshape(blk * grp, width)
                got = lax.all_to_all(copies, everyone, 0, 0)
                own_column = epsilon * target_logw - epsilon * lse(got)
        return row_pot, own_column

    rows_spec, blk_spec = P(("chip", "core", "grp")), P(("chip", "core"))
    in_specs = (rows_spec, blk_spec, blk_spec, rows_spec, blk_spec)
    out_specs = (rows_spec, blk_spec)
    shards = shards_square if chips == 4 else shards_any
    return jax.shard_map(shards, mesh=mesh, in_specs=in_specs, out_specs=out_specs, check_vma=False)
```

```python
import functools
import math

import jax
import jax.numpy as jnp
from jax import lax
from jax.experimental import pallas as pl
from jax.experimental.pallas import tpu as pltpu
from jax.sharding import Mesh, PartitionSpec as P

ITERS = 2
epsilon = 0.1
inverse_eps = 10.0
LOG2E = math.log2(math.e)
LN2 = math.log(2.0)
LANES = 128
SUBLANES = 8


def fetch(array, axis, step, size):
    return lax.ppermute(array, axis, [(i ^ step, i) for i in range(size)])


def doubled(held, step, chips):
    return jnp.concatenate([held, fetch(held, "chip", step, chips)])


def gather_any(array, small, chips):
    pair = jnp.stack([array, fetch(array, "core", 1, 2)])[None]
    smalls = jnp.stack([small, fetch(small, "core", 1, 2)])[None]
    step = 1
    while step < chips:
        pair = doubled(pair, step, chips)
        smalls = doubled(smalls, step, chips)
        step *= 2
    return pair.reshape(-1, array.shape[1]), smalls.reshape(-1, *small.shape)


def as_column(row):
    size = row.shape[1]
    here = lax.broadcasted_iota(jnp.int32, (LANES, LANES), 0)
    there = lax.broadcasted_iota(jnp.int32, (LANES, LANES), 1)
    parts = []
    for start in range(0, size, LANES):
        wide = jnp.broadcast_to(row[:, start : start + LANES], (LANES, LANES))
        parts.append(jnp.sum(jnp.where(here == there, wide, 0.0), axis=1, keepdims=True))
    return jnp.concatenate(parts, axis=0)


def as_row(column):
    size = column.shape[0]
    here = lax.broadcasted_iota(jnp.int32, (LANES, LANES), 0)
    there = lax.broadcasted_iota(jnp.int32, (LANES, LANES), 1)
    parts = []
    for start in range(0, size, LANES):
        wide = jnp.broadcast_to(column[start : start + LANES], (LANES, LANES))
        parts.append(jnp.sum(jnp.where(here == there, wide, 0.0), axis=0, keepdims=True))
    return jnp.concatenate(parts, axis=1)


def half_sweep(score_of, columns, rows, logw, row_pot_of, partial_of, rows_done=lambda: None):
    blocks = len(columns)
    chunk = 64
    chunks = [pl.ds(start, chunk) for start in range(0, rows, chunk)]
    tops = []
    for at in chunks:
        top = None
        for p in range(blocks):
            score = score_of(at, p) + columns[p]
            top = score if top is None else jnp.maximum(top, score)
        tops.append(jnp.max(top, axis=1, keepdims=True))
    for at, top in zip(chunks, tops):
        total = None
        for p in range(blocks):
            term = jnp.exp2(score_of(at, p) + (columns[p] - top))
            total = term if total is None else total + term
        total = jnp.sum(total, axis=1, keepdims=True)
        row_pot_of[at, :] = logw[at, :] - (top + jnp.log2(total))
    rows_done()
    folds = (chunk // SUBLANES, SUBLANES, LANES)
    found = [[] for _ in range(blocks)]
    for at in chunks:
        row_pot = row_pot_of[at, :]
        for p in range(blocks):
            score = score_of(at, p) + row_pot
            top = jnp.max(score.reshape(folds), axis=0)
            term = jnp.exp2(score.reshape(folds) - top[None])
            found[p].append((top, jnp.sum(term, axis=0)))
    for p in range(blocks):
        top = functools.reduce(jnp.maximum, [each for each, _ in found[p]])
        top = jnp.max(top, axis=0, keepdims=True)
        total = sum(each * jnp.exp2(at_top - top) for at_top, each in found[p])
        partial_of(p, top + jnp.log2(jnp.sum(total, axis=0, keepdims=True)))


def products(source, targets, factor, out):
    group = 2 * LANES
    for start in range(0, targets.shape[0], group):
        product = lax.dot_general(
            source[...],
            targets[start : start + group, :],
            (((1,), (1,)), ((), ())),
            preferred_element_type=jnp.float32,
        )
        out[:, start : start + group] = product * factor


def early_kernel(
    factor, source, own, init, target_logw, logw, sibling, held, scaled, small, row_logw,
    targets, init_row, logw_row, rows_row, sems,
):
    width = own.shape[0]
    copies = [
        pltpu.make_async_copy(source, held, sems.at[0]),
        pltpu.make_async_copy(own, targets.at[0:width], sems.at[1]),
        pltpu.make_async_copy(init, init_row, sems.at[2]),
        pltpu.make_async_copy(target_logw, logw_row, sems.at[3]),
        pltpu.make_async_copy(logw, rows_row, sems.at[4]),
    ]
    for copy in copies:
        copy.start()
    targets[width : 2 * width, :] = sibling[...]
    for copy in copies:
        copy.wait()
    small[0:1, :] = init_row[...]
    small[1:2, :] = logw_row[...]
    row_logw[...] = jnp.broadcast_to(as_column(rows_row[...] * LOG2E), row_logw.shape)
    products(held, targets, factor, scaled)


def half_kernel(start, block, small_x, small_y, half):
    half[...] = block[start : start + half.shape[0], :]


def middle_kernel(factor, source, over_x, sibling_x, over_y, sibling_y, scaled, targets):
    width = over_x.shape[0]
    for k, piece in enumerate((over_x, sibling_x, over_y, sibling_y)):
        targets[k * width : (k + 1) * width, :] = piece[...]
    products(source, targets, factor, scaled)


def blocks_of(parts):
    return [(part, k * LANES) for part in parts for k in range(part.shape[1] // LANES)]


def first_kernel(
    factor, source, far_a, far_b, sibling_a, sibling_b, early, middle, smalls, sibling_smalls, logw,
    late, message, targets, row_pot, ordered,
):
    me = lax.axis_index("chip") * 2 + lax.axis_index("core")
    half = far_a.shape[0]
    for k, piece in enumerate((far_a, far_b, sibling_a, sibling_b)):
        targets[k * half : (k + 1) * half, :] = piece[...]
    products(source, targets, factor, late)
    places = blocks_of((early, middle, late))
    columns = [
        (smalls, sibling_smalls)[p % 2][p // 2, 0:1, :] * (inverse_eps * LOG2E)
        for p in range(len(places))
    ]

    def score_of(at, p):
        part, lane = places[p]
        return part[at, lane : lane + LANES]

    def partial_of(p, value):
        ordered[pl.ds(jnp.bitwise_xor(me, p), 1), :] = value

    half_sweep(score_of, columns, early.shape[0], logw, row_pot, partial_of)
    message[...] = jnp.broadcast_to(ordered[...][None], message.shape)


def second_kernel(
    early, middle, late, got, smalls, sibling_smalls, logw, row_out, message, row_pot, ordered,
    row, sem,
):
    me = lax.axis_index("chip") * 2 + lax.axis_index("core")
    places = blocks_of((early, middle, late))
    copies = message.shape[0] // len(places)
    values = got[...]
    top = jnp.max(values, axis=0)
    ordered[...] = top + jnp.log2(jnp.sum(jnp.exp2(values - top[None]), axis=0))
    columns = []
    for p in range(len(places)):
        total = ordered[pl.ds(jnp.bitwise_xor(me, p), 1), :]
        columns.append((smalls, sibling_smalls)[p % 2][p // 2, 1:2, :] * LOG2E - total)

    def score_of(at, p):
        part, lane = places[p]
        return part[at, lane : lane + LANES]

    def partial_of(p, value):
        at = pl.ds(jnp.bitwise_xor(me, p) * copies, copies)
        message[at, :] = jnp.broadcast_to(value, (copies, LANES))

    copy = pltpu.make_async_copy(row, row_out, sem)

    def rows_done():
        row[...] = as_row(row_pot[:, 0:1]) * (epsilon * LN2)
        copy.start()

    half_sweep(score_of, columns, early.shape[0], logw, row_pot, partial_of, rows_done)
    copy.wait()


def lse(values):
    top = jnp.max(values, axis=0)
    return top + jnp.log(jnp.sum(jnp.exp(values - top[None]), axis=0))


def solution(mesh):
    blk, grp = mesh.shape["blk"], mesh.shape["grp"]
    chips = blk // 2
    mesh = Mesh(mesh.devices.reshape(chips, 2, grp), ("chip", "core", "grp"))
    everyone = ("chip", "core", "grp")

    def shards_square(source_embed, target_embed, target_init, source_logw, target_logw):
        rows, depth = source_embed.shape
        width = target_embed.shape[0]
        half = width // 2
        factor = inverse_eps * LOG2E / math.sqrt(depth)
        vmem, hbm = pl.BlockSpec(memory_space=pltpu.VMEM), pl.BlockSpec(memory_space=pltpu.HBM)
        params = pltpu.CompilerParams(vmem_limit_bytes=16 * 1024 * 1024)

        def values(*shape):
            return jax.ShapeDtypeStruct(shape, jnp.float32)

        def cost(targets, sweeps):
            return pl.CostEstimate(
                flops=2 * rows * targets * depth + 16 * sweeps * rows * blk * width,
                transcendentals=2 * sweeps * rows * blk * width,
                bytes_accessed=2 * (rows + targets) * depth,
            )

        def targets_of(count):
            return pltpu.VMEM((count * width, depth), target_embed.dtype)

        sibling = fetch(target_embed, "core", 1, 2)
        over_x = fetch(target_embed, "chip", 1, 4)
        over_y = fetch(target_embed, "chip", 2, 4)
        source, early, small, logw = pl.pallas_call(
            functools.partial(early_kernel, factor),
            out_shape=(
                jax.ShapeDtypeStruct((rows, depth), source_embed.dtype),
                values(rows, 2 * width),
                values(2, width),
                values(rows, LANES),
            ),
            in_specs=[hbm] * 5 + [vmem],
            out_specs=(vmem,) * 4,
            scratch_shapes=[
                targets_of(2),
                pltpu.VMEM((1, width), jnp.float32),
                pltpu.VMEM((1, width), jnp.float32),
                pltpu.VMEM((1, rows), jnp.float32),
                pltpu.SemaphoreType.DMA((5,)),
            ],
            compiler_params=params,
            cost_estimate=cost(2 * width, 0),
        )(
            *(
                pltpu.with_memory_space_constraint(argument, pltpu.HBM)
                for argument in (
                    source_embed,
                    target_embed,
                    target_init.reshape(1, width),
                    target_logw.reshape(1, width),
                    source_logw.reshape(1, rows),
                )
            ),
            sibling,
        )
        smalls = [small] + [fetch(small, "chip", step, 4) for step in range(1, 4)]

        def half_of(block, start):
            return pl.pallas_call(
                functools.partial(half_kernel, start),
                out_shape=jax.ShapeDtypeStruct((half, depth), block.dtype),
                in_specs=[vmem] * 3,
                out_specs=vmem,
                compiler_params=params,
            )(block, smalls[1], smalls[2])

        far_a = fetch(half_of(over_x, 0), "chip", 2, 4)
        far_b = fetch(half_of(over_y, half), "chip", 1, 4)
        smalls = jnp.stack(smalls)
        sibling_x = fetch(over_x, "core", 1, 2)
        sibling_y = fetch(over_y, "core", 1, 2)
        sibling_smalls = fetch(smalls, "core", 1, 2)
        middle = pl.pallas_call(
            functools.partial(middle_kernel, factor),
            out_shape=values(rows, 4 * width),
            in_specs=[vmem] * 5,
            out_specs=vmem,
            scratch_shapes=[targets_of(4)],
            compiler_params=params,
            cost_estimate=cost(4 * width, 0),
        )(source, over_x, sibling_x, over_y, sibling_y)
        sibling_a = fetch(far_a, "core", 1, 2)
        sibling_b = fetch(far_b, "core", 1, 2)
        row_scratch = pltpu.VMEM((rows, LANES), jnp.float32)
        block_scratch = pltpu.VMEM((blk, width), jnp.float32)
        late, message = pl.pallas_call(
            functools.partial(first_kernel, factor),
            out_shape=(values(rows, 2 * width), values(blk * grp, blk, width)),
            in_specs=[vmem] * 10,
            out_specs=(vmem, vmem),
            scratch_shapes=[targets_of(2), row_scratch, block_scratch],
            compiler_params=params,
            cost_estimate=cost(2 * width, 1),
        )(source, far_a, far_b, sibling_a, sibling_b, early, middle, smalls, sibling_smalls, logw)
        got = lax.all_to_all(message, everyone, 0, 0)
        row_pot, message = pl.pallas_call(
            second_kernel,
            out_shape=(values(1, rows), values(blk * grp, width)),
            in_specs=[vmem] * 7,
            out_specs=(hbm, vmem),
            scratch_shapes=[
                row_scratch,
                block_scratch,
                pltpu.VMEM((1, rows), jnp.float32),
                pltpu.SemaphoreType.DMA,
            ],
            compiler_params=params,
            cost_estimate=cost(0, 1),
        )(early, middle, late, got, smalls, sibling_smalls, logw)
        got = lax.all_to_all(message, everyone, 0, 0)
        top = jnp.max(got, axis=0)
        total = top + jnp.log2(jnp.sum(jnp.exp2(got - top[None]), axis=0))
        return row_pot.reshape(rows), epsilon * target_logw - (epsilon * LN2) * total

    def shards_any(source_embed, target_embed, target_init, source_logw, target_logw):
        width, depth = target_embed.shape
        factor = -1.0 / math.sqrt(depth)
        me = lax.axis_index("chip") * 2 + lax.axis_index("core")

        def swap_order(values):
            parts = values.reshape(blk, width)
            step = 1
            while step < blk:
                pairs = parts.reshape(blk // (2 * step), 2, step, width)
                pairs = jnp.where(me & step, pairs[:, ::-1], pairs)
                parts = pairs.reshape(blk, width)
                step *= 2
            return parts

        small = jnp.stack([target_init, target_logw])
        targets, smalls = gather_any(target_embed, small, chips)
        cost = (
            lax.dot_general(
                source_embed, targets, (((1,), (1,)), ((), ())), preferred_element_type=jnp.float32
            )
            * factor
        )
        column_pot, logw_all = smalls[:, 0].reshape(-1), smalls[:, 1].reshape(-1)
        for iteration in range(ITERS):
            scores = (column_pot[None, :] - cost) * inverse_eps
            row_top = jnp.max(scores, axis=1)
            row_sum = jnp.sum(jnp.exp(scores - row_top[:, None]), axis=1)
            row_pot = epsilon * source_logw - epsilon * (row_top + jnp.log(row_sum))
            part = swap_order(lse((row_pot[:, None] - cost) * inverse_eps))
            if iteration < ITERS - 1:
                copies = jnp.broadcast_to(part[None], (blk * grp, blk, width))
                got = lax.all_to_all(copies, everyone, 0, 0)
                total = swap_order(lse(got)).reshape(-1)
                column_pot = epsilon * logw_all - epsilon * total
            else:
                copies = jnp.broadcast_to(part[:, None], (blk, grp, width)).reshape(blk * grp, width)
                got = lax.all_to_all(copies, everyone, 0, 0)
                own_column = epsilon * target_logw - epsilon * lse(got)
        return row_pot, own_column

    rows_spec, blk_spec = P(("chip", "core", "grp")), P(("chip", "core"))
    in_specs = (rows_spec, blk_spec, blk_spec, rows_spec, blk_spec)
    out_specs = (rows_spec, blk_spec)
    shards = shards_square if chips == 4 else shards_any
    return jax.shard_map(shards, mesh=mesh, in_specs=in_specs, out_specs=out_specs, check_vma=False)
```

```python
import functools
import math

import jax
import jax.numpy as jnp
from jax import lax
from jax.experimental import pallas as pl
from jax.experimental.pallas import tpu as pltpu
from jax.sharding import Mesh, PartitionSpec as P

ITERS = 2
epsilon = 0.1
inverse_eps = 10.0
LOG2E = math.log2(math.e)
LN2 = math.log(2.0)
LANES = 128
SPARE = 16
SUBLANES = 8


def fetch(array, axis, step, size):
    return lax.ppermute(array, axis, [(i ^ step, i) for i in range(size)])


def doubled(held, step, chips):
    return jnp.concatenate([held, fetch(held, "chip", step, chips)])


def gather_any(array, small, chips):
    pair = jnp.stack([array, fetch(array, "core", 1, 2)])[None]
    smalls = jnp.stack([small, fetch(small, "core", 1, 2)])[None]
    step = 1
    while step < chips:
        pair = doubled(pair, step, chips)
        smalls = doubled(smalls, step, chips)
        step *= 2
    return pair.reshape(-1, array.shape[1]), smalls.reshape(-1, *small.shape)


def as_column(row):
    size = row.shape[1]
    here = lax.broadcasted_iota(jnp.int32, (LANES, LANES), 0)
    there = lax.broadcasted_iota(jnp.int32, (LANES, LANES), 1)
    parts = []
    for start in range(0, size, LANES):
        wide = jnp.broadcast_to(row[:, start : start + LANES], (LANES, LANES))
        parts.append(jnp.sum(jnp.where(here == there, wide, 0.0), axis=1, keepdims=True))
    return jnp.concatenate(parts, axis=0)


def as_row(column):
    size = column.shape[0]
    here = lax.broadcasted_iota(jnp.int32, (LANES, LANES), 0)
    there = lax.broadcasted_iota(jnp.int32, (LANES, LANES), 1)
    parts = []
    for start in range(0, size, LANES):
        wide = jnp.broadcast_to(column[start : start + LANES], (LANES, LANES))
        parts.append(jnp.sum(jnp.where(here == there, wide, 0.0), axis=0, keepdims=True))
    return jnp.concatenate(parts, axis=1)


def half_sweep(score_of, columns, rows, logw, row_pot_of, partial_of):
    blocks = len(columns)
    chunk = 64
    chunks = [pl.ds(start, chunk) for start in range(0, rows, chunk)]
    tops = []
    for at in chunks:
        top = None
        for p in range(blocks):
            score = score_of(at, p) + columns[p]
            top = score if top is None else jnp.maximum(top, score)
        tops.append(jnp.max(top, axis=1, keepdims=True))
    for at, top in zip(chunks, tops):
        total = None
        for p in range(blocks):
            term = jnp.exp2(score_of(at, p) + (columns[p] - top))
            total = term if total is None else total + term
        total = jnp.sum(total, axis=1, keepdims=True)
        row_pot_of[at, :] = logw[at, :] - (top + jnp.log2(total))
    folds = (chunk // SUBLANES, SUBLANES, LANES)
    found = [[] for _ in range(blocks)]
    for at in chunks:
        row_pot = row_pot_of[at, :]
        for p in range(blocks):
            score = score_of(at, p) + row_pot
            top = jnp.max(score.reshape(folds), axis=0)
            term = jnp.exp2(score.reshape(folds) - top[None])
            found[p].append((top, jnp.sum(term, axis=0)))
    for p in range(blocks):
        top = functools.reduce(jnp.maximum, [each for each, _ in found[p]])
        top = jnp.max(top, axis=0, keepdims=True)
        total = sum(each * jnp.exp2(at_top - top) for at_top, each in found[p])
        partial_of(p, top + jnp.log2(jnp.sum(total, axis=0, keepdims=True)))


def products(source, targets, factor, out):
    group = 2 * LANES
    for start in range(0, targets.shape[0], group):
        product = lax.dot_general(
            source[...],
            targets[start : start + group, :],
            (((1,), (1,)), ((), ())),
            preferred_element_type=jnp.float32,
        )
        out[:, start : start + group] = product * factor


def early_kernel(
    factor, source, own, init, target_logw, logw, sibling, held, scaled, small, row_logw,
    targets, init_row, logw_row, rows_row, sems,
):
    width = own.shape[0]
    copies = [
        pltpu.make_async_copy(source, held, sems.at[0]),
        pltpu.make_async_copy(own, targets.at[0:width], sems.at[1]),
        pltpu.make_async_copy(init, init_row, sems.at[2]),
        pltpu.make_async_copy(target_logw, logw_row, sems.at[3]),
        pltpu.make_async_copy(logw, rows_row, sems.at[4]),
    ]
    for copy in copies:
        copy.start()
    targets[width : 2 * width, :] = sibling[...]
    for copy in copies:
        copy.wait()
    small[0:1, :] = init_row[...]
    small[1:2, :] = logw_row[...]
    row_logw[...] = jnp.broadcast_to(as_column(rows_row[...] * LOG2E), row_logw.shape)
    products(held, targets, factor, scaled)


def pack_kernel(block, small, small_x, half, whole):
    rows, kept = block.shape[0], half.shape[0] - SPARE
    whole[0:rows, :] = block[...]
    half[0:kept, :] = block[0:kept, :]
    filler = jnp.zeros((SPARE - 4, LANES), jnp.float32)
    rest = jnp.concatenate([small[...], small_x[...], filler], axis=0)
    for k in range(block.shape[1] // LANES):
        lanes = slice(k * LANES, (k + 1) * LANES)
        part = (rest if k < 3 else jnp.zeros_like(rest)).astype(block.dtype)
        half[kept:, lanes] = part
        whole[rows:, lanes] = part
        rest = rest - part.astype(jnp.float32)


def unpack(message):
    rows = message.shape[0] - SPARE
    parts = [
        message[rows:, k * LANES : (k + 1) * LANES].astype(jnp.float32)[0:4] for k in range(3)
    ]
    return (parts[0] + parts[1]) + parts[2]


def pieces_kernel(factor, *refs):
    source, pieces, (scaled, targets) = refs[0], refs[1:-2], refs[-2:]
    rows = targets.shape[0] // len(pieces)
    for k, piece in enumerate(pieces):
        targets[k * rows : (k + 1) * rows, :] = piece[0:rows, :]
    products(source, targets, factor, scaled)


def block_places(parts):
    return [(part, k * LANES) for part in parts for k in range(part.shape[1] // LANES)]


def first_kernel(
    early, middle, late, small, small_x, far_a, sibling_x, sibling_a, logw,
    message, target_logw, row_pot, ordered,
):
    me = lax.axis_index("chip") * 2 + lax.axis_index("core")
    places = block_places((early, middle, late))
    smalls = (
        jnp.concatenate([small[...], small_x[...], unpack(far_a)], axis=0),
        jnp.concatenate([unpack(sibling_x), unpack(sibling_a)], axis=0),
    )
    columns = []
    for p in range(len(places)):
        pair = smalls[p % 2][p // 2 * 2 : p // 2 * 2 + 2]
        columns.append(pair[0:1] * (inverse_eps * LOG2E))
        target_logw[p : p + 1, :] = pair[1:2]

    def score_of(at, p):
        part, lane = places[p]
        return part[at, lane : lane + LANES]

    def partial_of(p, value):
        ordered[pl.ds(jnp.bitwise_xor(me, p), 1), :] = value

    half_sweep(score_of, columns, early.shape[0], logw, row_pot, partial_of)
    message[...] = jnp.broadcast_to(ordered[...][None], message.shape)


def second_kernel(
    early, middle, late, got, target_logw, logw, row, message, row_pot, ordered
):
    me = lax.axis_index("chip") * 2 + lax.axis_index("core")
    places = block_places((early, middle, late))
    copies = message.shape[0] // len(places)
    values = got[...]
    top = jnp.max(values, axis=0)
    ordered[...] = top + jnp.log2(jnp.sum(jnp.exp2(values - top[None]), axis=0))
    columns = []
    for p in range(len(places)):
        total = ordered[pl.ds(jnp.bitwise_xor(me, p), 1), :]
        columns.append(target_logw[p : p + 1, :] * LOG2E - total)

    def score_of(at, p):
        part, lane = places[p]
        return part[at, lane : lane + LANES]

    def partial_of(p, value):
        at = pl.ds(jnp.bitwise_xor(me, p) * copies, copies)
        message[at, :] = jnp.broadcast_to(value, (copies, LANES))

    half_sweep(score_of, columns, early.shape[0], logw, row_pot, partial_of)
    row[...] = as_row(row_pot[:, 0:1]) * (epsilon * LN2)


def last_kernel(got, small, row, row_out, column_out):
    values = got[...]
    top = jnp.max(values, axis=0, keepdims=True)
    total = top + jnp.log2(jnp.sum(jnp.exp2(values - top), axis=0, keepdims=True))
    column_out[...] = epsilon * small[1:2, :] - (epsilon * LN2) * total
    row_out[...] = row[...]


def lse(values):
    top = jnp.max(values, axis=0)
    return top + jnp.log(jnp.sum(jnp.exp(values - top[None]), axis=0))


def solution(mesh):
    blk, grp = mesh.shape["blk"], mesh.shape["grp"]
    chips = blk // 2
    mesh = Mesh(mesh.devices.reshape(chips, 2, grp), ("chip", "core", "grp"))
    everyone = ("chip", "core", "grp")

    def shards_square(source_embed, target_embed, target_init, source_logw, target_logw):
        rows, depth = source_embed.shape
        width = target_embed.shape[0]
        half = width // 2
        factor = inverse_eps * LOG2E / math.sqrt(depth)
        vmem, hbm = pl.BlockSpec(memory_space=pltpu.VMEM), pl.BlockSpec(memory_space=pltpu.HBM)
        params = pltpu.CompilerParams(vmem_limit_bytes=16 * 1024 * 1024)

        def values(*shape):
            return jax.ShapeDtypeStruct(shape, jnp.float32)

        def cost(targets, sweeps):
            return pl.CostEstimate(
                flops=2 * rows * targets * depth + 16 * sweeps * rows * blk * width,
                transcendentals=2 * sweeps * rows * blk * width,
                bytes_accessed=2 * (rows + targets) * depth,
            )

        def targets_of(count):
            return pltpu.VMEM((count * width, depth), target_embed.dtype)

        sibling = fetch(target_embed, "core", 1, 2)
        over_x = fetch(target_embed, "chip", 1, 4)
        over_y = fetch(target_embed, "chip", 2, 4)
        source, early, small, logw = pl.pallas_call(
            functools.partial(early_kernel, factor),
            out_shape=(
                jax.ShapeDtypeStruct((rows, depth), source_embed.dtype),
                values(rows, 2 * width),
                values(2, width),
                values(rows, LANES),
            ),
            in_specs=[hbm] * 5 + [vmem],
            out_specs=(vmem,) * 4,
            scratch_shapes=[
                targets_of(2),
                pltpu.VMEM((1, width), jnp.float32),
                pltpu.VMEM((1, width), jnp.float32),
                pltpu.VMEM((1, rows), jnp.float32),
                pltpu.SemaphoreType.DMA((5,)),
            ],
            compiler_params=params,
            cost_estimate=cost(2 * width, 0),
        )(
            *(
                pltpu.with_memory_space_constraint(argument, pltpu.HBM)
                for argument in (
                    source_embed,
                    target_embed,
                    target_init.reshape(1, width),
                    target_logw.reshape(1, width),
                    source_logw.reshape(1, rows),
                )
            ),
            sibling,
        )
        small_x = fetch(small, "chip", 1, 4)
        def block_of(size):
            return jax.ShapeDtypeStruct((size, depth), target_embed.dtype)

        packed_half, packed_x = pl.pallas_call(
            pack_kernel,
            out_shape=(block_of(half + SPARE), block_of(width + SPARE)),
            in_specs=[vmem] * 3,
            out_specs=(vmem, vmem),
            compiler_params=params,
        )(over_x, small, small_x)
        far_a = fetch(packed_half, "chip", 2, 4)
        far_b = fetch(over_y[half:], "chip", 1, 4)
        sibling_x = fetch(packed_x, "core", 1, 2)
        sibling_y = fetch(over_y, "core", 1, 2)
        sibling_a = fetch(far_a, "core", 1, 2)
        sibling_b = fetch(far_b, "core", 1, 2)

        def products_of(count, weight, *pieces):
            return pl.pallas_call(
                functools.partial(pieces_kernel, factor),
                out_shape=values(rows, count * width),
                in_specs=[vmem] * (1 + len(pieces)),
                out_specs=vmem,
                scratch_shapes=[targets_of(count)],
                compiler_params=params,
                cost_estimate=cost(weight * width, 0),
            )(source, *pieces)

        middle = products_of(4, 0, over_x, sibling_x, over_y, sibling_y)
        late = products_of(2, 40, far_a, far_b, sibling_a, sibling_b)
        row_scratch = pltpu.VMEM((rows, LANES), jnp.float32)
        block_scratch = pltpu.VMEM((blk, width), jnp.float32)
        message, logw_all = pl.pallas_call(
            first_kernel,
            out_shape=(values(blk * grp, blk, width), values(blk, width)),
            in_specs=[vmem] * 9,
            out_specs=(vmem, vmem),
            scratch_shapes=[row_scratch, block_scratch],
            compiler_params=params,
            cost_estimate=cost(0, 1),
        )(early, middle, late, small, small_x, far_a, sibling_x, sibling_a, logw)
        got = lax.all_to_all(message, everyone, 0, 0)
        row, message = pl.pallas_call(
            second_kernel,
            out_shape=(values(1, rows), values(blk * grp, width)),
            in_specs=[vmem] * 6,
            out_specs=(vmem, vmem),
            scratch_shapes=[row_scratch, block_scratch],
            compiler_params=params,
            cost_estimate=cost(0, 1),
        )(early, middle, late, got, logw_all, logw)
        got = lax.all_to_all(message, everyone, 0, 0)
        row_pot, column_pot = pl.pallas_call(
            last_kernel,
            out_shape=(values(1, rows), values(1, width)),
            in_specs=[vmem] * 3,
            out_specs=(vmem, vmem),
            compiler_params=params,
        )(got, small, row)
        return row_pot.reshape(rows), column_pot.reshape(width)

    def shards_any(source_embed, target_embed, target_init, source_logw, target_logw):
        width, depth = target_embed.shape
        factor = -1.0 / math.sqrt(depth)
        me = lax.axis_index("chip") * 2 + lax.axis_index("core")

        def swap_order(values):
            parts = values.reshape(blk, width)
            step = 1
            while step < blk:
                pairs = parts.reshape(blk // (2 * step), 2, step, width)
                pairs = jnp.where(me & step, pairs[:, ::-1], pairs)
                parts = pairs.reshape(blk, width)
                step *= 2
            return parts

        small = jnp.stack([target_init, target_logw])
        targets, smalls = gather_any(target_embed, small, chips)
        cost = (
            lax.dot_general(
                source_embed, targets, (((1,), (1,)), ((), ())), preferred_element_type=jnp.float32
            )
            * factor
        )
        column_pot, logw_all = smalls[:, 0].reshape(-1), smalls[:, 1].reshape(-1)
        for iteration in range(ITERS):
            scores = (column_pot[None, :] - cost) * inverse_eps
            row_top = jnp.max(scores, axis=1)
            row_sum = jnp.sum(jnp.exp(scores - row_top[:, None]), axis=1)
            row_pot = epsilon * source_logw - epsilon * (row_top + jnp.log(row_sum))
            part = swap_order(lse((row_pot[:, None] - cost) * inverse_eps))
            if iteration < ITERS - 1:
                copies = jnp.broadcast_to(part[None], (blk * grp, blk, width))
                got = lax.all_to_all(copies, everyone, 0, 0)
                total = swap_order(lse(got)).reshape(-1)
                column_pot = epsilon * logw_all - epsilon * total
            else:
                copies = jnp.broadcast_to(part[:, None], (blk, grp, width)).reshape(blk * grp, width)
                got = lax.all_to_all(copies, everyone, 0, 0)
                own_column = epsilon * target_logw - epsilon * lse(got)
        return row_pot, own_column

    rows_spec, blk_spec = P(("chip", "core", "grp")), P(("chip", "core"))
    in_specs = (rows_spec, blk_spec, blk_spec, rows_spec, blk_spec)
    out_specs = (rows_spec, blk_spec)
    shards = shards_square if chips == 4 else shards_any
    return jax.shard_map(shards, mesh=mesh, in_specs=in_specs, out_specs=out_specs, check_vma=False)
```

```python
import functools
import math

import jax
import jax.numpy as jnp
from jax import lax
from jax.experimental import pallas as pl
from jax.experimental.pallas import tpu as pltpu
from jax.sharding import Mesh, PartitionSpec as P

ITERS = 2
epsilon = 0.1
inverse_eps = 10.0
LOG2E = math.log2(math.e)
LN2 = math.log(2.0)
LANES = 128
SPARE = 16
SUBLANES = 8


def fetch(array, axis, step, size):
    return lax.ppermute(array, axis, [(i ^ step, i) for i in range(size)])


def doubled(held, step, chips):
    return jnp.concatenate([held, fetch(held, "chip", step, chips)])


def gather_any(array, small, chips):
    pair = jnp.stack([array, fetch(array, "core", 1, 2)])[None]
    smalls = jnp.stack([small, fetch(small, "core", 1, 2)])[None]
    step = 1
    while step < chips:
        pair = doubled(pair, step, chips)
        smalls = doubled(smalls, step, chips)
        step *= 2
    return pair.reshape(-1, array.shape[1]), smalls.reshape(-1, *small.shape)


def as_column(row):
    size = row.shape[1]
    here = lax.broadcasted_iota(jnp.int32, (LANES, LANES), 0)
    there = lax.broadcasted_iota(jnp.int32, (LANES, LANES), 1)
    parts = []
    for start in range(0, size, LANES):
        wide = jnp.broadcast_to(row[:, start : start + LANES], (LANES, LANES))
        parts.append(jnp.sum(jnp.where(here == there, wide, 0.0), axis=1, keepdims=True))
    return jnp.concatenate(parts, axis=0)


def as_row(column):
    size = column.shape[0]
    here = lax.broadcasted_iota(jnp.int32, (LANES, LANES), 0)
    there = lax.broadcasted_iota(jnp.int32, (LANES, LANES), 1)
    parts = []
    for start in range(0, size, LANES):
        wide = jnp.broadcast_to(column[start : start + LANES], (LANES, LANES))
        parts.append(jnp.sum(jnp.where(here == there, wide, 0.0), axis=0, keepdims=True))
    return jnp.concatenate(parts, axis=1)


def half_sweep(score_of, columns, rows, logw, row_pot_of, partial_of):
    blocks = len(columns)
    chunk = 64
    chunks = [pl.ds(start, chunk) for start in range(0, rows, chunk)]
    tops = []
    for at in chunks:
        top = None
        for p in range(blocks):
            score = score_of(at, p) + columns[p]
            top = score if top is None else jnp.maximum(top, score)
        tops.append(jnp.max(top, axis=1, keepdims=True))
    for at, top in zip(chunks, tops):
        total = None
        for p in range(blocks):
            term = jnp.exp2(score_of(at, p) + (columns[p] - top))
            total = term if total is None else total + term
        total = jnp.sum(total, axis=1, keepdims=True)
        row_pot_of[at, :] = logw[at, :] - (top + jnp.log2(total))
    folds = (chunk // SUBLANES, SUBLANES, LANES)
    found = [[] for _ in range(blocks)]
    for at in chunks:
        row_pot = row_pot_of[at, :]
        for p in range(blocks):
            score = score_of(at, p) + row_pot
            top = jnp.max(score.reshape(folds), axis=0)
            term = jnp.exp2(score.reshape(folds) - top[None])
            found[p].append((top, jnp.sum(term, axis=0)))
    for p in range(blocks):
        top = functools.reduce(jnp.maximum, [each for each, _ in found[p]])
        top = jnp.max(top, axis=0, keepdims=True)
        total = sum(each * jnp.exp2(at_top - top) for at_top, each in found[p])
        partial_of(p, top + jnp.log2(jnp.sum(total, axis=0, keepdims=True)))


def products(source, targets, factor, out):
    group = 2 * LANES
    for start in range(0, targets.shape[0], group):
        product = lax.dot_general(
            source[...],
            targets[start : start + group, :],
            (((1,), (1,)), ((), ())),
            preferred_element_type=jnp.float32,
        )
        out[:, start : start + group] = product * factor


def head_kernel(
    own, init, target_logw, first, second, whole, small, first_plain, second_plain, init_row,
    logw_row, sems,
):
    rows, half = own.shape[0], first_plain.shape[0]
    copies = [
        pltpu.make_async_copy(own, whole.at[0:rows], sems.at[0]),
        pltpu.make_async_copy(init, init_row, sems.at[1]),
        pltpu.make_async_copy(target_logw, logw_row, sems.at[2]),
    ]
    for copy in copies:
        copy.start()
    for copy in copies:
        copy.wait()
    for out in (first, first_plain):
        out[0:half, :] = whole[0:half, :]
    for out in (second, second_plain):
        out[0:half, :] = whole[half:rows, :]
    small[0:1, :] = init_row[...]
    small[1:2, :] = logw_row[...]
    filler = jnp.zeros((SPARE - 2, LANES), jnp.float32)
    rest = jnp.concatenate([init_row[...], logw_row[...], filler], axis=0)
    for k in range(whole.shape[1] // LANES):
        lanes = slice(k * LANES, (k + 1) * LANES)
        part = (rest if k < 3 else jnp.zeros_like(rest)).astype(whole.dtype)
        first[half:, lanes] = part
        second[half:, lanes] = part
        whole[rows:, lanes] = part
        rest = rest - part.astype(jnp.float32)


def source_kernel(source, logw, whole, held, row_logw, passed, rows_row, sems):
    copies = [
        pltpu.make_async_copy(source, held, sems.at[0]),
        pltpu.make_async_copy(logw, rows_row, sems.at[1]),
    ]
    for copy in copies:
        copy.start()
    passed[...] = whole[...]
    for copy in copies:
        copy.wait()
    row_logw[...] = jnp.broadcast_to(as_column(rows_row[...] * LOG2E), row_logw.shape)


def sibling_kernel(whole, x_first, x_second, y_first, y_second, out):
    half = x_second.shape[0]
    block = 2 * half + SPARE
    out[0:block, :] = whole[...]
    out[block : block + half, :] = x_first[0:half, :]
    out[block + half : block + 2 * half, :] = x_second[...]
    out[block + 2 * half : 2 * block, :] = x_first[half:, :]
    out[2 * block : 2 * block + half, :] = y_first[...]
    out[2 * block + half : 3 * block, :] = y_second[...]


def unpack(message, end=None):
    end = message.shape[0] if end is None else end
    parts = [
        message[end - SPARE : end, k * LANES : (k + 1) * LANES].astype(jnp.float32)[0:2]
        for k in range(3)
    ]
    return (parts[0] + parts[1]) + parts[2]


def near_kernel(factor, source, whole, x_first, x_second, y_first, y_second, sibling, scaled, targets):
    half = x_second.shape[0]
    width = 2 * half
    block = width + SPARE
    targets[0:width, :] = whole[0:width, :]
    for k, piece in enumerate((x_first, x_second)):
        targets[2 * width + k * half : 2 * width + (k + 1) * half, :] = piece[0:half, :]
    for k, piece in enumerate((y_first, y_second)):
        targets[4 * width + k * half : 4 * width + (k + 1) * half, :] = piece[0:half, :]
    for k in range(3):
        start = (2 * k + 1) * width
        targets[start : start + width, :] = sibling[k * block : k * block + width, :]
    products(source, targets, factor, scaled)


def pass_kernel(message, out):
    out[...] = message[...]


def far_kernel(factor, source, far_a, far_b, sibling_a, sibling_b, near, scaled, targets):
    half = targets.shape[0] // 4
    for k, piece in enumerate((far_a, far_b, sibling_a, sibling_b)):
        targets[k * half : (k + 1) * half, :] = piece[0:half, :]
    products(source, targets, factor, scaled)


def block_places(parts):
    return [(part, k * LANES) for part in parts for k in range(part.shape[1] // LANES)]


def first_kernel(
    near, far, small, x_first, y_second, far_a, sibling, sibling_a,
    logw, message, target_logw, row_pot, ordered,
):
    me = lax.axis_index("chip") * 2 + lax.axis_index("core")
    places = block_places((near, far))
    block = sibling.shape[0] // 3
    smalls = [small[...], unpack(sibling, block)]
    smalls += [unpack(x_first), unpack(sibling, 2 * block)]
    smalls += [unpack(y_second), unpack(sibling, 3 * block)]
    smalls += [unpack(far_a), unpack(sibling_a)]
    columns = []
    for p in range(len(places)):
        columns.append(smalls[p][0:1] * (inverse_eps * LOG2E))
        target_logw[p : p + 1, :] = smalls[p][1:2]

    def score_of(at, p):
        part, lane = places[p]
        return part[at, lane : lane + LANES]

    def partial_of(p, value):
        ordered[pl.ds(jnp.bitwise_xor(me, p), 1), :] = value

    half_sweep(score_of, columns, near.shape[0], logw, row_pot, partial_of)
    message[...] = jnp.broadcast_to(ordered[...][None], message.shape)


def second_kernel(
    near, far, got, target_logw, logw, row, message, row_pot, ordered
):
    me = lax.axis_index("chip") * 2 + lax.axis_index("core")
    places = block_places((near, far))
    copies = message.shape[0] // len(places)
    values = got[...]
    top = jnp.max(values, axis=0)
    ordered[...] = top + jnp.log2(jnp.sum(jnp.exp2(values - top[None]), axis=0))
    columns = []
    for p in range(len(places)):
        total = ordered[pl.ds(jnp.bitwise_xor(me, p), 1), :]
        columns.append(target_logw[p : p + 1, :] * LOG2E - total)

    def score_of(at, p):
        part, lane = places[p]
        return part[at, lane : lane + LANES]

    def partial_of(p, value):
        at = pl.ds(jnp.bitwise_xor(me, p) * copies, copies)
        message[at, :] = jnp.broadcast_to(value, (copies, LANES))

    half_sweep(score_of, columns, near.shape[0], logw, row_pot, partial_of)
    row[...] = as_row(row_pot[:, 0:1]) * (epsilon * LN2)


def last_kernel(got, small, row, row_out, column_out):
    values = got[...]
    top = jnp.max(values, axis=0, keepdims=True)
    total = top + jnp.log2(jnp.sum(jnp.exp2(values - top), axis=0, keepdims=True))
    column_out[...] = epsilon * small[1:2, :] - (epsilon * LN2) * total
    row_out[...] = row[...]


def lse(values):
    top = jnp.max(values, axis=0)
    return top + jnp.log(jnp.sum(jnp.exp(values - top[None]), axis=0))


def solution(mesh):
    blk, grp = mesh.shape["blk"], mesh.shape["grp"]
    chips = blk // 2
    mesh = Mesh(mesh.devices.reshape(chips, 2, grp), ("chip", "core", "grp"))
    everyone = ("chip", "core", "grp")

    def shards_square(source_embed, target_embed, target_init, source_logw, target_logw):
        rows, depth = source_embed.shape
        width = target_embed.shape[0]
        half = width // 2
        factor = inverse_eps * LOG2E / math.sqrt(depth)
        vmem, hbm = pl.BlockSpec(memory_space=pltpu.VMEM), pl.BlockSpec(memory_space=pltpu.HBM)
        params = pltpu.CompilerParams(vmem_limit_bytes=16 * 1024 * 1024)

        def values(*shape):
            return jax.ShapeDtypeStruct(shape, jnp.float32)

        def cost(targets, sweeps):
            return pl.CostEstimate(
                flops=2 * rows * targets * depth + 16 * sweeps * rows * blk * width,
                transcendentals=2 * sweeps * rows * blk * width,
                bytes_accessed=2 * (rows + targets) * depth,
            )

        def block_of(size):
            return jax.ShapeDtypeStruct((size, depth), target_embed.dtype)

        def in_hbm(*arrays):
            return [pltpu.with_memory_space_constraint(each, pltpu.HBM) for each in arrays]

        first, second, whole, small, first_plain, second_plain = pl.pallas_call(
            head_kernel,
            out_shape=(
                block_of(half + SPARE),
                block_of(half + SPARE),
                block_of(width + SPARE),
                values(2, width),
                block_of(half),
                block_of(half),
            ),
            in_specs=[hbm] * 3,
            out_specs=(vmem,) * 6,
            scratch_shapes=[
                pltpu.VMEM((1, width), jnp.float32),
                pltpu.VMEM((1, width), jnp.float32),
                pltpu.SemaphoreType.DMA((3,)),
            ],
            compiler_params=params,
        )(*in_hbm(target_embed, target_init.reshape(1, width), target_logw.reshape(1, width)))
        x_first = fetch(first, "chip", 1, 4)
        y_second = fetch(second, "chip", 2, 4)
        x_second = fetch(second_plain, "chip", 1, 4)
        y_first = fetch(first_plain, "chip", 2, 4)
        far_a = fetch(x_first, "chip", 2, 4)
        far_b = fetch(y_second, "chip", 1, 4)
        source, logw, passed = pl.pallas_call(
            source_kernel,
            out_shape=(
                jax.ShapeDtypeStruct((rows, depth), source_embed.dtype),
                values(rows, LANES),
                block_of(width + SPARE),
            ),
            in_specs=[hbm] * 2 + [vmem],
            out_specs=(vmem,) * 3,
            scratch_shapes=[pltpu.VMEM((1, rows), jnp.float32), pltpu.SemaphoreType.DMA((2,))],
            compiler_params=params,
        )(*in_hbm(source_embed, source_logw.reshape(1, rows)), whole)
        near = (x_first, x_second, y_first, y_second)
        sibling = pl.pallas_call(
            sibling_kernel,
            out_shape=block_of(3 * (width + SPARE)),
            in_specs=[vmem] * 5,
            out_specs=vmem,
            compiler_params=params,
            cost_estimate=cost(0, 0),
        )(passed, *near)
        sibling = fetch(sibling, "core", 1, 2)

        def passed_on(message, weight):
            return pl.pallas_call(
                pass_kernel,
                out_shape=jax.ShapeDtypeStruct(message.shape, message.dtype),
                in_specs=[vmem],
                out_specs=vmem,
                compiler_params=params,
                cost_estimate=cost(weight * width, 0),
            )(message)

        sibling_a = fetch(passed_on(far_a, 0), "core", 1, 2)
        sibling_b = fetch(passed_on(far_b, 50), "core", 1, 2)

        def products_of(kernel, blocks, weight, *pieces):
            return pl.pallas_call(
                functools.partial(kernel, factor),
                out_shape=values(rows, blocks * width),
                in_specs=[vmem] * (1 + len(pieces)),
                out_specs=vmem,
                scratch_shapes=[pltpu.VMEM((blocks * width, depth), target_embed.dtype)],
                compiler_params=params,
                cost_estimate=cost(weight * width, 0),
            )(source, *pieces)

        scores_near = products_of(near_kernel, 6, 0, whole, *near, sibling)
        scores_far = products_of(far_kernel, 2, 0, far_a, far_b, sibling_a, sibling_b, scores_near)
        row_scratch = pltpu.VMEM((rows, LANES), jnp.float32)
        block_scratch = pltpu.VMEM((blk, width), jnp.float32)
        message, logw_all = pl.pallas_call(
            first_kernel,
            out_shape=(values(blk * grp, blk, width), values(blk, width)),
            in_specs=[vmem] * 9,
            out_specs=(vmem, vmem),
            scratch_shapes=[row_scratch, block_scratch],
            compiler_params=params,
            cost_estimate=cost(0, 1),
        )(
            scores_near,
            scores_far,
            small,
            x_first,
            y_second,
            far_a,
            sibling,
            sibling_a,
            logw,
        )
        got = lax.all_to_all(message, everyone, 0, 0)
        row, message = pl.pallas_call(
            second_kernel,
            out_shape=(values(1, rows), values(blk * grp, width)),
            in_specs=[vmem] * 5,
            out_specs=(vmem, vmem),
            scratch_shapes=[row_scratch, block_scratch],
            compiler_params=params,
            cost_estimate=cost(0, 1),
        )(scores_near, scores_far, got, logw_all, logw)
        got = lax.all_to_all(message, everyone, 0, 0)
        row_pot, column_pot = pl.pallas_call(
            last_kernel,
            out_shape=(values(1, rows), values(1, width)),
            in_specs=[vmem] * 3,
            out_specs=(vmem, vmem),
            compiler_params=params,
        )(got, small, row)
        return row_pot.reshape(rows), column_pot.reshape(width)

    def shards_any(source_embed, target_embed, target_init, source_logw, target_logw):
        width, depth = target_embed.shape
        factor = -1.0 / math.sqrt(depth)
        me = lax.axis_index("chip") * 2 + lax.axis_index("core")

        def swap_order(values):
            parts = values.reshape(blk, width)
            step = 1
            while step < blk:
                pairs = parts.reshape(blk // (2 * step), 2, step, width)
                pairs = jnp.where(me & step, pairs[:, ::-1], pairs)
                parts = pairs.reshape(blk, width)
                step *= 2
            return parts

        small = jnp.stack([target_init, target_logw])
        targets, smalls = gather_any(target_embed, small, chips)
        cost = (
            lax.dot_general(
                source_embed, targets, (((1,), (1,)), ((), ())), preferred_element_type=jnp.float32
            )
            * factor
        )
        column_pot, logw_all = smalls[:, 0].reshape(-1), smalls[:, 1].reshape(-1)
        for iteration in range(ITERS):
            scores = (column_pot[None, :] - cost) * inverse_eps
            row_top = jnp.max(scores, axis=1)
            row_sum = jnp.sum(jnp.exp(scores - row_top[:, None]), axis=1)
            row_pot = epsilon * source_logw - epsilon * (row_top + jnp.log(row_sum))
            part = swap_order(lse((row_pot[:, None] - cost) * inverse_eps))
            if iteration < ITERS - 1:
                copies = jnp.broadcast_to(part[None], (blk * grp, blk, width))
                got = lax.all_to_all(copies, everyone, 0, 0)
                total = swap_order(lse(got)).reshape(-1)
                column_pot = epsilon * logw_all - epsilon * total
            else:
                copies = jnp.broadcast_to(part[:, None], (blk, grp, width)).reshape(blk * grp, width)
                got = lax.all_to_all(copies, everyone, 0, 0)
                own_column = epsilon * target_logw - epsilon * lse(got)
        return row_pot, own_column

    rows_spec, blk_spec = P(("chip", "core", "grp")), P(("chip", "core"))
    in_specs = (rows_spec, blk_spec, blk_spec, rows_spec, blk_spec)
    out_specs = (rows_spec, blk_spec)
    shards = shards_square if chips == 4 else shards_any
    return jax.shard_map(shards, mesh=mesh, in_specs=in_specs, out_specs=out_specs, check_vma=False)
```

```python
import functools
import math

import jax
import jax.numpy as jnp
from jax import lax
from jax.experimental import pallas as pl
from jax.experimental.pallas import tpu as pltpu
from jax.sharding import Mesh, PartitionSpec as P

ITERS = 2
epsilon = 0.1
inverse_eps = 10.0
LOG2E = math.log2(math.e)
LN2 = math.log(2.0)
LANES = 128
SPARE = 8
SUBLANES = 8


def fetch(array, axis, step, size):
    return lax.ppermute(array, axis, [(i ^ step, i) for i in range(size)])


def doubled(held, step, chips):
    return jnp.concatenate([held, fetch(held, "chip", step, chips)])


def gather_any(array, small, chips):
    pair = jnp.stack([array, fetch(array, "core", 1, 2)])[None]
    smalls = jnp.stack([small, fetch(small, "core", 1, 2)])[None]
    step = 1
    while step < chips:
        pair = doubled(pair, step, chips)
        smalls = doubled(smalls, step, chips)
        step *= 2
    return pair.reshape(-1, array.shape[1]), smalls.reshape(-1, *small.shape)


def as_column(row):
    size = row.shape[1]
    here = lax.broadcasted_iota(jnp.int32, (LANES, LANES), 0)
    there = lax.broadcasted_iota(jnp.int32, (LANES, LANES), 1)
    parts = []
    for start in range(0, size, LANES):
        wide = jnp.broadcast_to(row[:, start : start + LANES], (LANES, LANES))
        parts.append(jnp.sum(jnp.where(here == there, wide, 0.0), axis=1, keepdims=True))
    return jnp.concatenate(parts, axis=0)


def as_row(column):
    size = column.shape[0]
    here = lax.broadcasted_iota(jnp.int32, (LANES, LANES), 0)
    there = lax.broadcasted_iota(jnp.int32, (LANES, LANES), 1)
    parts = []
    for start in range(0, size, LANES):
        wide = jnp.broadcast_to(column[start : start + LANES], (LANES, LANES))
        parts.append(jnp.sum(jnp.where(here == there, wide, 0.0), axis=0, keepdims=True))
    return jnp.concatenate(parts, axis=1)


def half_sweep(score_of, columns, rows, logw, row_pot_of, partial_of):
    blocks = len(columns)
    chunk = 64
    chunks = [pl.ds(start, chunk) for start in range(0, rows, chunk)]
    tops = []
    for at in chunks:
        top = None
        for p in range(blocks):
            score = score_of(at, p) + columns[p]
            top = score if top is None else jnp.maximum(top, score)
        tops.append(jnp.max(top, axis=1, keepdims=True))
    for at, top in zip(chunks, tops):
        total = None
        for p in range(blocks):
            term = jnp.exp2(score_of(at, p) + (columns[p] - top))
            total = term if total is None else total + term
        total = jnp.sum(total, axis=1, keepdims=True)
        row_pot_of[at, :] = logw[at, :] - (top + jnp.log2(total))
    folds = (chunk // SUBLANES, SUBLANES, LANES)
    found = [[] for _ in range(blocks)]
    for at in chunks:
        row_pot = row_pot_of[at, :]
        for p in range(blocks):
            score = score_of(at, p) + row_pot
            top = jnp.max(score.reshape(folds), axis=0)
            term = jnp.exp2(score.reshape(folds) - top[None])
            found[p].append((top, jnp.sum(term, axis=0)))
    for p in range(blocks):
        top = functools.reduce(jnp.maximum, [each for each, _ in found[p]])
        top = jnp.max(top, axis=0, keepdims=True)
        total = sum(each * jnp.exp2(at_top - top) for at_top, each in found[p])
        partial_of(p, top + jnp.log2(jnp.sum(total, axis=0, keepdims=True)))


def products(source, targets, factor, out):
    group = 2 * LANES
    for start in range(0, targets.shape[0], group):
        product = lax.dot_general(
            source[...],
            targets[start : start + group, :],
            (((1,), (1,)), ((), ())),
            preferred_element_type=jnp.float32,
        )
        out[:, start : start + group] = product * factor


def head_kernel(
    own, init, target_logw, first, second, whole, small, first_plain, second_plain, init_row,
    logw_row, sems,
):
    rows, half = own.shape[0], first_plain.shape[0]
    copies = [
        pltpu.make_async_copy(own, whole.at[0:rows], sems.at[0]),
        pltpu.make_async_copy(init, init_row, sems.at[1]),
        pltpu.make_async_copy(target_logw, logw_row, sems.at[2]),
    ]
    for copy in copies:
        copy.start()
    for copy in copies:
        copy.wait()
    for out in (first, first_plain):
        out[0:half, :] = whole[0:half, :]
    for out in (second, second_plain):
        out[0:half, :] = whole[half:rows, :]
    small[0:1, :] = init_row[...]
    small[1:2, :] = logw_row[...]
    filler = jnp.zeros((SPARE - 2, LANES), jnp.float32)
    rest = jnp.concatenate([init_row[...], logw_row[...], filler], axis=0)
    for k in range(whole.shape[1] // LANES):
        lanes = slice(k * LANES, (k + 1) * LANES)
        part = (rest if k < 3 else jnp.zeros_like(rest)).astype(whole.dtype)
        first[half:, lanes] = part
        second[half:, lanes] = part
        whole[rows:, lanes] = part
        rest = rest - part.astype(jnp.float32)


def source_kernel(source, logw, whole, held, row_logw, passed, rows_row, sems):
    copies = [
        pltpu.make_async_copy(source, held, sems.at[0]),
        pltpu.make_async_copy(logw, rows_row, sems.at[1]),
    ]
    for copy in copies:
        copy.start()
    passed[...] = whole[...]
    for copy in copies:
        copy.wait()
    row_logw[...] = jnp.broadcast_to(as_column(rows_row[...] * LOG2E), row_logw.shape)


def sibling_kernel(whole, x_first, x_second, y_first, y_second, out):
    half = x_second.shape[0]
    block = 2 * half + SPARE
    out[0:block, :] = whole[...]
    out[block : block + half, :] = x_first[0:half, :]
    out[block + half : block + 2 * half, :] = x_second[...]
    out[block + 2 * half : 2 * block, :] = x_first[half:, :]
    out[2 * block : 2 * block + half, :] = y_first[...]
    out[2 * block + half : 3 * block, :] = y_second[...]


def unpack(message, end=None):
    end = message.shape[0] if end is None else end
    parts = [
        message[end - SPARE : end, k * LANES : (k + 1) * LANES].astype(jnp.float32)[0:2]
        for k in range(3)
    ]
    return (parts[0] + parts[1]) + parts[2]


def near_kernel(factor, source, whole, x_first, x_second, y_first, y_second, sibling, scaled, targets):
    half = x_second.shape[0]
    width = 2 * half
    block = width + SPARE
    targets[0:width, :] = whole[0:width, :]
    for k, piece in enumerate((x_first, x_second)):
        targets[2 * width + k * half : 2 * width + (k + 1) * half, :] = piece[0:half, :]
    for k, piece in enumerate((y_first, y_second)):
        targets[4 * width + k * half : 4 * width + (k + 1) * half, :] = piece[0:half, :]
    for k in range(3):
        start = (2 * k + 1) * width
        targets[start : start + width, :] = sibling[k * block : k * block + width, :]
    products(source, targets, factor, scaled)


def pass_kernel(message, out):
    out[...] = message[...]


def far_kernel(factor, source, far_a, far_b, sibling_a, sibling_b, near, scaled, targets):
    half = targets.shape[0] // 4
    for k, piece in enumerate((far_a, far_b, sibling_a, sibling_b)):
        targets[k * half : (k + 1) * half, :] = piece[0:half, :]
    products(source, targets, factor, scaled)


def block_places(parts):
    return [(part, k * LANES) for part in parts for k in range(part.shape[1] // LANES)]


def first_kernel(
    near, far, small, x_first, y_second, far_a, sibling, sibling_a,
    logw, message, target_logw, row_pot, ordered,
):
    me = lax.axis_index("blk")
    places = block_places((near, far))
    block = sibling.shape[0] // 3
    smalls = [small[...], unpack(sibling, block)]
    smalls += [unpack(x_first), unpack(sibling, 2 * block)]
    smalls += [unpack(y_second), unpack(sibling, 3 * block)]
    smalls += [unpack(far_a), unpack(sibling_a)]
    columns = []
    for p in range(len(places)):
        columns.append(smalls[p][0:1] * (inverse_eps * LOG2E))
        target_logw[p : p + 1, :] = smalls[p][1:2]

    def score_of(at, p):
        part, lane = places[p]
        return part[at, lane : lane + LANES]

    def partial_of(p, value):
        ordered[pl.ds(jnp.bitwise_xor(me, p), 1), :] = value

    half_sweep(score_of, columns, near.shape[0], logw, row_pot, partial_of)
    message[...] = jnp.broadcast_to(ordered[...][None], message.shape)


def second_kernel(
    copies, near, far, got, target_logw, logw, row, message, row_pot, ordered
):
    me = lax.axis_index("blk")
    places = block_places((near, far))
    values = got[...]
    top = jnp.max(values, axis=0)
    ordered[...] = top + jnp.log2(jnp.sum(jnp.exp2(values - top[None]), axis=0))
    columns = []
    for p in range(len(places)):
        total = ordered[pl.ds(jnp.bitwise_xor(me, p), 1), :]
        columns.append(target_logw[p : p + 1, :] * LOG2E - total)

    def score_of(at, p):
        part, lane = places[p]
        return part[at, lane : lane + LANES]

    def partial_of(p, value):
        at = pl.ds((len(places) - 1 - jnp.bitwise_xor(me, p)) * copies, copies)
        message[at, :] = jnp.broadcast_to(value, (copies, LANES))

    half_sweep(score_of, columns, near.shape[0], logw, row_pot, partial_of)
    row[...] = as_row(row_pot[:, 0:1]) * (epsilon * LN2)


def last_kernel(got, small, row, row_out, column_out):
    values = got[...]
    top = jnp.max(values, axis=0, keepdims=True)
    total = top + jnp.log2(jnp.sum(jnp.exp2(values - top), axis=0, keepdims=True))
    column_out[...] = epsilon * small[1:2, :] - (epsilon * LN2) * total
    row_out[...] = row[...]


def lse(values):
    top = jnp.max(values, axis=0)
    return top + jnp.log(jnp.sum(jnp.exp(values - top[None]), axis=0))


def solution(mesh):
    blk, grp = mesh.shape["blk"], mesh.shape["grp"]
    chips = blk // 2
    everyone = ("chip", "core", "grp")

    def shards_square(source_embed, target_embed, target_init, source_logw, target_logw):
        rows, depth = source_embed.shape
        width = target_embed.shape[0]
        half = width // 2
        factor = inverse_eps * LOG2E / math.sqrt(depth)
        vmem, hbm = pl.BlockSpec(memory_space=pltpu.VMEM), pl.BlockSpec(memory_space=pltpu.HBM)
        params = pltpu.CompilerParams(vmem_limit_bytes=16 * 1024 * 1024)

        def values(*shape):
            return jax.ShapeDtypeStruct(shape, jnp.float32)

        def cost(targets, sweeps):
            return pl.CostEstimate(
                flops=2 * rows * targets * depth + 16 * sweeps * rows * blk * width,
                transcendentals=2 * sweeps * rows * blk * width,
                bytes_accessed=2 * (rows + targets) * depth,
            )

        def over(array, step):
            return lax.ppermute(array, "blk", [(i ^ step, i) for i in range(blk)])

        def exchange(message):
            order = list(range(blk * grp))[::-1]
            return lax.all_to_all(message, ("blk", "grp"), 0, 0, axis_index_groups=[order])

        def block_of(size):
            return jax.ShapeDtypeStruct((size, depth), target_embed.dtype)

        def in_hbm(*arrays):
            return [pltpu.with_memory_space_constraint(each, pltpu.HBM) for each in arrays]

        first, second, whole, small, first_plain, second_plain = pl.pallas_call(
            head_kernel,
            out_shape=(
                block_of(half + SPARE),
                block_of(half + SPARE),
                block_of(width + SPARE),
                values(2, width),
                block_of(half),
                block_of(half),
            ),
            in_specs=[hbm] * 3,
            out_specs=(vmem,) * 6,
            scratch_shapes=[
                pltpu.VMEM((1, width), jnp.float32),
                pltpu.VMEM((1, width), jnp.float32),
                pltpu.SemaphoreType.DMA((3,)),
            ],
            compiler_params=params,
        )(*in_hbm(target_embed, target_init.reshape(1, width), target_logw.reshape(1, width)))
        x_first = over(first, 1 * 2)
        y_second = over(second, 2 * 2)
        x_second = over(second_plain, 1 * 2)
        y_first = over(first_plain, 2 * 2)
        far_a = over(x_first, 2 * 2)
        far_b = over(y_second, 1 * 2)
        source, logw, passed = pl.pallas_call(
            source_kernel,
            out_shape=(
                jax.ShapeDtypeStruct((rows, depth), source_embed.dtype),
                values(rows, LANES),
                block_of(width + SPARE),
            ),
            in_specs=[hbm] * 2 + [vmem],
            out_specs=(vmem,) * 3,
            scratch_shapes=[pltpu.VMEM((1, rows), jnp.float32), pltpu.SemaphoreType.DMA((2,))],
            compiler_params=params,
        )(*in_hbm(source_embed, source_logw.reshape(1, rows)), whole)
        near = (x_first, x_second, y_first, y_second)
        sibling = pl.pallas_call(
            sibling_kernel,
            out_shape=block_of(3 * (width + SPARE)),
            in_specs=[vmem] * 5,
            out_specs=vmem,
            compiler_params=params,
            cost_estimate=cost(0, 0),
        )(passed, *near)
        sibling = over(sibling, 1)

        def passed_on(message, weight):
            return pl.pallas_call(
                pass_kernel,
                out_shape=jax.ShapeDtypeStruct(message.shape, message.dtype),
                in_specs=[vmem],
                out_specs=vmem,
                compiler_params=params,
                cost_estimate=cost(weight * width, 0),
            )(message)

        sibling_a = over(passed_on(far_a, 0), 1)
        sibling_b = over(passed_on(far_b, 50), 1)

        def products_of(kernel, blocks, weight, *pieces):
            return pl.pallas_call(
                functools.partial(kernel, factor),
                out_shape=values(rows, blocks * width),
                in_specs=[vmem] * (1 + len(pieces)),
                out_specs=vmem,
                scratch_shapes=[pltpu.VMEM((blocks * width, depth), target_embed.dtype)],
                compiler_params=params,
                cost_estimate=cost(weight * width, 0),
            )(source, *pieces)

        scores_near = products_of(near_kernel, 6, 0, whole, *near, sibling)
        scores_far = products_of(far_kernel, 2, 0, far_a, far_b, sibling_a, sibling_b, scores_near)
        row_scratch = pltpu.VMEM((rows, LANES), jnp.float32)
        block_scratch = pltpu.VMEM((blk, width), jnp.float32)
        message, logw_all = pl.pallas_call(
            first_kernel,
            out_shape=(values(blk * grp, blk, width), values(blk, width)),
            in_specs=[vmem] * 9,
            out_specs=(vmem, vmem),
            scratch_shapes=[row_scratch, block_scratch],
            compiler_params=params,
            cost_estimate=cost(0, 1),
        )(
            scores_near,
            scores_far,
            small,
            x_first,
            y_second,
            far_a,
            sibling,
            sibling_a,
            logw,
        )
        got = exchange(message)
        row, message = pl.pallas_call(
            functools.partial(second_kernel, grp),
            out_shape=(values(1, rows), values(blk * grp, width)),
            in_specs=[vmem] * 5,
            out_specs=(vmem, vmem),
            scratch_shapes=[row_scratch, block_scratch],
            compiler_params=params,
            cost_estimate=cost(0, 1),
        )(scores_near, scores_far, got, logw_all, logw)
        got = exchange(message)
        row_pot, column_pot = pl.pallas_call(
            last_kernel,
            out_shape=(values(1, rows), values(1, width)),
            in_specs=[vmem] * 3,
            out_specs=(vmem, vmem),
            compiler_params=params,
        )(got, small, row)
        return row_pot.reshape(rows), column_pot.reshape(width)

    def shards_any(source_embed, target_embed, target_init, source_logw, target_logw):
        width, depth = target_embed.shape
        factor = -1.0 / math.sqrt(depth)
        me = lax.axis_index("chip") * 2 + lax.axis_index("core")

        def swap_order(values):
            parts = values.reshape(blk, width)
            step = 1
            while step < blk:
                pairs = parts.reshape(blk // (2 * step), 2, step, width)
                pairs = jnp.where(me & step, pairs[:, ::-1], pairs)
                parts = pairs.reshape(blk, width)
                step *= 2
            return parts

        small = jnp.stack([target_init, target_logw])
        targets, smalls = gather_any(target_embed, small, chips)
        cost = (
            lax.dot_general(
                source_embed, targets, (((1,), (1,)), ((), ())), preferred_element_type=jnp.float32
            )
            * factor
        )
        column_pot, logw_all = smalls[:, 0].reshape(-1), smalls[:, 1].reshape(-1)
        for iteration in range(ITERS):
            scores = (column_pot[None, :] - cost) * inverse_eps
            row_top = jnp.max(scores, axis=1)
            row_sum = jnp.sum(jnp.exp(scores - row_top[:, None]), axis=1)
            row_pot = epsilon * source_logw - epsilon * (row_top + jnp.log(row_sum))
            part = swap_order(lse((row_pot[:, None] - cost) * inverse_eps))
            if iteration < ITERS - 1:
                copies = jnp.broadcast_to(part[None], (blk * grp, blk, width))
                got = lax.all_to_all(copies, everyone, 0, 0)
                total = swap_order(lse(got)).reshape(-1)
                column_pot = epsilon * logw_all - epsilon * total
            else:
                copies = jnp.broadcast_to(part[:, None], (blk, grp, width)).reshape(blk * grp, width)
                got = lax.all_to_all(copies, everyone, 0, 0)
                own_column = epsilon * target_logw - epsilon * lse(got)
        return row_pot, own_column

    if chips == 4:
        shards = shards_square
        rows_spec, blk_spec = P(("blk", "grp")), P("blk")
    else:
        shards = shards_any
        rows_spec, blk_spec = P(everyone), P(("chip", "core"))
        mesh = Mesh(mesh.devices.reshape(chips, 2, grp), everyone)
    in_specs = (rows_spec, blk_spec, blk_spec, rows_spec, blk_spec)
    out_specs = (rows_spec, blk_spec)
    return jax.shard_map(shards, mesh=mesh, in_specs=in_specs, out_specs=out_specs, check_vma=False)
```

```python
import functools
import math

import jax
import jax.numpy as jnp
from jax import lax
from jax.experimental import pallas as pl
from jax.experimental.pallas import tpu as pltpu
from jax.sharding import Mesh, PartitionSpec as P

ITERS = 2
epsilon = 0.1
inverse_eps = 10.0
LOG2E = math.log2(math.e)
LN2 = math.log(2.0)
LANES = 128
SPARE = 8
SUBLANES = 8


def fetch(array, axis, step, size):
    return lax.ppermute(array, axis, [(i ^ step, i) for i in range(size)])


def doubled(held, step, chips):
    return jnp.concatenate([held, fetch(held, "chip", step, chips)])


def gather_any(array, small, chips):
    pair = jnp.stack([array, fetch(array, "core", 1, 2)])[None]
    smalls = jnp.stack([small, fetch(small, "core", 1, 2)])[None]
    step = 1
    while step < chips:
        pair = doubled(pair, step, chips)
        smalls = doubled(smalls, step, chips)
        step *= 2
    return pair.reshape(-1, array.shape[1]), smalls.reshape(-1, *small.shape)


def as_column(row):
    size = row.shape[1]
    here = lax.broadcasted_iota(jnp.int32, (LANES, LANES), 0)
    there = lax.broadcasted_iota(jnp.int32, (LANES, LANES), 1)
    parts = []
    for start in range(0, size, LANES):
        wide = jnp.broadcast_to(row[:, start : start + LANES], (LANES, LANES))
        parts.append(jnp.sum(jnp.where(here == there, wide, 0.0), axis=1, keepdims=True))
    return jnp.concatenate(parts, axis=0)


def as_row(column):
    size = column.shape[0]
    here = lax.broadcasted_iota(jnp.int32, (LANES, LANES), 0)
    there = lax.broadcasted_iota(jnp.int32, (LANES, LANES), 1)
    parts = []
    for start in range(0, size, LANES):
        wide = jnp.broadcast_to(column[start : start + LANES], (LANES, LANES))
        parts.append(jnp.sum(jnp.where(here == there, wide, 0.0), axis=0, keepdims=True))
    return jnp.concatenate(parts, axis=1)


def half_sweep(score_of, columns, rows, logw, row_pot_of, partial_of):
    blocks = len(columns)
    chunk = 64
    chunks = [pl.ds(start, chunk) for start in range(0, rows, chunk)]
    tops = []
    for at in chunks:
        top = None
        for p in range(blocks):
            score = score_of(at, p) + columns[p]
            top = score if top is None else jnp.maximum(top, score)
        tops.append(jnp.max(top, axis=1, keepdims=True))
    for at, top in zip(chunks, tops):
        total = None
        for p in range(blocks):
            term = jnp.exp2(score_of(at, p) + (columns[p] - top))
            total = term if total is None else total + term
        total = jnp.sum(total, axis=1, keepdims=True)
        row_pot_of[at, :] = logw[at, :] - (top + jnp.log2(total))
    folds = (chunk // SUBLANES, SUBLANES, LANES)
    found = [[] for _ in range(blocks)]
    for at in chunks:
        row_pot = row_pot_of[at, :]
        for p in range(blocks):
            score = score_of(at, p) + row_pot
            top = jnp.max(score.reshape(folds), axis=0)
            term = jnp.exp2(score.reshape(folds) - top[None])
            found[p].append((top, jnp.sum(term, axis=0)))
    for p in range(blocks):
        top = functools.reduce(jnp.maximum, [each for each, _ in found[p]])
        top = jnp.max(top, axis=0, keepdims=True)
        total = sum(each * jnp.exp2(at_top - top) for at_top, each in found[p])
        partial_of(p, top + jnp.log2(jnp.sum(total, axis=0, keepdims=True)))


def products(source, targets, factor, out):
    group = 2 * LANES
    for start in range(0, targets.shape[0], group):
        product = lax.dot_general(
            source[...],
            targets[start : start + group, :],
            (((1,), (1,)), ((), ())),
            preferred_element_type=jnp.float32,
        )
        out[:, start : start + group] = product * factor


def head_kernel(
    own, init, target_logw, first, second, whole, small, first_plain, second_plain, init_row,
    logw_row, sems,
):
    rows, half = own.shape[0], first_plain.shape[0]
    copies = [
        pltpu.make_async_copy(own, whole.at[0:rows], sems.at[0]),
        pltpu.make_async_copy(init, init_row, sems.at[1]),
        pltpu.make_async_copy(target_logw, logw_row, sems.at[2]),
    ]
    for copy in copies:
        copy.start()
    for copy in copies:
        copy.wait()
    for out in (first, first_plain):
        out[0:half, :] = whole[0:half, :]
    for out in (second, second_plain):
        out[0:half, :] = whole[half:rows, :]
    small[0:1, :] = init_row[...]
    small[1:2, :] = logw_row[...]
    filler = jnp.zeros((SPARE - 2, LANES), jnp.float32)
    rest = jnp.concatenate([init_row[...], logw_row[...], filler], axis=0)
    for k in range(whole.shape[1] // LANES):
        lanes = slice(k * LANES, (k + 1) * LANES)
        part = (rest if k < 3 else jnp.zeros_like(rest)).astype(whole.dtype)
        first[half:, lanes] = part
        second[half:, lanes] = part
        whole[rows:, lanes] = part
        rest = rest - part.astype(jnp.float32)


def source_kernel(source, logw, whole, held, row_logw, passed, rows_row, sems):
    copies = [
        pltpu.make_async_copy(source, held, sems.at[0]),
        pltpu.make_async_copy(logw, rows_row, sems.at[1]),
    ]
    for copy in copies:
        copy.start()
    passed[...] = whole[...]
    for copy in copies:
        copy.wait()
    row_logw[...] = jnp.broadcast_to(as_column(rows_row[...] * LOG2E), row_logw.shape)


def sibling_kernel(whole, a_first, a_second, b_first, b_second, out):
    half = a_second.shape[0]
    block = 2 * half + SPARE
    out[0:block, :] = whole[...]
    out[block : block + half, :] = a_first[0:half, :]
    out[block + half : block + 2 * half, :] = a_second[...]
    out[block + 2 * half : 2 * block, :] = a_first[half:, :]
    out[2 * block : 2 * block + half, :] = b_first[...]
    out[2 * block + half : 3 * block, :] = b_second[...]


def unpack(message, end=None):
    end = message.shape[0] if end is None else end
    parts = [
        message[end - SPARE : end, k * LANES : (k + 1) * LANES].astype(jnp.float32)[0:2]
        for k in range(3)
    ]
    return (parts[0] + parts[1]) + parts[2]


def near_kernel(factor, source, whole, a_first, a_second, b_first, b_second, sibling, scaled, targets):
    half = a_second.shape[0]
    width = 2 * half
    block = width + SPARE
    targets[0:width, :] = whole[0:width, :]
    for k, piece in enumerate((a_first, a_second)):
        targets[2 * width + k * half : 2 * width + (k + 1) * half, :] = piece[0:half, :]
    for k, piece in enumerate((b_first, b_second)):
        targets[4 * width + k * half : 4 * width + (k + 1) * half, :] = piece[0:half, :]
    for k in range(3):
        start = (2 * k + 1) * width
        targets[start : start + width, :] = sibling[k * block : k * block + width, :]
    products(source, targets, factor, scaled)


def pass_kernel(message, out):
    out[...] = message[...]


def far_kernel(factor, source, far_a, far_b, sibling_a, sibling_b, near, scaled, targets):
    half = targets.shape[0] // 4
    for k, piece in enumerate((far_a, far_b, sibling_a, sibling_b)):
        targets[k * half : (k + 1) * half, :] = piece[0:half, :]
    products(source, targets, factor, scaled)


def neighbour_step(me, turn):
    step = 2 + 2 * (me % 2)
    return step if turn == 0 else 6 - step


def positions(me):
    sibling = me ^ 1
    own = [me, me ^ neighbour_step(me, 0), me ^ neighbour_step(me, 1), me ^ 6]
    other = [
        sibling,
        sibling ^ neighbour_step(sibling, 0),
        sibling ^ neighbour_step(sibling, 1),
        sibling ^ 6,
    ]
    return [block for pair in zip(own, other) for block in pair]


def block_places(parts):
    return [(part, k * LANES) for part in parts for k in range(part.shape[1] // LANES)]


def first_kernel(
    near, far, small, a_first, b_second, far_a, sibling, sibling_a,
    logw, message, target_logw, row_pot, ordered,
):
    order = positions(lax.axis_index("blk"))
    places = block_places((near, far))
    block = sibling.shape[0] // 3
    smalls = [small[...], unpack(sibling, block)]
    smalls += [unpack(a_first), unpack(sibling, 2 * block)]
    smalls += [unpack(b_second), unpack(sibling, 3 * block)]
    smalls += [unpack(far_a), unpack(sibling_a)]
    columns = []
    for p in range(len(places)):
        columns.append(smalls[p][0:1] * (inverse_eps * LOG2E))
        target_logw[p : p + 1, :] = smalls[p][1:2]

    def score_of(at, p):
        part, lane = places[p]
        return part[at, lane : lane + LANES]

    def partial_of(p, value):
        ordered[pl.ds(order[p], 1), :] = value

    half_sweep(score_of, columns, near.shape[0], logw, row_pot, partial_of)
    message[...] = jnp.broadcast_to(ordered[...][None], message.shape)


def second_kernel(
    copies, near, far, got, target_logw, logw, row, message, row_pot, ordered
):
    order = positions(lax.axis_index("blk"))
    places = block_places((near, far))
    values = got[...]
    top = jnp.max(values, axis=0)
    ordered[...] = top + jnp.log2(jnp.sum(jnp.exp2(values - top[None]), axis=0))
    columns = []
    for p in range(len(places)):
        total = ordered[pl.ds(order[p], 1), :]
        columns.append(target_logw[p : p + 1, :] * LOG2E - total)

    def score_of(at, p):
        part, lane = places[p]
        return part[at, lane : lane + LANES]

    def partial_of(p, value):
        at = pl.ds((len(places) - 1 - order[p]) * copies, copies)
        message[at, :] = jnp.broadcast_to(value, (copies, LANES))

    half_sweep(score_of, columns, near.shape[0], logw, row_pot, partial_of)
    row[...] = as_row(row_pot[:, 0:1]) * (epsilon * LN2)


def last_kernel(got, small, row, row_out, column_out):
    values = got[...]
    top = jnp.max(values, axis=0, keepdims=True)
    total = top + jnp.log2(jnp.sum(jnp.exp2(values - top), axis=0, keepdims=True))
    column_out[...] = epsilon * small[1:2, :] - (epsilon * LN2) * total
    row_out[...] = row[...]


def lse(values):
    top = jnp.max(values, axis=0)
    return top + jnp.log(jnp.sum(jnp.exp(values - top[None]), axis=0))


def solution(mesh):
    blk, grp = mesh.shape["blk"], mesh.shape["grp"]
    chips = blk // 2
    everyone = ("chip", "core", "grp")

    def shards_square(source_embed, target_embed, target_init, source_logw, target_logw):
        rows, depth = source_embed.shape
        width = target_embed.shape[0]
        half = width // 2
        factor = inverse_eps * LOG2E / math.sqrt(depth)
        vmem, hbm = pl.BlockSpec(memory_space=pltpu.VMEM), pl.BlockSpec(memory_space=pltpu.HBM)
        params = pltpu.CompilerParams(vmem_limit_bytes=16 * 1024 * 1024)

        def values(*shape):
            return jax.ShapeDtypeStruct(shape, jnp.float32)

        def cost(targets, sweeps):
            return pl.CostEstimate(
                flops=2 * rows * targets * depth + 16 * sweeps * rows * blk * width,
                transcendentals=2 * sweeps * rows * blk * width,
                bytes_accessed=2 * (rows + targets) * depth,
            )

        def along(array, turn):
            return lax.ppermute(
                array, "blk", [(i ^ neighbour_step(i, turn), i) for i in range(blk)]
            )

        def to_sibling(array):
            return fetch(array, "blk", 1, blk)

        def exchange(message):
            order = list(range(blk * grp))[::-1]
            return lax.all_to_all(message, ("blk", "grp"), 0, 0, axis_index_groups=[order])

        def block_of(size):
            return jax.ShapeDtypeStruct((size, depth), target_embed.dtype)

        def in_hbm(*arrays):
            return [pltpu.with_memory_space_constraint(each, pltpu.HBM) for each in arrays]

        first, second, whole, small, first_plain, second_plain = pl.pallas_call(
            head_kernel,
            out_shape=(
                block_of(half + SPARE),
                block_of(half + SPARE),
                block_of(width + SPARE),
                values(2, width),
                block_of(half),
                block_of(half),
            ),
            in_specs=[hbm] * 3,
            out_specs=(vmem,) * 6,
            scratch_shapes=[
                pltpu.VMEM((1, width), jnp.float32),
                pltpu.VMEM((1, width), jnp.float32),
                pltpu.SemaphoreType.DMA((3,)),
            ],
            compiler_params=params,
        )(*in_hbm(target_embed, target_init.reshape(1, width), target_logw.reshape(1, width)))
        a_first = along(first, 0)
        b_second = along(second, 1)
        a_second = along(second_plain, 0)
        b_first = along(first_plain, 1)
        far_a = along(a_first, 1)
        far_b = along(b_second, 0)
        source, logw, passed = pl.pallas_call(
            source_kernel,
            out_shape=(
                jax.ShapeDtypeStruct((rows, depth), source_embed.dtype),
                values(rows, LANES),
                block_of(width + SPARE),
            ),
            in_specs=[hbm] * 2 + [vmem],
            out_specs=(vmem,) * 3,
            scratch_shapes=[pltpu.VMEM((1, rows), jnp.float32), pltpu.SemaphoreType.DMA((2,))],
            compiler_params=params,
        )(*in_hbm(source_embed, source_logw.reshape(1, rows)), whole)
        near = (a_first, a_second, b_first, b_second)
        sibling = pl.pallas_call(
            sibling_kernel,
            out_shape=block_of(3 * (width + SPARE)),
            in_specs=[vmem] * 5,
            out_specs=vmem,
            compiler_params=params,
            cost_estimate=cost(0, 0),
        )(passed, *near)
        sibling = to_sibling(sibling)

        def passed_on(message, weight):
            return pl.pallas_call(
                pass_kernel,
                out_shape=jax.ShapeDtypeStruct(message.shape, message.dtype),
                in_specs=[vmem],
                out_specs=vmem,
                compiler_params=params,
                cost_estimate=cost(weight * width, 0),
            )(message)

        sibling_a = to_sibling(passed_on(far_a, 0))
        sibling_b = to_sibling(passed_on(far_b, 50))

        def products_of(kernel, blocks, weight, *pieces):
            return pl.pallas_call(
                functools.partial(kernel, factor),
                out_shape=values(rows, blocks * width),
                in_specs=[vmem] * (1 + len(pieces)),
                out_specs=vmem,
                scratch_shapes=[pltpu.VMEM((blocks * width, depth), target_embed.dtype)],
                compiler_params=params,
                cost_estimate=cost(weight * width, 0),
            )(source, *pieces)

        scores_near = products_of(near_kernel, 6, 0, whole, *near, sibling)
        scores_far = products_of(far_kernel, 2, 0, far_a, far_b, sibling_a, sibling_b, scores_near)
        row_scratch = pltpu.VMEM((rows, LANES), jnp.float32)
        block_scratch = pltpu.VMEM((blk, width), jnp.float32)
        message, logw_all = pl.pallas_call(
            first_kernel,
            out_shape=(values(blk * grp, blk, width), values(blk, width)),
            in_specs=[vmem] * 9,
            out_specs=(vmem, vmem),
            scratch_shapes=[row_scratch, block_scratch],
            compiler_params=params,
            cost_estimate=cost(0, 1),
        )(
            scores_near,
            scores_far,
            small,
            a_first,
            b_second,
            far_a,
            sibling,
            sibling_a,
            logw,
        )
        got = exchange(message)
        row, message = pl.pallas_call(
            functools.partial(second_kernel, grp),
            out_shape=(values(1, rows), values(blk * grp, width)),
            in_specs=[vmem] * 5,
            out_specs=(vmem, vmem),
            scratch_shapes=[row_scratch, block_scratch],
            compiler_params=params,
            cost_estimate=cost(0, 1),
        )(scores_near, scores_far, got, logw_all, logw)
        got = exchange(message)
        row_pot, column_pot = pl.pallas_call(
            last_kernel,
            out_shape=(values(1, rows), values(1, width)),
            in_specs=[vmem] * 3,
            out_specs=(vmem, vmem),
            compiler_params=params,
        )(got, small, row)
        return row_pot.reshape(rows), column_pot.reshape(width)

    def shards_any(source_embed, target_embed, target_init, source_logw, target_logw):
        width, depth = target_embed.shape
        factor = -1.0 / math.sqrt(depth)
        me = lax.axis_index("chip") * 2 + lax.axis_index("core")

        def swap_order(values):
            parts = values.reshape(blk, width)
            step = 1
            while step < blk:
                pairs = parts.reshape(blk // (2 * step), 2, step, width)
                pairs = jnp.where(me & step, pairs[:, ::-1], pairs)
                parts = pairs.reshape(blk, width)
                step *= 2
            return parts

        small = jnp.stack([target_init, target_logw])
        targets, smalls = gather_any(target_embed, small, chips)
        cost = (
            lax.dot_general(
                source_embed, targets, (((1,), (1,)), ((), ())), preferred_element_type=jnp.float32
            )
            * factor
        )
        column_pot, logw_all = smalls[:, 0].reshape(-1), smalls[:, 1].reshape(-1)
        for iteration in range(ITERS):
            scores = (column_pot[None, :] - cost) * inverse_eps
            row_top = jnp.max(scores, axis=1)
            row_sum = jnp.sum(jnp.exp(scores - row_top[:, None]), axis=1)
            row_pot = epsilon * source_logw - epsilon * (row_top + jnp.log(row_sum))
            part = swap_order(lse((row_pot[:, None] - cost) * inverse_eps))
            if iteration < ITERS - 1:
                copies = jnp.broadcast_to(part[None], (blk * grp, blk, width))
                got = lax.all_to_all(copies, everyone, 0, 0)
                total = swap_order(lse(got)).reshape(-1)
                column_pot = epsilon * logw_all - epsilon * total
            else:
                copies = jnp.broadcast_to(part[:, None], (blk, grp, width)).reshape(blk * grp, width)
                got = lax.all_to_all(copies, everyone, 0, 0)
                own_column = epsilon * target_logw - epsilon * lse(got)
        return row_pot, own_column

    if chips == 4:
        shards = shards_square
        rows_spec, blk_spec = P(("blk", "grp")), P("blk")
    else:
        shards = shards_any
        rows_spec, blk_spec = P(everyone), P(("chip", "core"))
        mesh = Mesh(mesh.devices.reshape(chips, 2, grp), everyone)
    in_specs = (rows_spec, blk_spec, blk_spec, rows_spec, blk_spec)
    out_specs = (rows_spec, blk_spec)
    return jax.shard_map(shards, mesh=mesh, in_specs=in_specs, out_specs=out_specs, check_vma=False)
```

```python
import functools
import math

import jax
import jax.numpy as jnp
from jax import lax
from jax.experimental import pallas as pl
from jax.experimental.pallas import tpu as pltpu
from jax.sharding import Mesh, PartitionSpec as P

ITERS = 2
epsilon = 0.1
inverse_eps = 10.0
LOG2E = math.log2(math.e)
LN2 = math.log(2.0)
LANES = 128
SPARE = 8
SUBLANES = 8


def fetch(array, axis, step, size):
    return lax.ppermute(array, axis, [(i ^ step, i) for i in range(size)])


def doubled(held, step, chips):
    return jnp.concatenate([held, fetch(held, "chip", step, chips)])


def gather_any(array, small, chips):
    pair = jnp.stack([array, fetch(array, "core", 1, 2)])[None]
    smalls = jnp.stack([small, fetch(small, "core", 1, 2)])[None]
    step = 1
    while step < chips:
        pair = doubled(pair, step, chips)
        smalls = doubled(smalls, step, chips)
        step *= 2
    return pair.reshape(-1, array.shape[1]), smalls.reshape(-1, *small.shape)


def as_column(row):
    size = row.shape[1]
    here = lax.broadcasted_iota(jnp.int32, (LANES, LANES), 0)
    there = lax.broadcasted_iota(jnp.int32, (LANES, LANES), 1)
    parts = []
    for start in range(0, size, LANES):
        wide = jnp.broadcast_to(row[:, start : start + LANES], (LANES, LANES))
        parts.append(jnp.sum(jnp.where(here == there, wide, 0.0), axis=1, keepdims=True))
    return jnp.concatenate(parts, axis=0)


def as_row(column):
    size = column.shape[0]
    here = lax.broadcasted_iota(jnp.int32, (LANES, LANES), 0)
    there = lax.broadcasted_iota(jnp.int32, (LANES, LANES), 1)
    parts = []
    for start in range(0, size, LANES):
        wide = jnp.broadcast_to(column[start : start + LANES], (LANES, LANES))
        parts.append(jnp.sum(jnp.where(here == there, wide, 0.0), axis=0, keepdims=True))
    return jnp.concatenate(parts, axis=1)


CHUNK = 64


def chunks_of(rows):
    return [pl.ds(start, CHUNK) for start in range(0, rows, CHUNK)]


def row_sweep(score_of, blocks, rows, found_of, columns=None, others=None):
    tops = []
    for at in chunks_of(rows):
        top = None if others is None else others[at, :]
        for p in blocks:
            score = score_of(at, p)
            score = score if columns is None else score + columns[p]
            top = score if top is None else jnp.maximum(top, score)
        tops.append(jnp.max(top, axis=1, keepdims=True))
    for at, top in zip(chunks_of(rows), tops):
        total = None
        for p in blocks:
            shift = -top if columns is None else columns[p] - top
            term = jnp.exp2(score_of(at, p) + shift)
            total = term if total is None else total + term
        total = jnp.sum(total, axis=1, keepdims=True)
        if others is not None:
            total = total + jnp.exp2(others[at, :] - top)
        found_of(at, top + jnp.log2(total))


def column_sweep(score_of, blocks, rows, row_pot, found_of):
    folds = (CHUNK // SUBLANES, SUBLANES, LANES)
    found = [[] for _ in blocks]
    for at in chunks_of(rows):
        addend = row_pot[at, :]
        for p in blocks:
            score = (score_of(at, p) + addend).reshape(folds)
            top = jnp.max(score, axis=0)
            found[p].append((top, jnp.sum(jnp.exp2(score - top[None]), axis=0)))
    for p in blocks:
        top = functools.reduce(jnp.maximum, [each for each, _ in found[p]])
        top = jnp.max(top, axis=0, keepdims=True)
        total = sum(each * jnp.exp2(at_top - top) for at_top, each in found[p])
        found_of(p, top + jnp.log2(jnp.sum(total, axis=0, keepdims=True)))


def products(source, targets, factor, smalls, scaled, table):
    for p, small in enumerate(smalls):
        table[0, p : p + 1, :] = small[1:2] * LOG2E
        table[1, p : p + 1, :] = small[0:1] * (inverse_eps * LOG2E)
    for p in range(0, len(smalls), 2):
        lanes = slice(p * LANES, (p + 2) * LANES)
        product = lax.dot_general(
            source[...], targets[lanes, :], (((1,), (1,)), ((), ())),
            preferred_element_type=jnp.float32,
        )
        shift = jnp.concatenate([table[1, p : p + 1, :], table[1, p + 1 : p + 2, :]], axis=1)
        scaled[:, lanes] = product * factor + shift


def head_kernel(
    own, init, target_logw, first, second, whole, small, first_plain, second_plain, init_row,
    logw_row, sems,
):
    rows, half = own.shape[0], first_plain.shape[0]
    copies = [
        pltpu.make_async_copy(own, whole.at[0:rows], sems.at[0]),
        pltpu.make_async_copy(init, init_row, sems.at[1]),
        pltpu.make_async_copy(target_logw, logw_row, sems.at[2]),
    ]
    for copy in copies:
        copy.start()
    for copy in copies:
        copy.wait()
    for out in (first, first_plain):
        out[0:half, :] = whole[0:half, :]
    for out in (second, second_plain):
        out[0:half, :] = whole[half:rows, :]
    small[0:1, :] = init_row[...]
    small[1:2, :] = logw_row[...]
    filler = jnp.zeros((SPARE - 2, LANES), jnp.float32)
    rest = jnp.concatenate([init_row[...], logw_row[...], filler], axis=0)
    for k in range(whole.shape[1] // LANES):
        lanes = slice(k * LANES, (k + 1) * LANES)
        part = (rest if k < 3 else jnp.zeros_like(rest)).astype(whole.dtype)
        first[half:, lanes] = part
        second[half:, lanes] = part
        whole[rows:, lanes] = part
        rest = rest - part.astype(jnp.float32)


def source_kernel(source, logw, whole, held, row_logw, passed, rows_row, sems):
    copies = [
        pltpu.make_async_copy(source, held, sems.at[0]),
        pltpu.make_async_copy(logw, rows_row, sems.at[1]),
    ]
    for copy in copies:
        copy.start()
    passed[...] = whole[...]
    for copy in copies:
        copy.wait()
    row_logw[...] = jnp.broadcast_to(as_column(rows_row[...] * LOG2E), row_logw.shape)


def sibling_kernel(whole, a_first, a_second, b_first, b_second, out):
    half = a_second.shape[0]
    block = 2 * half + SPARE
    out[0:block, :] = whole[...]
    out[block : block + half, :] = a_first[0:half, :]
    out[block + half : block + 2 * half, :] = a_second[...]
    out[block + 2 * half : 2 * block, :] = a_first[half:, :]
    out[2 * block : 2 * block + half, :] = b_first[...]
    out[2 * block + half : 3 * block, :] = b_second[...]


def unpack(message, end=None):
    end = message.shape[0] if end is None else end
    parts = [
        message[end - SPARE : end, k * LANES : (k + 1) * LANES].astype(jnp.float32)[0:2]
        for k in range(3)
    ]
    return (parts[0] + parts[1]) + parts[2]


def near_kernel(
    factor, source, whole, a_first, a_second, b_first, b_second, sibling, scaled, table, found,
    targets,
):
    half = a_second.shape[0]
    width = 2 * half
    block = width + SPARE
    targets[0:width, :] = whole[0:width, :]
    for k, piece in enumerate((a_first, a_second)):
        targets[2 * width + k * half : 2 * width + (k + 1) * half, :] = piece[0:half, :]
    for k, piece in enumerate((b_first, b_second)):
        targets[4 * width + k * half : 4 * width + (k + 1) * half, :] = piece[0:half, :]
    for k in range(3):
        start = (2 * k + 1) * width
        targets[start : start + width, :] = sibling[k * block : k * block + width, :]
    smalls = []
    for k, message in enumerate((whole, a_first, b_second)):
        smalls += [unpack(message), unpack(sibling, (k + 1) * block)]
    products(source, targets, factor, smalls, scaled, table)

    def score_of(at, p):
        return scaled[at, p * LANES : (p + 1) * LANES]

    def found_of(at, value):
        found[at, :] = jnp.broadcast_to(value, (CHUNK, LANES))

    row_sweep(score_of, range(len(smalls)), scaled.shape[0], found_of)


def pass_kernel(message, out):
    out[...] = message[...]


def far_kernel(
    factor, source, far_a, far_b, sibling_a, sibling_b, near, scaled, table, targets
):
    half = targets.shape[0] // 4
    for k, piece in enumerate((far_a, far_b, sibling_a, sibling_b)):
        targets[k * half : (k + 1) * half, :] = piece[0:half, :]
    smalls = [unpack(far_a), unpack(sibling_a)]
    products(source, targets, factor, smalls, scaled, table)


def neighbour_step(me, turn):
    step = 2 + 2 * (me % 2)
    return step if turn == 0 else 6 - step


def positions(me):
    sibling = me ^ 1
    own = [me, me ^ neighbour_step(me, 0), me ^ neighbour_step(me, 1), me ^ 6]
    other = [
        sibling,
        sibling ^ neighbour_step(sibling, 0),
        sibling ^ neighbour_step(sibling, 1),
        sibling ^ 6,
    ]
    return [block for pair in zip(own, other) for block in pair]


class Held:

    def __init__(self, near, near_table, far, far_table):
        self.count = near.shape[1] // LANES
        self.total = self.count + far.shape[1] // LANES
        self.near, self.near_table, self.far, self.far_table = near, near_table, far, far_table

    def score(self, at, p):
        part, p = (self.near, p) if p < self.count else (self.far, p - self.count)
        return part[at, p * LANES : (p + 1) * LANES]

    def row(self, kind, p):
        table, p = (self.near_table, p) if p < self.count else (self.far_table, p - self.count)
        return table[kind, p : p + 1, :]


def first_kernel(near, near_table, found, far, far_table, logw, message, row_pot, ordered):
    order = positions(lax.axis_index("blk"))
    held = Held(near, near_table, far, far_table)
    rows = near.shape[0]

    def row_found(at, value):
        row_pot[at, :] = logw[at, :] - value

    def column_found(p, value):
        ordered[pl.ds(order[p], 1), :] = value - held.row(1, p)

    row_sweep(held.score, range(held.count, held.total), rows, row_found, others=found)
    column_sweep(held.score, range(held.total), rows, row_pot, column_found)
    message[...] = jnp.broadcast_to(ordered[...][None], message.shape)


def second_kernel(
    copies, near, near_table, far, far_table, got, logw, row, message, row_pot, ordered
):
    order = positions(lax.axis_index("blk"))
    held = Held(near, near_table, far, far_table)
    rows = near.shape[0]
    values = got[...]
    top = jnp.max(values, axis=0)
    ordered[...] = top + jnp.log2(jnp.sum(jnp.exp2(values - top[None]), axis=0))
    columns = []
    for p in range(held.total):
        columns.append(held.row(0, p) - ordered[pl.ds(order[p], 1), :] - held.row(1, p))

    def row_found(at, value):
        row_pot[at, :] = logw[at, :] - value

    def column_found(p, value):
        at = pl.ds((held.total - 1 - order[p]) * copies, copies)
        message[at, :] = jnp.broadcast_to(value - held.row(1, p), (copies, LANES))

    row_sweep(held.score, range(held.total), rows, row_found, columns=columns)
    column_sweep(held.score, range(held.total), rows, row_pot, column_found)
    row[...] = as_row(row_pot[:, 0:1]) * (epsilon * LN2)


def last_kernel(got, small, row, row_out, column_out):
    values = got[...]
    top = jnp.max(values, axis=0, keepdims=True)
    total = top + jnp.log2(jnp.sum(jnp.exp2(values - top), axis=0, keepdims=True))
    column_out[...] = epsilon * small[1:2, :] - (epsilon * LN2) * total
    row_out[...] = row[...]


def lse(values):
    top = jnp.max(values, axis=0)
    return top + jnp.log(jnp.sum(jnp.exp(values - top[None]), axis=0))


def solution(mesh):
    blk, grp = mesh.shape["blk"], mesh.shape["grp"]
    chips = blk // 2
    everyone = ("chip", "core", "grp")

    def shards_square(source_embed, target_embed, target_init, source_logw, target_logw):
        rows, depth = source_embed.shape
        width = target_embed.shape[0]
        half = width // 2
        factor = inverse_eps * LOG2E / math.sqrt(depth)
        vmem, hbm = pl.BlockSpec(memory_space=pltpu.VMEM), pl.BlockSpec(memory_space=pltpu.HBM)
        params = pltpu.CompilerParams(vmem_limit_bytes=16 * 1024 * 1024)

        def values(*shape):
            return jax.ShapeDtypeStruct(shape, jnp.float32)

        def cost(targets, sweeps):
            return pl.CostEstimate(
                flops=2 * rows * targets * depth + 16 * sweeps * rows * blk * width,
                transcendentals=2 * sweeps * rows * blk * width,
                bytes_accessed=2 * (rows + targets) * depth,
            )

        def along(array, turn):
            return lax.ppermute(
                array, "blk", [(i ^ neighbour_step(i, turn), i) for i in range(blk)]
            )

        def to_sibling(array):
            return fetch(array, "blk", 1, blk)

        def exchange(message):
            order = list(range(blk * grp))[::-1]
            return lax.all_to_all(message, ("blk", "grp"), 0, 0, axis_index_groups=[order])

        def block_of(size):
            return jax.ShapeDtypeStruct((size, depth), target_embed.dtype)

        def in_hbm(*arrays):
            return [pltpu.with_memory_space_constraint(each, pltpu.HBM) for each in arrays]

        first, second, whole, small, first_plain, second_plain = pl.pallas_call(
            head_kernel,
            out_shape=(
                block_of(half + SPARE),
                block_of(half + SPARE),
                block_of(width + SPARE),
                values(2, width),
                block_of(half),
                block_of(half),
            ),
            in_specs=[hbm] * 3,
            out_specs=(vmem,) * 6,
            scratch_shapes=[
                pltpu.VMEM((1, width), jnp.float32),
                pltpu.VMEM((1, width), jnp.float32),
                pltpu.SemaphoreType.DMA((3,)),
            ],
            compiler_params=params,
        )(*in_hbm(target_embed, target_init.reshape(1, width), target_logw.reshape(1, width)))
        a_first = along(first, 0)
        b_second = along(second, 1)
        a_second = along(second_plain, 0)
        b_first = along(first_plain, 1)
        far_a = along(a_first, 1)
        far_b = along(b_second, 0)
        source, logw, passed = pl.pallas_call(
            source_kernel,
            out_shape=(
                jax.ShapeDtypeStruct((rows, depth), source_embed.dtype),
                values(rows, LANES),
                block_of(width + SPARE),
            ),
            in_specs=[hbm] * 2 + [vmem],
            out_specs=(vmem,) * 3,
            scratch_shapes=[pltpu.VMEM((1, rows), jnp.float32), pltpu.SemaphoreType.DMA((2,))],
            compiler_params=params,
        )(*in_hbm(source_embed, source_logw.reshape(1, rows)), whole)
        near = (a_first, a_second, b_first, b_second)
        sibling = pl.pallas_call(
            sibling_kernel,
            out_shape=block_of(3 * (width + SPARE)),
            in_specs=[vmem] * 5,
            out_specs=vmem,
            compiler_params=params,
            cost_estimate=cost(0, 0),
        )(passed, *near)
        sibling = to_sibling(sibling)

        def passed_on(message, weight):
            return pl.pallas_call(
                pass_kernel,
                out_shape=jax.ShapeDtypeStruct(message.shape, message.dtype),
                in_specs=[vmem],
                out_specs=vmem,
                compiler_params=params,
                cost_estimate=cost(weight * width, 0),
            )(message)

        sibling_a = to_sibling(passed_on(far_a, 0))
        sibling_b = to_sibling(passed_on(far_b, 50))

        def table():
            return values(2, SUBLANES, width)

        scores_near, table_near, found = pl.pallas_call(
            functools.partial(near_kernel, factor),
            out_shape=(values(rows, 6 * width), table(), values(rows, LANES)),
            in_specs=[vmem] * 7,
            out_specs=(vmem,) * 3,
            scratch_shapes=[pltpu.VMEM((6 * width, depth), target_embed.dtype)],
            compiler_params=params,
            cost_estimate=cost(0, 0),
        )(source, whole, *near, sibling)
        scores_far, table_far = pl.pallas_call(
            functools.partial(far_kernel, factor),
            out_shape=(values(rows, 2 * width), table()),
            in_specs=[vmem] * 6,
            out_specs=(vmem, vmem),
            scratch_shapes=[pltpu.VMEM((2 * width, depth), target_embed.dtype)],
            compiler_params=params,
            cost_estimate=cost(0, 0),
        )(source, far_a, far_b, sibling_a, sibling_b, scores_near)
        scores = (scores_far, table_far)
        row_scratch = pltpu.VMEM((rows, LANES), jnp.float32)
        block_scratch = pltpu.VMEM((blk, width), jnp.float32)
        message = pl.pallas_call(
            first_kernel,
            out_shape=values(blk * grp, blk, width),
            in_specs=[vmem] * 6,
            out_specs=vmem,
            scratch_shapes=[row_scratch, block_scratch],
            compiler_params=params,
            cost_estimate=cost(0, 1),
        )(scores_near, table_near, found, *scores, logw)
        got = exchange(message)
        row, message = pl.pallas_call(
            functools.partial(second_kernel, grp),
            out_shape=(values(1, rows), values(blk * grp, width)),
            in_specs=[vmem] * 6,
            out_specs=(vmem, vmem),
            scratch_shapes=[row_scratch, block_scratch],
            compiler_params=params,
            cost_estimate=cost(0, 1),
        )(scores_near, table_near, *scores, got, logw)
        got = exchange(message)
        row_pot, column_pot = pl.pallas_call(
            last_kernel,
            out_shape=(values(1, rows), values(1, width)),
            in_specs=[vmem] * 3,
            out_specs=(vmem, vmem),
            compiler_params=params,
        )(got, small, row)
        return row_pot.reshape(rows), column_pot.reshape(width)

    def shards_any(source_embed, target_embed, target_init, source_logw, target_logw):
        width, depth = target_embed.shape
        factor = -1.0 / math.sqrt(depth)
        me = lax.axis_index("chip") * 2 + lax.axis_index("core")

        def swap_order(values):
            parts = values.reshape(blk, width)
            step = 1
            while step < blk:
                pairs = parts.reshape(blk // (2 * step), 2, step, width)
                pairs = jnp.where(me & step, pairs[:, ::-1], pairs)
                parts = pairs.reshape(blk, width)
                step *= 2
            return parts

        small = jnp.stack([target_init, target_logw])
        targets, smalls = gather_any(target_embed, small, chips)
        cost = (
            lax.dot_general(
                source_embed, targets, (((1,), (1,)), ((), ())), preferred_element_type=jnp.float32
            )
            * factor
        )
        column_pot, logw_all = smalls[:, 0].reshape(-1), smalls[:, 1].reshape(-1)
        for iteration in range(ITERS):
            scores = (column_pot[None, :] - cost) * inverse_eps
            row_top = jnp.max(scores, axis=1)
            row_sum = jnp.sum(jnp.exp(scores - row_top[:, None]), axis=1)
            row_pot = epsilon * source_logw - epsilon * (row_top + jnp.log(row_sum))
            part = swap_order(lse((row_pot[:, None] - cost) * inverse_eps))
            if iteration < ITERS - 1:
                copies = jnp.broadcast_to(part[None], (blk * grp, blk, width))
                got = lax.all_to_all(copies, everyone, 0, 0)
                total = swap_order(lse(got)).reshape(-1)
                column_pot = epsilon * logw_all - epsilon * total
            else:
                copies = jnp.broadcast_to(part[:, None], (blk, grp, width)).reshape(blk * grp, width)
                got = lax.all_to_all(copies, everyone, 0, 0)
                own_column = epsilon * target_logw - epsilon * lse(got)
        return row_pot, own_column

    if chips == 4:
        shards = shards_square
        rows_spec, blk_spec = P(("blk", "grp")), P("blk")
    else:
        shards = shards_any
        rows_spec, blk_spec = P(everyone), P(("chip", "core"))
        mesh = Mesh(mesh.devices.reshape(chips, 2, grp), everyone)
    in_specs = (rows_spec, blk_spec, blk_spec, rows_spec, blk_spec)
    out_specs = (rows_spec, blk_spec)
    return jax.shard_map(shards, mesh=mesh, in_specs=in_specs, out_specs=out_specs, check_vma=False)
```

```python
import functools
import math

import jax
import jax.numpy as jnp
from jax import lax
from jax.experimental import pallas as pl
from jax.experimental.pallas import tpu as pltpu
from jax.sharding import Mesh, PartitionSpec as P

ITERS = 2
epsilon = 0.1
inverse_eps = 10.0
LOG2E = math.log2(math.e)
LN2 = math.log(2.0)
LANES = 128
SPARE = 8
SUBLANES = 8


def fetch(array, axis, step, size):
    return lax.ppermute(array, axis, [(i ^ step, i) for i in range(size)])


def doubled(held, step, chips):
    return jnp.concatenate([held, fetch(held, "chip", step, chips)])


def gather_any(array, small, chips):
    pair = jnp.stack([array, fetch(array, "core", 1, 2)])[None]
    smalls = jnp.stack([small, fetch(small, "core", 1, 2)])[None]
    step = 1
    while step < chips:
        pair = doubled(pair, step, chips)
        smalls = doubled(smalls, step, chips)
        step *= 2
    return pair.reshape(-1, array.shape[1]), smalls.reshape(-1, *small.shape)


def as_column(row):
    size = row.shape[1]
    here = lax.broadcasted_iota(jnp.int32, (LANES, LANES), 0)
    there = lax.broadcasted_iota(jnp.int32, (LANES, LANES), 1)
    parts = []
    for start in range(0, size, LANES):
        wide = jnp.broadcast_to(row[:, start : start + LANES], (LANES, LANES))
        parts.append(jnp.sum(jnp.where(here == there, wide, 0.0), axis=1, keepdims=True))
    return jnp.concatenate(parts, axis=0)


def as_row(column):
    size = column.shape[0]
    here = lax.broadcasted_iota(jnp.int32, (LANES, LANES), 0)
    there = lax.broadcasted_iota(jnp.int32, (LANES, LANES), 1)
    parts = []
    for start in range(0, size, LANES):
        wide = jnp.broadcast_to(column[start : start + LANES], (LANES, LANES))
        parts.append(jnp.sum(jnp.where(here == there, wide, 0.0), axis=0, keepdims=True))
    return jnp.concatenate(parts, axis=1)


CHUNK = 64


def chunks_of(rows):
    return [pl.ds(start, CHUNK) for start in range(0, rows, CHUNK)]


def row_sweep(score_of, blocks, rows, found_of, columns=None, others=None):
    tops = []
    for at in chunks_of(rows):
        top = None if others is None else others[at, :]
        for p in blocks:
            score = score_of(at, p)
            score = score if columns is None else score + columns[p]
            top = score if top is None else jnp.maximum(top, score)
        tops.append(jnp.max(top, axis=1, keepdims=True))
    for at, top in zip(chunks_of(rows), tops):
        total = None
        for p in blocks:
            shift = -top if columns is None else columns[p] - top
            term = jnp.exp2(score_of(at, p) + shift)
            total = term if total is None else total + term
        total = jnp.sum(total, axis=1, keepdims=True)
        if others is not None:
            total = total + jnp.exp2(others[at, :] - top)
        found_of(at, top + jnp.log2(total))


def column_sweep(score_of, blocks, rows, row_pot, found_of):
    folds = (CHUNK // SUBLANES, SUBLANES, LANES)
    found = [[] for _ in blocks]
    for at in chunks_of(rows):
        addend = row_pot[at, :]
        for p in blocks:
            score = (score_of(at, p) + addend).reshape(folds)
            top = jnp.max(score, axis=0)
            found[p].append((top, jnp.sum(jnp.exp2(score - top[None]), axis=0)))
    for p in blocks:
        top = functools.reduce(jnp.maximum, [each for each, _ in found[p]])
        top = jnp.max(top, axis=0, keepdims=True)
        total = sum(each * jnp.exp2(at_top - top) for at_top, each in found[p])
        found_of(p, top + jnp.log2(jnp.sum(total, axis=0, keepdims=True)))


def products(source, targets, factor, smalls, scaled, table):
    for p, small in enumerate(smalls):
        table[0, p : p + 1, :] = small[1:2] * LOG2E
        table[1, p : p + 1, :] = small[0:1] * (inverse_eps * LOG2E)
    for p in range(0, len(smalls), 2):
        lanes = slice(p * LANES, (p + 2) * LANES)
        product = lax.dot_general(
            source[...], targets[lanes, :], (((1,), (1,)), ((), ())),
            preferred_element_type=jnp.float32,
        )
        shift = jnp.concatenate([table[1, p : p + 1, :], table[1, p + 1 : p + 2, :]], axis=1)
        scaled[:, lanes] = product * factor + shift


def head_kernel(
    own, init, target_logw, first, second, whole, small, first_plain, second_plain, init_row,
    logw_row, sems,
):
    rows, half = own.shape[0], first_plain.shape[0]
    copies = [
        pltpu.make_async_copy(own, whole.at[0:rows], sems.at[0]),
        pltpu.make_async_copy(init, init_row, sems.at[1]),
        pltpu.make_async_copy(target_logw, logw_row, sems.at[2]),
    ]
    for copy in copies:
        copy.start()
    for copy in copies:
        copy.wait()
    for out in (first, first_plain):
        out[0:half, :] = whole[0:half, :]
    for out in (second, second_plain):
        out[0:half, :] = whole[half:rows, :]
    small[0:1, :] = init_row[...]
    small[1:2, :] = logw_row[...]
    filler = jnp.zeros((SPARE - 2, LANES), jnp.float32)
    rest = jnp.concatenate([init_row[...], logw_row[...], filler], axis=0)
    for k in range(whole.shape[1] // LANES):
        lanes = slice(k * LANES, (k + 1) * LANES)
        part = (rest if k < 3 else jnp.zeros_like(rest)).astype(whole.dtype)
        first[half:, lanes] = part
        second[half:, lanes] = part
        whole[rows:, lanes] = part
        rest = rest - part.astype(jnp.float32)


def source_kernel(
    source, logw, first, second, held, row_logw, first_out, second_out, rows_row, sems
):
    copies = [
        pltpu.make_async_copy(source, held, sems.at[0]),
        pltpu.make_async_copy(logw, rows_row, sems.at[1]),
    ]
    for copy in copies:
        copy.start()
    first_out[...] = first[...]
    second_out[...] = second[...]
    for copy in copies:
        copy.wait()
    row_logw[...] = jnp.broadcast_to(as_column(rows_row[...] * LOG2E), row_logw.shape)


def sibling_kernel(whole, a_first, a_second, b_first, b_second, out):
    half = a_second.shape[0]
    block = 2 * half + SPARE
    out[0:block, :] = whole[...]
    out[block : block + half, :] = a_first[0:half, :]
    out[block + half : block + 2 * half, :] = a_second[...]
    out[block + 2 * half : 2 * block, :] = a_first[half:, :]
    out[2 * block : 2 * block + half, :] = b_first[...]
    out[2 * block + half : 3 * block, :] = b_second[...]


def unpack(message, end=None):
    end = message.shape[0] if end is None else end
    parts = [
        message[end - SPARE : end, k * LANES : (k + 1) * LANES].astype(jnp.float32)[0:2]
        for k in range(3)
    ]
    return (parts[0] + parts[1]) + parts[2]


def near_kernel(
    factor, source, whole, a_first, a_second, b_first, b_second, sibling, scaled, table, found,
    targets,
):
    half = a_second.shape[0]
    width = 2 * half
    block = width + SPARE
    targets[0:width, :] = whole[0:width, :]
    for k, piece in enumerate((a_first, a_second)):
        targets[2 * width + k * half : 2 * width + (k + 1) * half, :] = piece[0:half, :]
    for k, piece in enumerate((b_first, b_second)):
        targets[4 * width + k * half : 4 * width + (k + 1) * half, :] = piece[0:half, :]
    for k in range(3):
        start = (2 * k + 1) * width
        targets[start : start + width, :] = sibling[k * block : k * block + width, :]
    smalls = []
    for k, message in enumerate((whole, a_first, b_second)):
        smalls += [unpack(message), unpack(sibling, (k + 1) * block)]
    products(source, targets, factor, smalls, scaled, table)

    def score_of(at, p):
        return scaled[at, p * LANES : (p + 1) * LANES]

    def found_of(at, value):
        found[at, :] = jnp.broadcast_to(value, (CHUNK, LANES))

    row_sweep(score_of, range(len(smalls)), scaled.shape[0], found_of)


def pass_kernel(message, out):
    out[...] = message[...]


def far_kernel(
    factor, source, far_a, far_b, sibling_a, sibling_b, near, scaled, table, targets
):
    half = targets.shape[0] // 4
    for k, piece in enumerate((far_a, far_b, sibling_a, sibling_b)):
        targets[k * half : (k + 1) * half, :] = piece[0:half, :]
    smalls = [unpack(far_a), unpack(sibling_a)]
    products(source, targets, factor, smalls, scaled, table)


def neighbour_step(me, turn):
    step = 2 + 2 * (me % 2)
    return step if turn == 0 else 6 - step


def positions(me):
    sibling = me ^ 1
    own = [me, me ^ neighbour_step(me, 0), me ^ neighbour_step(me, 1), me ^ 6]
    other = [
        sibling,
        sibling ^ neighbour_step(sibling, 0),
        sibling ^ neighbour_step(sibling, 1),
        sibling ^ 6,
    ]
    return [block for pair in zip(own, other) for block in pair]


class Held:

    def __init__(self, near, near_table, far, far_table):
        self.count = near.shape[1] // LANES
        self.total = self.count + far.shape[1] // LANES
        self.near, self.near_table, self.far, self.far_table = near, near_table, far, far_table

    def score(self, at, p):
        part, p = (self.near, p) if p < self.count else (self.far, p - self.count)
        return part[at, p * LANES : (p + 1) * LANES]

    def row(self, kind, p):
        table, p = (self.near_table, p) if p < self.count else (self.far_table, p - self.count)
        return table[kind, p : p + 1, :]


def first_kernel(near, near_table, found, far, far_table, logw, message, row_pot, ordered):
    order = positions(lax.axis_index("blk"))
    held = Held(near, near_table, far, far_table)
    rows = near.shape[0]

    def row_found(at, value):
        row_pot[at, :] = logw[at, :] - value

    def column_found(p, value):
        ordered[pl.ds(order[p], 1), :] = value - held.row(1, p)

    row_sweep(held.score, range(held.count, held.total), rows, row_found, others=found)
    column_sweep(held.score, range(held.total), rows, row_pot, column_found)
    message[...] = jnp.broadcast_to(ordered[...][None], message.shape)


def second_kernel(
    copies, near, near_table, far, far_table, got, logw, row, message, row_pot, ordered
):
    order = positions(lax.axis_index("blk"))
    held = Held(near, near_table, far, far_table)
    rows = near.shape[0]
    values = got[...]
    top = jnp.max(values, axis=0)
    ordered[...] = top + jnp.log2(jnp.sum(jnp.exp2(values - top[None]), axis=0))
    columns = []
    for p in range(held.total):
        columns.append(held.row(0, p) - ordered[pl.ds(order[p], 1), :] - held.row(1, p))

    def row_found(at, value):
        row_pot[at, :] = logw[at, :] - value

    def column_found(p, value):
        at = pl.ds((held.total - 1 - order[p]) * copies, copies)
        message[at, :] = jnp.broadcast_to(value - held.row(1, p), (copies, LANES))

    row_sweep(held.score, range(held.total), rows, row_found, columns=columns)
    column_sweep(held.score, range(held.total), rows, row_pot, column_found)
    row[...] = as_row(row_pot[:, 0:1]) * (epsilon * LN2)


def last_kernel(got, small, row, row_out, column_out):
    values = got[...]
    top = jnp.max(values, axis=0, keepdims=True)
    total = top + jnp.log2(jnp.sum(jnp.exp2(values - top), axis=0, keepdims=True))
    column_out[...] = epsilon * small[1:2, :] - (epsilon * LN2) * total
    row_out[...] = row[...]


def lse(values):
    top = jnp.max(values, axis=0)
    return top + jnp.log(jnp.sum(jnp.exp(values - top[None]), axis=0))


def solution(mesh):
    blk, grp = mesh.shape["blk"], mesh.shape["grp"]
    chips = blk // 2
    everyone = ("chip", "core", "grp")

    def shards_square(source_embed, target_embed, target_init, source_logw, target_logw):
        rows, depth = source_embed.shape
        width = target_embed.shape[0]
        half = width // 2
        factor = inverse_eps * LOG2E / math.sqrt(depth)
        vmem, hbm = pl.BlockSpec(memory_space=pltpu.VMEM), pl.BlockSpec(memory_space=pltpu.HBM)
        params = pltpu.CompilerParams(vmem_limit_bytes=16 * 1024 * 1024)

        def values(*shape):
            return jax.ShapeDtypeStruct(shape, jnp.float32)

        def cost(targets, sweeps):
            return pl.CostEstimate(
                flops=2 * rows * targets * depth + 16 * sweeps * rows * blk * width,
                transcendentals=2 * sweeps * rows * blk * width,
                bytes_accessed=2 * (rows + targets) * depth,
            )

        def along(array, turn):
            return lax.ppermute(
                array, "blk", [(i ^ neighbour_step(i, turn), i) for i in range(blk)]
            )

        def to_sibling(array):
            return fetch(array, "blk", 1, blk)

        def exchange(message):
            order = list(range(blk * grp))[::-1]
            return lax.all_to_all(message, ("blk", "grp"), 0, 0, axis_index_groups=[order])

        def block_of(size):
            return jax.ShapeDtypeStruct((size, depth), target_embed.dtype)

        def in_hbm(*arrays):
            return [pltpu.with_memory_space_constraint(each, pltpu.HBM) for each in arrays]

        first, second, whole, small, first_plain, second_plain = pl.pallas_call(
            head_kernel,
            out_shape=(
                block_of(half + SPARE),
                block_of(half + SPARE),
                block_of(width + SPARE),
                values(2, width),
                block_of(half),
                block_of(half),
            ),
            in_specs=[hbm] * 3,
            out_specs=(vmem,) * 6,
            scratch_shapes=[
                pltpu.VMEM((1, width), jnp.float32),
                pltpu.VMEM((1, width), jnp.float32),
                pltpu.SemaphoreType.DMA((3,)),
            ],
            compiler_params=params,
        )(*in_hbm(target_embed, target_init.reshape(1, width), target_logw.reshape(1, width)))
        source, logw, first_plain, second_plain = pl.pallas_call(
            source_kernel,
            out_shape=(
                jax.ShapeDtypeStruct((rows, depth), source_embed.dtype),
                values(rows, LANES),
                block_of(half),
                block_of(half),
            ),
            in_specs=[hbm] * 2 + [vmem] * 2,
            out_specs=(vmem,) * 4,
            scratch_shapes=[pltpu.VMEM((1, rows), jnp.float32), pltpu.SemaphoreType.DMA((2,))],
            compiler_params=params,
        )(*in_hbm(source_embed, source_logw.reshape(1, rows)), first_plain, second_plain)
        a_first = along(first, 0)
        b_second = along(second, 1)
        a_second = along(second_plain, 0)
        b_first = along(first_plain, 1)
        far_a = along(a_first, 1)
        far_b = along(b_second, 0)
        near = (a_first, a_second, b_first, b_second)
        sibling = pl.pallas_call(
            sibling_kernel,
            out_shape=block_of(3 * (width + SPARE)),
            in_specs=[vmem] * 5,
            out_specs=vmem,
            compiler_params=params,
            cost_estimate=cost(0, 0),
        )(whole, *near)
        sibling = to_sibling(sibling)

        def passed_on(message, weight):
            return pl.pallas_call(
                pass_kernel,
                out_shape=jax.ShapeDtypeStruct(message.shape, message.dtype),
                in_specs=[vmem],
                out_specs=vmem,
                compiler_params=params,
                cost_estimate=cost(weight * width, 0),
            )(message)

        sibling_a = to_sibling(passed_on(far_a, 0))
        sibling_b = to_sibling(passed_on(far_b, 50))

        def table():
            return values(2, SUBLANES, width)

        scores_near, table_near, found = pl.pallas_call(
            functools.partial(near_kernel, factor),
            out_shape=(values(rows, 6 * width), table(), values(rows, LANES)),
            in_specs=[vmem] * 7,
            out_specs=(vmem,) * 3,
            scratch_shapes=[pltpu.VMEM((6 * width, depth), target_embed.dtype)],
            compiler_params=params,
            cost_estimate=cost(0, 0),
        )(source, whole, *near, sibling)
        scores_far, table_far = pl.pallas_call(
            functools.partial(far_kernel, factor),
            out_shape=(values(rows, 2 * width), table()),
            in_specs=[vmem] * 6,
            out_specs=(vmem, vmem),
            scratch_shapes=[pltpu.VMEM((2 * width, depth), target_embed.dtype)],
            compiler_params=params,
            cost_estimate=cost(0, 0),
        )(source, far_a, far_b, sibling_a, sibling_b, scores_near)
        scores = (scores_far, table_far)
        row_scratch = pltpu.VMEM((rows, LANES), jnp.float32)
        block_scratch = pltpu.VMEM((blk, width), jnp.float32)
        message = pl.pallas_call(
            first_kernel,
            out_shape=values(blk * grp, blk, width),
            in_specs=[vmem] * 6,
            out_specs=vmem,
            scratch_shapes=[row_scratch, block_scratch],
            compiler_params=params,
            cost_estimate=cost(0, 1),
        )(scores_near, table_near, found, *scores, logw)
        got = exchange(message)
        row, message = pl.pallas_call(
            functools.partial(second_kernel, grp),
            out_shape=(values(1, rows), values(blk * grp, width)),
            in_specs=[vmem] * 6,
            out_specs=(vmem, vmem),
            scratch_shapes=[row_scratch, block_scratch],
            compiler_params=params,
            cost_estimate=cost(0, 1),
        )(scores_near, table_near, *scores, got, logw)
        got = exchange(message)
        row_pot, column_pot = pl.pallas_call(
            last_kernel,
            out_shape=(values(1, rows), values(1, width)),
            in_specs=[vmem] * 3,
            out_specs=(vmem, vmem),
            compiler_params=params,
        )(got, small, row)
        return row_pot.reshape(rows), column_pot.reshape(width)

    def shards_any(source_embed, target_embed, target_init, source_logw, target_logw):
        width, depth = target_embed.shape
        factor = -1.0 / math.sqrt(depth)
        me = lax.axis_index("chip") * 2 + lax.axis_index("core")

        def swap_order(values):
            parts = values.reshape(blk, width)
            step = 1
            while step < blk:
                pairs = parts.reshape(blk // (2 * step), 2, step, width)
                pairs = jnp.where(me & step, pairs[:, ::-1], pairs)
                parts = pairs.reshape(blk, width)
                step *= 2
            return parts

        small = jnp.stack([target_init, target_logw])
        targets, smalls = gather_any(target_embed, small, chips)
        cost = (
            lax.dot_general(
                source_embed, targets, (((1,), (1,)), ((), ())), preferred_element_type=jnp.float32
            )
            * factor
        )
        column_pot, logw_all = smalls[:, 0].reshape(-1), smalls[:, 1].reshape(-1)
        for iteration in range(ITERS):
            scores = (column_pot[None, :] - cost) * inverse_eps
            row_top = jnp.max(scores, axis=1)
            row_sum = jnp.sum(jnp.exp(scores - row_top[:, None]), axis=1)
            row_pot = epsilon * source_logw - epsilon * (row_top + jnp.log(row_sum))
            part = swap_order(lse((row_pot[:, None] - cost) * inverse_eps))
            if iteration < ITERS - 1:
                copies = jnp.broadcast_to(part[None], (blk * grp, blk, width))
                got = lax.all_to_all(copies, everyone, 0, 0)
                total = swap_order(lse(got)).reshape(-1)
                column_pot = epsilon * logw_all - epsilon * total
            else:
                copies = jnp.broadcast_to(part[:, None], (blk, grp, width)).reshape(blk * grp, width)
                got = lax.all_to_all(copies, everyone, 0, 0)
                own_column = epsilon * target_logw - epsilon * lse(got)
        return row_pot, own_column

    if chips == 4:
        shards = shards_square
        rows_spec, blk_spec = P(("blk", "grp")), P("blk")
    else:
        shards = shards_any
        rows_spec, blk_spec = P(everyone), P(("chip", "core"))
        mesh = Mesh(mesh.devices.reshape(chips, 2, grp), everyone)
    in_specs = (rows_spec, blk_spec, blk_spec, rows_spec, blk_spec)
    out_specs = (rows_spec, blk_spec)
    return jax.shard_map(shards, mesh=mesh, in_specs=in_specs, out_specs=out_specs, check_vma=False)
```

```python
import functools
import math

import jax
import jax.numpy as jnp
from jax import lax
from jax.experimental import pallas as pl
from jax.experimental.pallas import tpu as pltpu
from jax.sharding import Mesh, PartitionSpec as P

ITERS = 2
epsilon = 0.1
inverse_eps = 10.0
LOG2E = math.log2(math.e)
LN2 = math.log(2.0)
LANES = 128
SPARE = 8
SUBLANES = 8


def fetch(array, axis, step, size):
    return lax.ppermute(array, axis, [(i ^ step, i) for i in range(size)])


def doubled(held, step, chips):
    return jnp.concatenate([held, fetch(held, "chip", step, chips)])


def gather_any(array, small, chips):
    pair = jnp.stack([array, fetch(array, "core", 1, 2)])[None]
    smalls = jnp.stack([small, fetch(small, "core", 1, 2)])[None]
    step = 1
    while step < chips:
        pair = doubled(pair, step, chips)
        smalls = doubled(smalls, step, chips)
        step *= 2
    return pair.reshape(-1, array.shape[1]), smalls.reshape(-1, *small.shape)


def as_column(row):
    size = row.shape[1]
    here = lax.broadcasted_iota(jnp.int32, (LANES, LANES), 0)
    there = lax.broadcasted_iota(jnp.int32, (LANES, LANES), 1)
    parts = []
    for start in range(0, size, LANES):
        wide = jnp.broadcast_to(row[:, start : start + LANES], (LANES, LANES))
        parts.append(jnp.sum(jnp.where(here == there, wide, 0.0), axis=1, keepdims=True))
    return jnp.concatenate(parts, axis=0)


def as_row(column):
    size = column.shape[0]
    here = lax.broadcasted_iota(jnp.int32, (LANES, LANES), 0)
    there = lax.broadcasted_iota(jnp.int32, (LANES, LANES), 1)
    parts = []
    for start in range(0, size, LANES):
        wide = jnp.broadcast_to(column[start : start + LANES], (LANES, LANES))
        parts.append(jnp.sum(jnp.where(here == there, wide, 0.0), axis=0, keepdims=True))
    return jnp.concatenate(parts, axis=1)


CHUNK = 64


def chunks_of(rows):
    return [pl.ds(start, CHUNK) for start in range(0, rows, CHUNK)]


def row_sweep(score_of, blocks, rows, found_of, columns=None, others=None):
    tops = []
    for at in chunks_of(rows):
        top = None if others is None else others[at, :]
        for p in blocks:
            score = score_of(at, p)
            score = score if columns is None else score + columns[p]
            top = score if top is None else jnp.maximum(top, score)
        tops.append(jnp.max(top, axis=1, keepdims=True))
    for at, top in zip(chunks_of(rows), tops):
        total = None
        for p in blocks:
            shift = -top if columns is None else columns[p] - top
            term = jnp.exp2(score_of(at, p) + shift)
            total = term if total is None else total + term
        total = jnp.sum(total, axis=1, keepdims=True)
        if others is not None:
            total = total + jnp.exp2(others[at, :] - top)
        found_of(at, top + jnp.log2(total))


def column_sweep(score_of, blocks, rows, row_pot, found_of):
    folds = (CHUNK // SUBLANES, SUBLANES, LANES)
    found = [[] for _ in blocks]
    for at in chunks_of(rows):
        addend = row_pot[at, :]
        for p in blocks:
            score = (score_of(at, p) + addend).reshape(folds)
            top = jnp.max(score, axis=0)
            found[p].append((top, jnp.sum(jnp.exp2(score - top[None]), axis=0)))
    for p in blocks:
        top = functools.reduce(jnp.maximum, [each for each, _ in found[p]])
        top = jnp.max(top, axis=0, keepdims=True)
        total = sum(each * jnp.exp2(at_top - top) for at_top, each in found[p])
        found_of(p, top + jnp.log2(jnp.sum(total, axis=0, keepdims=True)))


def products(source, targets, factor, smalls, scaled, table):
    for p, small in enumerate(smalls):
        table[0, p : p + 1, :] = small[1:2] * LOG2E
        table[1, p : p + 1, :] = small[0:1] * (inverse_eps * LOG2E)
    for p in range(0, len(smalls), 2):
        lanes = slice(p * LANES, (p + 2) * LANES)
        product = lax.dot_general(
            source[...], targets[lanes, :], (((1,), (1,)), ((), ())),
            preferred_element_type=jnp.float32,
        )
        shift = jnp.concatenate([table[1, p : p + 1, :], table[1, p + 1 : p + 2, :]], axis=1)
        scaled[:, lanes] = product * factor + shift


def head_kernel(
    own, init, target_logw, first, second, whole, small, first_plain, second_plain, init_row,
    logw_row, sems,
):
    rows, half = own.shape[0], first_plain.shape[0]
    copies = [
        pltpu.make_async_copy(own, whole.at[0:rows], sems.at[0]),
        pltpu.make_async_copy(init, init_row, sems.at[1]),
        pltpu.make_async_copy(target_logw, logw_row, sems.at[2]),
    ]
    for copy in copies:
        copy.start()
    for copy in copies:
        copy.wait()
    for out in (first, first_plain):
        out[0:half, :] = whole[0:half, :]
    for out in (second, second_plain):
        out[0:half, :] = whole[half:rows, :]
    small[0:1, :] = init_row[...]
    small[1:2, :] = logw_row[...]
    filler = jnp.zeros((SPARE - 2, LANES), jnp.float32)
    rest = jnp.concatenate([init_row[...], logw_row[...], filler], axis=0)
    for k in range(whole.shape[1] // LANES):
        lanes = slice(k * LANES, (k + 1) * LANES)
        part = (rest if k < 3 else jnp.zeros_like(rest)).astype(whole.dtype)
        first[half:, lanes] = part
        second[half:, lanes] = part
        whole[rows:, lanes] = part
        rest = rest - part.astype(jnp.float32)


def source_kernel(source, logw, whole, held, row_logw, passed, rows_row, sems):
    copies = [
        pltpu.make_async_copy(source, held, sems.at[0]),
        pltpu.make_async_copy(logw, rows_row, sems.at[1]),
    ]
    for copy in copies:
        copy.start()
    passed[...] = whole[...]
    for copy in copies:
        copy.wait()
    row_logw[...] = jnp.broadcast_to(as_column(rows_row[...] * LOG2E), row_logw.shape)


def sibling_kernel(whole, a_first, a_second, b_first, b_second, out):
    half = a_second.shape[0]
    block = 2 * half + SPARE
    out[0:block, :] = whole[...]
    out[block : block + half, :] = a_first[0:half, :]
    out[block + half : block + 2 * half, :] = a_second[...]
    out[block + 2 * half : 2 * block, :] = a_first[half:, :]
    out[2 * block : 2 * block + half, :] = b_first[...]
    out[2 * block + half : 3 * block, :] = b_second[...]


def unpack(message, end=None):
    end = message.shape[0] if end is None else end
    parts = [
        message[end - SPARE : end, k * LANES : (k + 1) * LANES].astype(jnp.float32)[0:2]
        for k in range(3)
    ]
    return (parts[0] + parts[1]) + parts[2]


def near_kernel(
    factor, source, whole, a_first, a_second, b_first, b_second, sibling, scaled, table, found,
    targets,
):
    half = a_second.shape[0]
    width = 2 * half
    block = width + SPARE
    targets[0:width, :] = whole[0:width, :]
    for k, piece in enumerate((a_first, a_second)):
        targets[2 * width + k * half : 2 * width + (k + 1) * half, :] = piece[0:half, :]
    for k, piece in enumerate((b_first, b_second)):
        targets[4 * width + k * half : 4 * width + (k + 1) * half, :] = piece[0:half, :]
    for k in range(3):
        start = (2 * k + 1) * width
        targets[start : start + width, :] = sibling[k * block : k * block + width, :]
    smalls = []
    for k, message in enumerate((whole, a_first, b_second)):
        smalls += [unpack(message), unpack(sibling, (k + 1) * block)]
    products(source, targets, factor, smalls, scaled, table)

    def score_of(at, p):
        return scaled[at, p * LANES : (p + 1) * LANES]

    def found_of(at, value):
        found[at, :] = jnp.broadcast_to(value, (CHUNK, LANES))

    row_sweep(score_of, range(len(smalls)), scaled.shape[0], found_of)


def pass_kernel(message, out):
    out[...] = message[...]


def far_kernel(
    factor, source, far_a, far_b, sibling_a, sibling_b, near, scaled, table, targets
):
    half = targets.shape[0] // 4
    for k, piece in enumerate((far_a, far_b, sibling_a, sibling_b)):
        targets[k * half : (k + 1) * half, :] = piece[0:half, :]
    smalls = [unpack(far_a), unpack(sibling_a)]
    products(source, targets, factor, smalls, scaled, table)


def neighbour_step(me, turn):
    step = 2 + 2 * (me % 2)
    return step if turn == 0 else 6 - step


def positions(me):
    sibling = me ^ 1
    own = [me, me ^ neighbour_step(me, 0), me ^ neighbour_step(me, 1), me ^ 6]
    other = [
        sibling,
        sibling ^ neighbour_step(sibling, 0),
        sibling ^ neighbour_step(sibling, 1),
        sibling ^ 6,
    ]
    return [block for pair in zip(own, other) for block in pair]


class Held:

    def __init__(self, near, near_table, far, far_table):
        self.count = near.shape[1] // LANES
        self.total = self.count + far.shape[1] // LANES
        self.near, self.near_table, self.far, self.far_table = near, near_table, far, far_table

    def score(self, at, p):
        part, p = (self.near, p) if p < self.count else (self.far, p - self.count)
        return part[at, p * LANES : (p + 1) * LANES]

    def row(self, kind, p):
        table, p = (self.near_table, p) if p < self.count else (self.far_table, p - self.count)
        return table[kind, p : p + 1, :]


def first_kernel(near, near_table, found, far, far_table, logw, message, row_pot, ordered):
    order = positions(lax.axis_index("blk"))
    held = Held(near, near_table, far, far_table)
    rows = near.shape[0]

    def row_found(at, value):
        row_pot[at, :] = logw[at, :] - value

    def column_found(p, value):
        ordered[pl.ds(order[p], 1), :] = value - held.row(1, p)

    row_sweep(held.score, range(held.count, held.total), rows, row_found, others=found)
    column_sweep(held.score, range(held.total), rows, row_pot, column_found)
    message[...] = jnp.broadcast_to(ordered[...][None], message.shape)


def second_kernel(
    near, near_table, far, far_table, got, logw, row, message, row_pot, ordered
):
    order = positions(lax.axis_index("blk"))
    held = Held(near, near_table, far, far_table)
    rows = near.shape[0]
    values = got[...]
    top = jnp.max(values, axis=0)
    ordered[...] = top + jnp.log2(jnp.sum(jnp.exp2(values - top[None]), axis=0))
    columns = []
    for p in range(held.total):
        columns.append(held.row(0, p) - ordered[pl.ds(order[p], 1), :] - held.row(1, p))

    def row_found(at, value):
        row_pot[at, :] = logw[at, :] - value

    def column_found(p, value):
        value = (value - held.row(1, p))[None]
        message[:, pl.ds(held.total - 1 - order[p], 1), :] = jnp.broadcast_to(
            value, (message.shape[0], 1, LANES)
        )

    row_sweep(held.score, range(held.total), rows, row_found, columns=columns)
    column_sweep(held.score, range(held.total), rows, row_pot, column_found)
    row[...] = as_row(row_pot[:, 0:1]) * (epsilon * LN2)


def last_kernel(got, small, row, row_out, column_out):
    values = got[...]
    top = jnp.max(values, axis=0, keepdims=True)
    total = top + jnp.log2(jnp.sum(jnp.exp2(values - top), axis=0, keepdims=True))
    column_out[...] = epsilon * small[1:2, :] - (epsilon * LN2) * total
    row_out[...] = row[...]


def lse(values):
    top = jnp.max(values, axis=0)
    return top + jnp.log(jnp.sum(jnp.exp(values - top[None]), axis=0))


def solution(mesh):
    blk, grp = mesh.shape["blk"], mesh.shape["grp"]
    chips = blk // 2
    everyone = ("chip", "core", "grp")

    def shards_square(source_embed, target_embed, target_init, source_logw, target_logw):
        rows, depth = source_embed.shape
        width = target_embed.shape[0]
        half = width // 2
        factor = inverse_eps * LOG2E / math.sqrt(depth)
        vmem, hbm = pl.BlockSpec(memory_space=pltpu.VMEM), pl.BlockSpec(memory_space=pltpu.HBM)
        params = pltpu.CompilerParams(vmem_limit_bytes=16 * 1024 * 1024)

        def values(*shape):
            return jax.ShapeDtypeStruct(shape, jnp.float32)

        def cost(targets, sweeps):
            return pl.CostEstimate(
                flops=2 * rows * targets * depth + 16 * sweeps * rows * blk * width,
                transcendentals=2 * sweeps * rows * blk * width,
                bytes_accessed=2 * (rows + targets) * depth,
            )

        def along(array, turn):
            return lax.ppermute(
                array, "blk", [(i ^ neighbour_step(i, turn), i) for i in range(blk)]
            )

        def to_sibling(array):
            return fetch(array, "blk", 1, blk)

        def exchange(message):
            order = [b * grp + g for g in reversed(range(grp)) for b in reversed(range(blk))]
            message = message.reshape(blk * grp, -1, width)
            return lax.all_to_all(message, ("blk", "grp"), 0, 0, axis_index_groups=[order])

        def block_of(size):
            return jax.ShapeDtypeStruct((size, depth), target_embed.dtype)

        def in_hbm(*arrays):
            return [pltpu.with_memory_space_constraint(each, pltpu.HBM) for each in arrays]

        first, second, whole, small, first_plain, second_plain = pl.pallas_call(
            head_kernel,
            out_shape=(
                block_of(half + SPARE),
                block_of(half + SPARE),
                block_of(width + SPARE),
                values(2, width),
                block_of(half),
                block_of(half),
            ),
            in_specs=[hbm] * 3,
            out_specs=(vmem,) * 6,
            scratch_shapes=[
                pltpu.VMEM((1, width), jnp.float32),
                pltpu.VMEM((1, width), jnp.float32),
                pltpu.SemaphoreType.DMA((3,)),
            ],
            compiler_params=params,
        )(*in_hbm(target_embed, target_init.reshape(1, width), target_logw.reshape(1, width)))
        a_first = along(first, 0)
        b_second = along(second, 1)
        a_second = along(second_plain, 0)
        b_first = along(first_plain, 1)
        far_a = along(a_first, 1)
        far_b = along(b_second[:half], 0)
        source, logw, passed = pl.pallas_call(
            source_kernel,
            out_shape=(
                jax.ShapeDtypeStruct((rows, depth), source_embed.dtype),
                values(rows, LANES),
                block_of(width + SPARE),
            ),
            in_specs=[hbm] * 2 + [vmem],
            out_specs=(vmem,) * 3,
            scratch_shapes=[pltpu.VMEM((1, rows), jnp.float32), pltpu.SemaphoreType.DMA((2,))],
            compiler_params=params,
        )(*in_hbm(source_embed, source_logw.reshape(1, rows)), whole)
        near = (a_first, a_second, b_first, b_second)
        sibling = pl.pallas_call(
            sibling_kernel,
            out_shape=block_of(3 * (width + SPARE)),
            in_specs=[vmem] * 5,
            out_specs=vmem,
            compiler_params=params,
            cost_estimate=cost(0, 0),
        )(passed, *near)
        sibling = to_sibling(sibling)

        def passed_on(message, weight):
            return pl.pallas_call(
                pass_kernel,
                out_shape=jax.ShapeDtypeStruct(message.shape, message.dtype),
                in_specs=[vmem],
                out_specs=vmem,
                compiler_params=params,
                cost_estimate=cost(weight * width, 0),
            )(message)

        sibling_a = to_sibling(passed_on(far_a, 0))
        sibling_b = to_sibling(passed_on(far_b, 50))

        def table():
            return values(2, SUBLANES, width)

        scores_near, table_near, found = pl.pallas_call(
            functools.partial(near_kernel, factor),
            out_shape=(values(rows, 6 * width), table(), values(rows, LANES)),
            in_specs=[vmem] * 7,
            out_specs=(vmem,) * 3,
            scratch_shapes=[pltpu.VMEM((6 * width, depth), target_embed.dtype)],
            compiler_params=params,
            cost_estimate=cost(0, 0),
        )(source, whole, *near, sibling)
        scores_far, table_far = pl.pallas_call(
            functools.partial(far_kernel, factor),
            out_shape=(values(rows, 2 * width), table()),
            in_specs=[vmem] * 6,
            out_specs=(vmem, vmem),
            scratch_shapes=[pltpu.VMEM((2 * width, depth), target_embed.dtype)],
            compiler_params=params,
            cost_estimate=cost(0, 0),
        )(source, far_a, far_b, sibling_a, sibling_b, scores_near)
        scores = (scores_far, table_far)
        row_scratch = pltpu.VMEM((rows, LANES), jnp.float32)
        block_scratch = pltpu.VMEM((blk, width), jnp.float32)
        message = pl.pallas_call(
            first_kernel,
            out_shape=values(blk * grp, blk, width),
            in_specs=[vmem] * 6,
            out_specs=vmem,
            scratch_shapes=[row_scratch, block_scratch],
            compiler_params=params,
            cost_estimate=cost(0, 1),
        )(scores_near, table_near, found, *scores, logw)
        got = exchange(message)
        row, message = pl.pallas_call(
            second_kernel,
            out_shape=(values(1, rows), values(grp, blk, width)),
            in_specs=[vmem] * 6,
            out_specs=(vmem, vmem),
            scratch_shapes=[row_scratch, block_scratch],
            compiler_params=params,
            cost_estimate=cost(0, 1),
        )(scores_near, table_near, *scores, got, logw)
        got = exchange(message).reshape(blk * grp, width)
        row_pot, column_pot = pl.pallas_call(
            last_kernel,
            out_shape=(values(1, rows), values(1, width)),
            in_specs=[vmem] * 3,
            out_specs=(vmem, vmem),
            compiler_params=params,
        )(got, small, row)
        return row_pot.reshape(rows), column_pot.reshape(width)

    def shards_any(source_embed, target_embed, target_init, source_logw, target_logw):
        width, depth = target_embed.shape
        factor = -1.0 / math.sqrt(depth)
        me = lax.axis_index("chip") * 2 + lax.axis_index("core")

        def swap_order(values):
            parts = values.reshape(blk, width)
            step = 1
            while step < blk:
                pairs = parts.reshape(blk // (2 * step), 2, step, width)
                pairs = jnp.where(me & step, pairs[:, ::-1], pairs)
                parts = pairs.reshape(blk, width)
                step *= 2
            return parts

        small = jnp.stack([target_init, target_logw])
        targets, smalls = gather_any(target_embed, small, chips)
        cost = (
            lax.dot_general(
                source_embed, targets, (((1,), (1,)), ((), ())), preferred_element_type=jnp.float32
            )
            * factor
        )
        column_pot, logw_all = smalls[:, 0].reshape(-1), smalls[:, 1].reshape(-1)
        for iteration in range(ITERS):
            scores = (column_pot[None, :] - cost) * inverse_eps
            row_top = jnp.max(scores, axis=1)
            row_sum = jnp.sum(jnp.exp(scores - row_top[:, None]), axis=1)
            row_pot = epsilon * source_logw - epsilon * (row_top + jnp.log(row_sum))
            part = swap_order(lse((row_pot[:, None] - cost) * inverse_eps))
            if iteration < ITERS - 1:
                copies = jnp.broadcast_to(part[None], (blk * grp, blk, width))
                got = lax.all_to_all(copies, everyone, 0, 0)
                total = swap_order(lse(got)).reshape(-1)
                column_pot = epsilon * logw_all - epsilon * total
            else:
                copies = jnp.broadcast_to(part[:, None], (blk, grp, width)).reshape(blk * grp, width)
                got = lax.all_to_all(copies, everyone, 0, 0)
                own_column = epsilon * target_logw - epsilon * lse(got)
        return row_pot, own_column

    if chips == 4:
        shards = shards_square
        rows_spec, blk_spec = P(("blk", "grp")), P("blk")
    else:
        shards = shards_any
        rows_spec, blk_spec = P(everyone), P(("chip", "core"))
        mesh = Mesh(mesh.devices.reshape(chips, 2, grp), everyone)
    in_specs = (rows_spec, blk_spec, blk_spec, rows_spec, blk_spec)
    out_specs = (rows_spec, blk_spec)
    return jax.shard_map(shards, mesh=mesh, in_specs=in_specs, out_specs=out_specs, check_vma=False)
```

```python
import functools
import math

import jax
import jax.numpy as jnp
from jax import lax
from jax.experimental import pallas as pl
from jax.experimental.pallas import tpu as pltpu
from jax.sharding import Mesh, PartitionSpec as P

ITERS = 2
epsilon = 0.1
inverse_eps = 10.0
LOG2E = math.log2(math.e)
LN2 = math.log(2.0)
LANES = 128
SPARE = 8
SUBLANES = 8


def fetch(array, axis, step, size):
    return lax.ppermute(array, axis, [(i ^ step, i) for i in range(size)])


def doubled(held, step, chips):
    return jnp.concatenate([held, fetch(held, "chip", step, chips)])


def gather_any(array, small, chips):
    pair = jnp.stack([array, fetch(array, "core", 1, 2)])[None]
    smalls = jnp.stack([small, fetch(small, "core", 1, 2)])[None]
    step = 1
    while step < chips:
        pair = doubled(pair, step, chips)
        smalls = doubled(smalls, step, chips)
        step *= 2
    return pair.reshape(-1, array.shape[1]), smalls.reshape(-1, *small.shape)


def as_column(row):
    size = row.shape[1]
    here = lax.broadcasted_iota(jnp.int32, (LANES, LANES), 0)
    there = lax.broadcasted_iota(jnp.int32, (LANES, LANES), 1)
    parts = []
    for start in range(0, size, LANES):
        wide = jnp.broadcast_to(row[:, start : start + LANES], (LANES, LANES))
        parts.append(jnp.sum(jnp.where(here == there, wide, 0.0), axis=1, keepdims=True))
    return jnp.concatenate(parts, axis=0)


def as_row(column):
    size = column.shape[0]
    here = lax.broadcasted_iota(jnp.int32, (LANES, LANES), 0)
    there = lax.broadcasted_iota(jnp.int32, (LANES, LANES), 1)
    parts = []
    for start in range(0, size, LANES):
        wide = jnp.broadcast_to(column[start : start + LANES], (LANES, LANES))
        parts.append(jnp.sum(jnp.where(here == there, wide, 0.0), axis=0, keepdims=True))
    return jnp.concatenate(parts, axis=1)


CHUNK = 64


def chunks_of(rows):
    return [pl.ds(start, CHUNK) for start in range(0, rows, CHUNK)]


def row_sweep(score_of, blocks, rows, found_of, columns=None, others=None):
    tops = []
    for at in chunks_of(rows):
        top = None if others is None else others[at, :]
        for p in blocks:
            score = score_of(at, p)
            score = score if columns is None else score + columns[p]
            top = score if top is None else jnp.maximum(top, score)
        tops.append(jnp.max(top, axis=1, keepdims=True))
    for at, top in zip(chunks_of(rows), tops):
        total = None
        for p in blocks:
            shift = -top if columns is None else columns[p] - top
            term = jnp.exp2(score_of(at, p) + shift)
            total = term if total is None else total + term
        total = jnp.sum(total, axis=1, keepdims=True)
        if others is not None:
            total = total + jnp.exp2(others[at, :] - top)
        found_of(at, top + jnp.log2(total))


def column_sweep(score_of, blocks, rows, row_pot, found_of):
    folds = (CHUNK // SUBLANES, SUBLANES, LANES)
    found = [[] for _ in blocks]
    for at in chunks_of(rows):
        addend = row_pot[at, :]
        for p in blocks:
            score = (score_of(at, p) + addend).reshape(folds)
            top = jnp.max(score, axis=0)
            found[p].append((top, jnp.sum(jnp.exp2(score - top[None]), axis=0)))
    for p in blocks:
        top = functools.reduce(jnp.maximum, [each for each, _ in found[p]])
        top = jnp.max(top, axis=0, keepdims=True)
        total = sum(each * jnp.exp2(at_top - top) for at_top, each in found[p])
        found_of(p, top + jnp.log2(jnp.sum(total, axis=0, keepdims=True)))


def products(source, targets, factor, smalls, scaled, table):
    for p, small in enumerate(smalls):
        table[0, p : p + 1, :] = small[1:2] * LOG2E
        table[1, p : p + 1, :] = small[0:1] * (inverse_eps * LOG2E)
    for p in range(0, len(smalls), 2):
        lanes = slice(p * LANES, (p + 2) * LANES)
        product = lax.dot_general(
            source[...], targets[lanes, :], (((1,), (1,)), ((), ())),
            preferred_element_type=jnp.float32,
        )
        shift = jnp.concatenate([table[1, p : p + 1, :], table[1, p + 1 : p + 2, :]], axis=1)
        scaled[:, lanes] = product * factor + shift


def head_kernel(
    own, init, target_logw, first, second, whole, small, first_plain, second_plain, init_row,
    logw_row, sems,
):
    rows, half = own.shape[0], first_plain.shape[0]
    copies = [
        pltpu.make_async_copy(own, whole.at[0:rows], sems.at[0]),
        pltpu.make_async_copy(init, init_row, sems.at[1]),
        pltpu.make_async_copy(target_logw, logw_row, sems.at[2]),
    ]
    for copy in copies:
        copy.start()
    for copy in copies:
        copy.wait()
    for out in (first, first_plain):
        out[0:half, :] = whole[0:half, :]
    for out in (second, second_plain):
        out[0:half, :] = whole[half:rows, :]
    small[0:1, :] = init_row[...]
    small[1:2, :] = logw_row[...]
    filler = jnp.zeros((SPARE - 2, LANES), jnp.float32)
    rest = jnp.concatenate([init_row[...], logw_row[...], filler], axis=0)
    for k in range(whole.shape[1] // LANES):
        lanes = slice(k * LANES, (k + 1) * LANES)
        part = (rest if k < 3 else jnp.zeros_like(rest)).astype(whole.dtype)
        first[half:, lanes] = part
        second[half:, lanes] = part
        whole[rows:, lanes] = part
        rest = rest - part.astype(jnp.float32)


def source_kernel(source, logw, whole, held, row_logw, passed, rows_row, sems):
    copies = [
        pltpu.make_async_copy(source, held, sems.at[0]),
        pltpu.make_async_copy(logw, rows_row, sems.at[1]),
    ]
    for copy in copies:
        copy.start()
    passed[...] = whole[...]
    for copy in copies:
        copy.wait()
    row_logw[...] = jnp.broadcast_to(as_column(rows_row[...] * LOG2E), row_logw.shape)


def sibling_kernel(whole, a_first, a_second, b_first, b_second, out):
    half = a_second.shape[0]
    block = 2 * half + SPARE
    out[0:block, :] = whole[...]
    out[block : block + half, :] = a_first[0:half, :]
    out[block + half : block + 2 * half, :] = a_second[...]
    out[block + 2 * half : 2 * block, :] = a_first[half:, :]
    out[2 * block : 2 * block + half, :] = b_first[...]
    out[2 * block + half : 3 * block, :] = b_second[...]


def unpack(message, end=None):
    end = message.shape[0] if end is None else end
    parts = [
        message[end - SPARE : end, k * LANES : (k + 1) * LANES].astype(jnp.float32)[0:2]
        for k in range(3)
    ]
    return (parts[0] + parts[1]) + parts[2]


def near_kernel(
    factor, source, whole, a_first, a_second, b_first, b_second, sibling, scaled, table, found,
    targets,
):
    half = a_second.shape[0]
    width = 2 * half
    block = width + SPARE
    targets[0:width, :] = whole[0:width, :]
    for k, piece in enumerate((a_first, a_second)):
        targets[2 * width + k * half : 2 * width + (k + 1) * half, :] = piece[0:half, :]
    for k, piece in enumerate((b_first, b_second)):
        targets[4 * width + k * half : 4 * width + (k + 1) * half, :] = piece[0:half, :]
    for k in range(3):
        start = (2 * k + 1) * width
        targets[start : start + width, :] = sibling[k * block : k * block + width, :]
    smalls = []
    for k, message in enumerate((whole, a_first, b_second)):
        smalls += [unpack(message), unpack(sibling, (k + 1) * block)]
    products(source, targets, factor, smalls, scaled, table)

    def score_of(at, p):
        return scaled[at, p * LANES : (p + 1) * LANES]

    def found_of(at, value):
        found[at, :] = jnp.broadcast_to(value, (CHUNK, LANES))

    row_sweep(score_of, range(len(smalls)), scaled.shape[0], found_of)


def pass_kernel(message, out):
    out[...] = message[...]


def far_kernel(
    factor, source, far_a, far_b, sibling_a, sibling_b, near, scaled, table, targets
):
    half = targets.shape[0] // 4
    for k, piece in enumerate((far_a, far_b, sibling_a, sibling_b)):
        targets[k * half : (k + 1) * half, :] = piece[0:half, :]
    smalls = [unpack(far_a), unpack(sibling_a)]
    products(source, targets, factor, smalls, scaled, table)


def neighbour_step(me, turn):
    step = 2 + 2 * (me % 2)
    return step if turn == 0 else 6 - step


def positions(me):
    sibling = me ^ 1
    own = [me, me ^ neighbour_step(me, 0), me ^ neighbour_step(me, 1), me ^ 6]
    other = [
        sibling,
        sibling ^ neighbour_step(sibling, 0),
        sibling ^ neighbour_step(sibling, 1),
        sibling ^ 6,
    ]
    return [block for pair in zip(own, other) for block in pair]


class Held:

    def __init__(self, near, near_table, far, far_table):
        self.count = near.shape[1] // LANES
        self.total = self.count + far.shape[1] // LANES
        self.near, self.near_table, self.far, self.far_table = near, near_table, far, far_table

    def score(self, at, p):
        part, p = (self.near, p) if p < self.count else (self.far, p - self.count)
        return part[at, p * LANES : (p + 1) * LANES]

    def row(self, kind, p):
        table, p = (self.near_table, p) if p < self.count else (self.far_table, p - self.count)
        return table[kind, p : p + 1, :]


def first_kernel(near, near_table, found, far, far_table, logw, message, row_pot, ordered):
    order = positions(lax.axis_index("blk"))
    held = Held(near, near_table, far, far_table)
    rows = near.shape[0]

    def row_found(at, value):
        row_pot[at, :] = logw[at, :] - value

    def column_found(p, value):
        ordered[pl.ds(order[p], 1), :] = value - held.row(1, p)

    row_sweep(held.score, range(held.count, held.total), rows, row_found, others=found)
    column_sweep(held.score, range(held.total), rows, row_pot, column_found)
    message[...] = jnp.broadcast_to(ordered[...][None], message.shape)


def second_kernel(
    copies, near, near_table, far, far_table, got, logw, row, message, row_pot, ordered
):
    order = positions(lax.axis_index("blk"))
    held = Held(near, near_table, far, far_table)
    rows = near.shape[0]
    values = got[...]
    top = jnp.max(values, axis=0)
    ordered[...] = top + jnp.log2(jnp.sum(jnp.exp2(values - top[None]), axis=0))
    columns = []
    for p in range(held.total):
        columns.append(held.row(0, p) - ordered[pl.ds(order[p], 1), :] - held.row(1, p))

    def row_found(at, value):
        row_pot[at, :] = logw[at, :] - value

    def column_found(p, value):
        place = order[p] ^ (order[p] >> 1) ^ (order[p] >> 2)
        message[pl.ds(place * copies, copies), :] = jnp.broadcast_to(
            value - held.row(1, p), (copies, LANES)
        )

    row_sweep(held.score, range(held.total), rows, row_found, columns=columns)
    column_sweep(held.score, range(held.total), rows, row_pot, column_found)
    row[...] = as_row(row_pot[:, 0:1]) * (epsilon * LN2)


def last_kernel(got, small, row, row_out, column_out):
    values = got[...]
    top = jnp.max(values, axis=0, keepdims=True)
    total = top + jnp.log2(jnp.sum(jnp.exp2(values - top), axis=0, keepdims=True))
    column_out[...] = epsilon * small[1:2, :] - (epsilon * LN2) * total
    row_out[...] = row[...]


def lse(values):
    top = jnp.max(values, axis=0)
    return top + jnp.log(jnp.sum(jnp.exp(values - top[None]), axis=0))


def solution(mesh):
    blk, grp = mesh.shape["blk"], mesh.shape["grp"]
    chips = blk // 2
    everyone = ("chip", "core", "grp")

    def shards_square(source_embed, target_embed, target_init, source_logw, target_logw):
        rows, depth = source_embed.shape
        width = target_embed.shape[0]
        half = width // 2
        factor = inverse_eps * LOG2E / math.sqrt(depth)
        vmem, hbm = pl.BlockSpec(memory_space=pltpu.VMEM), pl.BlockSpec(memory_space=pltpu.HBM)
        params = pltpu.CompilerParams(vmem_limit_bytes=16 * 1024 * 1024)

        def values(*shape):
            return jax.ShapeDtypeStruct(shape, jnp.float32)

        def cost(targets, sweeps):
            return pl.CostEstimate(
                flops=2 * rows * targets * depth + 16 * sweeps * rows * blk * width,
                transcendentals=2 * sweeps * rows * blk * width,
                bytes_accessed=2 * (rows + targets) * depth,
            )

        def along(array, turn):
            return lax.ppermute(
                array, "blk", [(i ^ neighbour_step(i, turn), i) for i in range(blk)]
            )

        def to_sibling(array):
            return fetch(array, "blk", 1, blk)

        def exchange(message):
            order = []
            for k in range(blk):
                column = [(k ^ (k >> 1)) * grp + g for g in range(grp)]
                order += column if k % 2 == 0 else column[::-1]
            message = message.reshape(blk * grp, -1, width)
            return lax.all_to_all(message, ("blk", "grp"), 0, 0, axis_index_groups=[order])

        def block_of(size):
            return jax.ShapeDtypeStruct((size, depth), target_embed.dtype)

        def in_hbm(*arrays):
            return [pltpu.with_memory_space_constraint(each, pltpu.HBM) for each in arrays]

        first, second, whole, small, first_plain, second_plain = pl.pallas_call(
            head_kernel,
            out_shape=(
                block_of(half + SPARE),
                block_of(half + SPARE),
                block_of(width + SPARE),
                values(2, width),
                block_of(half),
                block_of(half),
            ),
            in_specs=[hbm] * 3,
            out_specs=(vmem,) * 6,
            scratch_shapes=[
                pltpu.VMEM((1, width), jnp.float32),
                pltpu.VMEM((1, width), jnp.float32),
                pltpu.SemaphoreType.DMA((3,)),
            ],
            compiler_params=params,
        )(*in_hbm(target_embed, target_init.reshape(1, width), target_logw.reshape(1, width)))
        a_first = along(first, 0)
        b_second = along(second, 1)
        a_second = along(second_plain, 0)
        b_first = along(first_plain, 1)
        far_a = along(a_first, 1)
        far_b = along(b_second[:half], 0)
        source, logw, passed = pl.pallas_call(
            source_kernel,
            out_shape=(
                jax.ShapeDtypeStruct((rows, depth), source_embed.dtype),
                values(rows, LANES),
                block_of(width + SPARE),
            ),
            in_specs=[hbm] * 2 + [vmem],
            out_specs=(vmem,) * 3,
            scratch_shapes=[pltpu.VMEM((1, rows), jnp.float32), pltpu.SemaphoreType.DMA((2,))],
            compiler_params=params,
        )(*in_hbm(source_embed, source_logw.reshape(1, rows)), whole)
        near = (a_first, a_second, b_first, b_second)
        sibling = pl.pallas_call(
            sibling_kernel,
            out_shape=block_of(3 * (width + SPARE)),
            in_specs=[vmem] * 5,
            out_specs=vmem,
            compiler_params=params,
            cost_estimate=cost(0, 0),
        )(passed, *near)
        sibling = to_sibling(sibling)

        def passed_on(message, weight):
            return pl.pallas_call(
                pass_kernel,
                out_shape=jax.ShapeDtypeStruct(message.shape, message.dtype),
                in_specs=[vmem],
                out_specs=vmem,
                compiler_params=params,
                cost_estimate=cost(weight * width, 0),
            )(message)

        sibling_a = to_sibling(passed_on(far_a, 0))
        sibling_b = to_sibling(passed_on(far_b, 50))

        def table():
            return values(2, SUBLANES, width)

        scores_near, table_near, found = pl.pallas_call(
            functools.partial(near_kernel, factor),
            out_shape=(values(rows, 6 * width), table(), values(rows, LANES)),
            in_specs=[vmem] * 7,
            out_specs=(vmem,) * 3,
            scratch_shapes=[pltpu.VMEM((6 * width, depth), target_embed.dtype)],
            compiler_params=params,
            cost_estimate=cost(0, 0),
        )(source, whole, *near, sibling)
        scores_far, table_far = pl.pallas_call(
            functools.partial(far_kernel, factor),
            out_shape=(values(rows, 2 * width), table()),
            in_specs=[vmem] * 6,
            out_specs=(vmem, vmem),
            scratch_shapes=[pltpu.VMEM((2 * width, depth), target_embed.dtype)],
            compiler_params=params,
            cost_estimate=cost(0, 0),
        )(source, far_a, far_b, sibling_a, sibling_b, scores_near)
        scores = (scores_far, table_far)
        row_scratch = pltpu.VMEM((rows, LANES), jnp.float32)
        block_scratch = pltpu.VMEM((blk, width), jnp.float32)
        message = pl.pallas_call(
            first_kernel,
            out_shape=values(blk * grp, blk, width),
            in_specs=[vmem] * 6,
            out_specs=vmem,
            scratch_shapes=[row_scratch, block_scratch],
            compiler_params=params,
            cost_estimate=cost(0, 1),
        )(scores_near, table_near, found, *scores, logw)
        got = exchange(message)
        row, message = pl.pallas_call(
            functools.partial(second_kernel, grp),
            out_shape=(values(1, rows), values(blk * grp, width)),
            in_specs=[vmem] * 6,
            out_specs=(vmem, vmem),
            scratch_shapes=[row_scratch, block_scratch],
            compiler_params=params,
            cost_estimate=cost(0, 1),
        )(scores_near, table_near, *scores, got, logw)
        got = exchange(message).reshape(blk * grp, width)
        row_pot, column_pot = pl.pallas_call(
            last_kernel,
            out_shape=(values(1, rows), values(1, width)),
            in_specs=[vmem] * 3,
            out_specs=(vmem, vmem),
            compiler_params=params,
        )(got, small, row)
        return row_pot.reshape(rows), column_pot.reshape(width)

    def shards_any(source_embed, target_embed, target_init, source_logw, target_logw):
        width, depth = target_embed.shape
        factor = -1.0 / math.sqrt(depth)
        me = lax.axis_index("chip") * 2 + lax.axis_index("core")

        def swap_order(values):
            parts = values.reshape(blk, width)
            step = 1
            while step < blk:
                pairs = parts.reshape(blk // (2 * step), 2, step, width)
                pairs = jnp.where(me & step, pairs[:, ::-1], pairs)
                parts = pairs.reshape(blk, width)
                step *= 2
            return parts

        small = jnp.stack([target_init, target_logw])
        targets, smalls = gather_any(target_embed, small, chips)
        cost = (
            lax.dot_general(
                source_embed, targets, (((1,), (1,)), ((), ())), preferred_element_type=jnp.float32
            )
            * factor
        )
        column_pot, logw_all = smalls[:, 0].reshape(-1), smalls[:, 1].reshape(-1)
        for iteration in range(ITERS):
            scores = (column_pot[None, :] - cost) * inverse_eps
            row_top = jnp.max(scores, axis=1)
            row_sum = jnp.sum(jnp.exp(scores - row_top[:, None]), axis=1)
            row_pot = epsilon * source_logw - epsilon * (row_top + jnp.log(row_sum))
            part = swap_order(lse((row_pot[:, None] - cost) * inverse_eps))
            if iteration < ITERS - 1:
                copies = jnp.broadcast_to(part[None], (blk * grp, blk, width))
                got = lax.all_to_all(copies, everyone, 0, 0)
                total = swap_order(lse(got)).reshape(-1)
                column_pot = epsilon * logw_all - epsilon * total
            else:
                copies = jnp.broadcast_to(part[:, None], (blk, grp, width)).reshape(blk * grp, width)
                got = lax.all_to_all(copies, everyone, 0, 0)
                own_column = epsilon * target_logw - epsilon * lse(got)
        return row_pot, own_column

    if chips == 4:
        shards = shards_square
        rows_spec, blk_spec = P(("blk", "grp")), P("blk")
    else:
        shards = shards_any
        rows_spec, blk_spec = P(everyone), P(("chip", "core"))
        mesh = Mesh(mesh.devices.reshape(chips, 2, grp), everyone)
    in_specs = (rows_spec, blk_spec, blk_spec, rows_spec, blk_spec)
    out_specs = (rows_spec, blk_spec)
    return jax.shard_map(shards, mesh=mesh, in_specs=in_specs, out_specs=out_specs, check_vma=False)
```

```python
import functools
import math

import jax
import jax.numpy as jnp
from jax import lax
from jax.experimental import pallas as pl
from jax.experimental.pallas import tpu as pltpu
from jax.sharding import Mesh, PartitionSpec as P

ITERS = 2
epsilon = 0.1
inverse_eps = 10.0
LOG2E = math.log2(math.e)
LN2 = math.log(2.0)
LANES = 128
SPARE = 8
SUBLANES = 8


def fetch(array, axis, step, size):
    return lax.ppermute(array, axis, [(i ^ step, i) for i in range(size)])


def doubled(held, step, chips):
    return jnp.concatenate([held, fetch(held, "chip", step, chips)])


def gather_any(array, small, chips):
    pair = jnp.stack([array, fetch(array, "core", 1, 2)])[None]
    smalls = jnp.stack([small, fetch(small, "core", 1, 2)])[None]
    step = 1
    while step < chips:
        pair = doubled(pair, step, chips)
        smalls = doubled(smalls, step, chips)
        step *= 2
    return pair.reshape(-1, array.shape[1]), smalls.reshape(-1, *small.shape)


def as_column(row):
    size = row.shape[1]
    here = lax.broadcasted_iota(jnp.int32, (LANES, LANES), 0)
    there = lax.broadcasted_iota(jnp.int32, (LANES, LANES), 1)
    parts = []
    for start in range(0, size, LANES):
        wide = jnp.broadcast_to(row[:, start : start + LANES], (LANES, LANES))
        parts.append(jnp.sum(jnp.where(here == there, wide, 0.0), axis=1, keepdims=True))
    return jnp.concatenate(parts, axis=0)


def as_row(column):
    size = column.shape[0]
    here = lax.broadcasted_iota(jnp.int32, (LANES, LANES), 0)
    there = lax.broadcasted_iota(jnp.int32, (LANES, LANES), 1)
    parts = []
    for start in range(0, size, LANES):
        wide = jnp.broadcast_to(column[start : start + LANES], (LANES, LANES))
        parts.append(jnp.sum(jnp.where(here == there, wide, 0.0), axis=0, keepdims=True))
    return jnp.concatenate(parts, axis=1)


CHUNK = 64


def chunks_of(rows):
    return [pl.ds(start, CHUNK) for start in range(0, rows, CHUNK)]


def row_sweep(score_of, blocks, rows, found_of, columns=None, others=None):
    tops = []
    for at in chunks_of(rows):
        top = None if others is None else others[at, :]
        for p in blocks:
            score = score_of(at, p)
            score = score if columns is None else score + columns[p]
            top = score if top is None else jnp.maximum(top, score)
        tops.append(jnp.max(top, axis=1, keepdims=True))
    for at, top in zip(chunks_of(rows), tops):
        total = None
        for p in blocks:
            shift = -top if columns is None else columns[p] - top
            term = jnp.exp2(score_of(at, p) + shift)
            total = term if total is None else total + term
        total = jnp.sum(total, axis=1, keepdims=True)
        if others is not None:
            total = total + jnp.exp2(others[at, :] - top)
        found_of(at, top + jnp.log2(total))


def column_sweep(score_of, blocks, rows, row_pot, found_of):
    folds = (CHUNK // SUBLANES, SUBLANES, LANES)
    found = [[] for _ in blocks]
    for at in chunks_of(rows):
        addend = row_pot[at, :]
        for p in blocks:
            score = (score_of(at, p) + addend).reshape(folds)
            top = jnp.max(score, axis=0)
            found[p].append((top, jnp.sum(jnp.exp2(score - top[None]), axis=0)))
    for p in blocks:
        top = functools.reduce(jnp.maximum, [each for each, _ in found[p]])
        top = jnp.max(top, axis=0, keepdims=True)
        total = sum(each * jnp.exp2(at_top - top) for at_top, each in found[p])
        found_of(p, top + jnp.log2(jnp.sum(total, axis=0, keepdims=True)))


def products(source, targets, factor, smalls, scaled, table):
    for p, small in enumerate(smalls):
        table[0, p : p + 1, :] = small[1:2] * LOG2E
        table[1, p : p + 1, :] = small[0:1] * (inverse_eps * LOG2E)
    for p in range(0, len(smalls), 2):
        end = min(p + 2, len(smalls))
        lanes = slice(p * LANES, end * LANES)
        product = lax.dot_general(
            source[...], targets[lanes, :], (((1,), (1,)), ((), ())),
            preferred_element_type=jnp.float32,
        )
        shift = jnp.concatenate([table[1, q : q + 1, :] for q in range(p, end)], axis=1)
        scaled[:, lanes] = product * factor + shift


def head_kernel(
    own, init, target_logw, first, second, whole, small, first_plain, second_plain, init_row,
    logw_row, sems,
):
    rows, half = own.shape[0], first_plain.shape[0]
    copies = [
        pltpu.make_async_copy(own, whole.at[0:rows], sems.at[0]),
        pltpu.make_async_copy(init, init_row, sems.at[1]),
        pltpu.make_async_copy(target_logw, logw_row, sems.at[2]),
    ]
    for copy in copies:
        copy.start()
    for copy in copies:
        copy.wait()
    for out in (first, first_plain):
        out[0:half, :] = whole[0:half, :]
    for out in (second, second_plain):
        out[0:half, :] = whole[half:rows, :]
    small[0:1, :] = init_row[...]
    small[1:2, :] = logw_row[...]
    filler = jnp.zeros((SPARE - 2, LANES), jnp.float32)
    rest = jnp.concatenate([init_row[...], logw_row[...], filler], axis=0)
    for k in range(whole.shape[1] // LANES):
        lanes = slice(k * LANES, (k + 1) * LANES)
        part = (rest if k < 3 else jnp.zeros_like(rest)).astype(whole.dtype)
        first[half:, lanes] = part
        second[half:, lanes] = part
        whole[rows:, lanes] = part
        rest = rest - part.astype(jnp.float32)


def source_kernel(source, logw, whole, held, row_logw, passed, rows_row, sems):
    copies = [
        pltpu.make_async_copy(source, held, sems.at[0]),
        pltpu.make_async_copy(logw, rows_row, sems.at[1]),
    ]
    for copy in copies:
        copy.start()
    passed[...] = whole[...]
    for copy in copies:
        copy.wait()
    row_logw[...] = jnp.broadcast_to(as_column(rows_row[...] * LOG2E), row_logw.shape)


def sibling_kernel(whole, a_first, a_second, b_first, b_second, out):
    half = a_second.shape[0]
    block = 2 * half + SPARE
    out[0:block, :] = whole[...]
    out[block : block + half, :] = a_first[0:half, :]
    out[block + half : block + 2 * half, :] = a_second[...]
    out[block + 2 * half : 2 * block, :] = a_first[half:, :]
    out[2 * block : 2 * block + half, :] = b_first[...]
    out[2 * block + half : 3 * block, :] = b_second[...]


def unpack(message, end=None):
    end = message.shape[0] if end is None else end
    parts = [
        message[end - SPARE : end, k * LANES : (k + 1) * LANES].astype(jnp.float32)[0:2]
        for k in range(3)
    ]
    return (parts[0] + parts[1]) + parts[2]


def own_kernel(
    factor, source, whole, a_first, a_second, b_first, b_second, scaled, table, targets
):
    half = a_second.shape[0]
    pieces = (whole, whole, a_first, a_second, b_first, b_second)
    targets[0 : 2 * half, :] = whole[0 : 2 * half, :]
    for k in range(2, 6):
        targets[k * half : (k + 1) * half, :] = pieces[k][0:half, :]
    smalls = [unpack(whole), unpack(a_first), unpack(b_second)]
    products(source, targets, factor, smalls, scaled, table)


def sibling_scores_kernel(factor, source, sibling, own, scaled, table, found, targets):
    width = targets.shape[0] // 3
    block = width + SPARE
    smalls = []
    for k in range(3):
        targets[k * width : (k + 1) * width, :] = sibling[k * block : k * block + width, :]
        smalls.append(unpack(sibling, (k + 1) * block))
    products(source, targets, factor, smalls, scaled, table)

    def score_of(at, p):
        part = (own, scaled)[p % 2]
        return part[at, p // 2 * LANES : (p // 2 + 1) * LANES]

    def found_of(at, value):
        found[at, :] = jnp.broadcast_to(value, (CHUNK, LANES))

    row_sweep(score_of, range(6), scaled.shape[0], found_of)


def pass_kernel(message, tie, out):
    out[...] = message[...]


def far_kernel(
    factor, source, far_a, far_b, sibling_a, sibling_b, near, scaled, table, targets
):
    half = targets.shape[0] // 4
    for k, piece in enumerate((far_a, far_b, sibling_a, sibling_b)):
        targets[k * half : (k + 1) * half, :] = piece[0:half, :]
    smalls = [unpack(far_a), unpack(sibling_a)]
    products(source, targets, factor, smalls, scaled, table)


def neighbour_step(me, turn):
    step = 2 + 2 * (me % 2)
    return step if turn == 0 else 6 - step


def positions(me):
    sibling = me ^ 1
    own = [me, me ^ neighbour_step(me, 0), me ^ neighbour_step(me, 1), me ^ 6]
    other = [
        sibling,
        sibling ^ neighbour_step(sibling, 0),
        sibling ^ neighbour_step(sibling, 1),
        sibling ^ 6,
    ]
    return [block for pair in zip(own, other) for block in pair]


class Held:

    def __init__(self, own, own_table, sibling, sibling_table, far, far_table):
        self.near = own.shape[1] // LANES * 2
        self.total = self.near + far.shape[1] // LANES
        self.scores, self.tables = (own, sibling, far), (own_table, sibling_table, far_table)

    def place(self, p):
        return (p % 2, p // 2) if p < self.near else (2, p - self.near)

    def score(self, at, p):
        part, k = self.place(p)
        return self.scores[part][at, k * LANES : (k + 1) * LANES]

    def row(self, kind, p):
        part, k = self.place(p)
        return self.tables[part][kind, k : k + 1, :]


def first_kernel(
    own, own_table, sibling, sibling_table, far, far_table, found, logw, message, row_pot, ordered
):
    order = positions(lax.axis_index("blk"))
    held = Held(own, own_table, sibling, sibling_table, far, far_table)
    rows = own.shape[0]

    def row_found(at, value):
        row_pot[at, :] = logw[at, :] - value

    def column_found(p, value):
        ordered[pl.ds(order[p], 1), :] = value - held.row(1, p)

    row_sweep(held.score, range(held.near, held.total), rows, row_found, others=found)
    column_sweep(held.score, range(held.total), rows, row_pot, column_found)
    message[...] = jnp.broadcast_to(ordered[...][None], message.shape)


def second_kernel(
    copies, own, own_table, sibling, sibling_table, far, far_table, got, logw, row, message,
    row_pot, ordered,
):
    order = positions(lax.axis_index("blk"))
    held = Held(own, own_table, sibling, sibling_table, far, far_table)
    rows = own.shape[0]
    values = got[...]
    top = jnp.max(values, axis=0)
    ordered[...] = top + jnp.log2(jnp.sum(jnp.exp2(values - top[None]), axis=0))
    columns = []
    for p in range(held.total):
        columns.append(held.row(0, p) - ordered[pl.ds(order[p], 1), :] - held.row(1, p))

    def row_found(at, value):
        row_pot[at, :] = logw[at, :] - value

    def column_found(p, value):
        at = pl.ds((held.total - 1 - order[p]) * copies, copies)
        message[at, :] = jnp.broadcast_to(value - held.row(1, p), (copies, LANES))

    row_sweep(held.score, range(held.total), rows, row_found, columns=columns)
    column_sweep(held.score, range(held.total), rows, row_pot, column_found)
    row[...] = as_row(row_pot[:, 0:1]) * (epsilon * LN2)


def last_kernel(got, small, row, row_out, column_out):
    values = got[...]
    top = jnp.max(values, axis=0, keepdims=True)
    total = top + jnp.log2(jnp.sum(jnp.exp2(values - top), axis=0, keepdims=True))
    column_out[...] = epsilon * small[1:2, :] - (epsilon * LN2) * total
    row_out[...] = row[...]


def lse(values):
    top = jnp.max(values, axis=0)
    return top + jnp.log(jnp.sum(jnp.exp(values - top[None]), axis=0))


def solution(mesh):
    blk, grp = mesh.shape["blk"], mesh.shape["grp"]
    chips = blk // 2
    everyone = ("chip", "core", "grp")

    def shards_square(source_embed, target_embed, target_init, source_logw, target_logw):
        rows, depth = source_embed.shape
        width = target_embed.shape[0]
        half = width // 2
        factor = inverse_eps * LOG2E / math.sqrt(depth)
        vmem, hbm = pl.BlockSpec(memory_space=pltpu.VMEM), pl.BlockSpec(memory_space=pltpu.HBM)
        params = pltpu.CompilerParams(vmem_limit_bytes=16 * 1024 * 1024)

        def values(*shape):
            return jax.ShapeDtypeStruct(shape, jnp.float32)

        def cost(targets, sweeps):
            return pl.CostEstimate(
                flops=2 * rows * targets * depth + 16 * sweeps * rows * blk * width,
                transcendentals=2 * sweeps * rows * blk * width,
                bytes_accessed=2 * (rows + targets) * depth,
            )

        def along(array, turn):
            return lax.ppermute(
                array, "blk", [(i ^ neighbour_step(i, turn), i) for i in range(blk)]
            )

        def to_sibling(array):
            return fetch(array, "blk", 1, blk)

        def exchange(message):
            order = list(range(blk * grp))[::-1]
            return lax.all_to_all(message, ("blk", "grp"), 0, 0, axis_index_groups=[order])

        def block_of(size):
            return jax.ShapeDtypeStruct((size, depth), target_embed.dtype)

        def in_hbm(*arrays):
            return [pltpu.with_memory_space_constraint(each, pltpu.HBM) for each in arrays]

        first, second, whole, small, first_plain, second_plain = pl.pallas_call(
            head_kernel,
            out_shape=(
                block_of(half + SPARE),
                block_of(half + SPARE),
                block_of(width + SPARE),
                values(2, width),
                block_of(half),
                block_of(half),
            ),
            in_specs=[hbm] * 3,
            out_specs=(vmem,) * 6,
            scratch_shapes=[
                pltpu.VMEM((1, width), jnp.float32),
                pltpu.VMEM((1, width), jnp.float32),
                pltpu.SemaphoreType.DMA((3,)),
            ],
            compiler_params=params,
        )(*in_hbm(target_embed, target_init.reshape(1, width), target_logw.reshape(1, width)))
        a_first = along(first, 0)
        b_second = along(second, 1)
        a_second = along(second_plain, 0)
        b_first = along(first_plain, 1)
        far_a = along(a_first, 1)
        far_b = along(b_second[:half], 0)
        source, logw, passed = pl.pallas_call(
            source_kernel,
            out_shape=(
                jax.ShapeDtypeStruct((rows, depth), source_embed.dtype),
                values(rows, LANES),
                block_of(width + SPARE),
            ),
            in_specs=[hbm] * 2 + [vmem],
            out_specs=(vmem,) * 3,
            scratch_shapes=[pltpu.VMEM((1, rows), jnp.float32), pltpu.SemaphoreType.DMA((2,))],
            compiler_params=params,
        )(*in_hbm(source_embed, source_logw.reshape(1, rows)), whole)
        near = (a_first, a_second, b_first, b_second)
        sibling = pl.pallas_call(
            sibling_kernel,
            out_shape=block_of(3 * (width + SPARE)),
            in_specs=[vmem] * 5,
            out_specs=vmem,
            compiler_params=params,
            cost_estimate=cost(0, 0),
        )(passed, *near)
        sibling = to_sibling(sibling)

        def table():
            return values(2, SUBLANES, width)

        def scores_of(kernel, blocks, pieces, extra=()):
            return pl.pallas_call(
                functools.partial(kernel, factor),
                out_shape=(values(rows, blocks * width), table(), *extra),
                in_specs=[vmem] * (1 + len(pieces)),
                out_specs=(vmem,) * (2 + len(extra)),
                scratch_shapes=[pltpu.VMEM((blocks * width, depth), target_embed.dtype)],
                compiler_params=params,
                cost_estimate=cost(0, 0),
            )(source, *pieces)

        own = scores_of(own_kernel, 3, (whole, *near))

        def passed_on(message, tie, weight):
            return pl.pallas_call(
                pass_kernel,
                out_shape=jax.ShapeDtypeStruct(message.shape, message.dtype),
                in_specs=[vmem] * 2,
                out_specs=vmem,
                compiler_params=params,
                cost_estimate=cost(weight * width, 0),
            )(message, tie)

        sibling_a = to_sibling(passed_on(far_a, own[1], 0))
        sibling_b = to_sibling(passed_on(far_b, own[1], 50))
        *other, found = scores_of(
            sibling_scores_kernel, 3, (sibling, own[0]), (values(rows, LANES),)
        )
        far = scores_of(far_kernel, 2, (far_a, far_b, sibling_a, sibling_b, other[0]))
        scores = (*own, *other, *far)
        row_scratch = pltpu.VMEM((rows, LANES), jnp.float32)
        block_scratch = pltpu.VMEM((blk, width), jnp.float32)
        message = pl.pallas_call(
            first_kernel,
            out_shape=values(blk * grp, blk, width),
            in_specs=[vmem] * 8,
            out_specs=vmem,
            scratch_shapes=[row_scratch, block_scratch],
            compiler_params=params,
            cost_estimate=cost(0, 1),
        )(*scores, found, logw)
        got = exchange(message)
        row, message = pl.pallas_call(
            functools.partial(second_kernel, grp),
            out_shape=(values(1, rows), values(blk * grp, width)),
            in_specs=[vmem] * 8,
            out_specs=(vmem, vmem),
            scratch_shapes=[row_scratch, block_scratch],
            compiler_params=params,
            cost_estimate=cost(0, 1),
        )(*scores, got, logw)
        got = exchange(message)
        row_pot, column_pot = pl.pallas_call(
            last_kernel,
            out_shape=(values(1, rows), values(1, width)),
            in_specs=[vmem] * 3,
            out_specs=(vmem, vmem),
            compiler_params=params,
        )(got, small, row)
        return row_pot.reshape(rows), column_pot.reshape(width)

    def shards_any(source_embed, target_embed, target_init, source_logw, target_logw):
        width, depth = target_embed.shape
        factor = -1.0 / math.sqrt(depth)
        me = lax.axis_index("chip") * 2 + lax.axis_index("core")

        def swap_order(values):
            parts = values.reshape(blk, width)
            step = 1
            while step < blk:
                pairs = parts.reshape(blk // (2 * step), 2, step, width)
                pairs = jnp.where(me & step, pairs[:, ::-1], pairs)
                parts = pairs.reshape(blk, width)
                step *= 2
            return parts

        small = jnp.stack([target_init, target_logw])
        targets, smalls = gather_any(target_embed, small, chips)
        cost = (
            lax.dot_general(
                source_embed, targets, (((1,), (1,)), ((), ())), preferred_element_type=jnp.float32
            )
            * factor
        )
        column_pot, logw_all = smalls[:, 0].reshape(-1), smalls[:, 1].reshape(-1)
        for iteration in range(ITERS):
            scores = (column_pot[None, :] - cost) * inverse_eps
            row_top = jnp.max(scores, axis=1)
            row_sum = jnp.sum(jnp.exp(scores - row_top[:, None]), axis=1)
            row_pot = epsilon * source_logw - epsilon * (row_top + jnp.log(row_sum))
            part = swap_order(lse((row_pot[:, None] - cost) * inverse_eps))
            if iteration < ITERS - 1:
                copies = jnp.broadcast_to(part[None], (blk * grp, blk, width))
                got = lax.all_to_all(copies, everyone, 0, 0)
                total = swap_order(lse(got)).reshape(-1)
                column_pot = epsilon * logw_all - epsilon * total
            else:
                copies = jnp.broadcast_to(part[:, None], (blk, grp, width)).reshape(blk * grp, width)
                got = lax.all_to_all(copies, everyone, 0, 0)
                own_column = epsilon * target_logw - epsilon * lse(got)
        return row_pot, own_column

    if chips == 4:
        shards = shards_square
        rows_spec, blk_spec = P(("blk", "grp")), P("blk")
    else:
        shards = shards_any
        rows_spec, blk_spec = P(everyone), P(("chip", "core"))
        mesh = Mesh(mesh.devices.reshape(chips, 2, grp), everyone)
    in_specs = (rows_spec, blk_spec, blk_spec, rows_spec, blk_spec)
    out_specs = (rows_spec, blk_spec)
    return jax.shard_map(shards, mesh=mesh, in_specs=in_specs, out_specs=out_specs, check_vma=False)
```

```python
import functools
import math

import jax
import jax.numpy as jnp
from jax import lax
from jax.experimental import pallas as pl
from jax.experimental.pallas import tpu as pltpu
from jax.sharding import Mesh, PartitionSpec as P

ITERS = 2
epsilon = 0.1
inverse_eps = 10.0
LOG2E = math.log2(math.e)
LN2 = math.log(2.0)
LANES = 128
SPARE = 8
SUBLANES = 8


def fetch(array, axis, step, size):
    return lax.ppermute(array, axis, [(i ^ step, i) for i in range(size)])


def doubled(held, step, chips):
    return jnp.concatenate([held, fetch(held, "chip", step, chips)])


def gather_any(array, small, chips):
    pair = jnp.stack([array, fetch(array, "core", 1, 2)])[None]
    smalls = jnp.stack([small, fetch(small, "core", 1, 2)])[None]
    step = 1
    while step < chips:
        pair = doubled(pair, step, chips)
        smalls = doubled(smalls, step, chips)
        step *= 2
    return pair.reshape(-1, array.shape[1]), smalls.reshape(-1, *small.shape)


def as_column(row):
    size = row.shape[1]
    here = lax.broadcasted_iota(jnp.int32, (LANES, LANES), 0)
    there = lax.broadcasted_iota(jnp.int32, (LANES, LANES), 1)
    parts = []
    for start in range(0, size, LANES):
        wide = jnp.broadcast_to(row[:, start : start + LANES], (LANES, LANES))
        parts.append(jnp.sum(jnp.where(here == there, wide, 0.0), axis=1, keepdims=True))
    return jnp.concatenate(parts, axis=0)


def as_row(column):
    size = column.shape[0]
    here = lax.broadcasted_iota(jnp.int32, (LANES, LANES), 0)
    there = lax.broadcasted_iota(jnp.int32, (LANES, LANES), 1)
    parts = []
    for start in range(0, size, LANES):
        wide = jnp.broadcast_to(column[start : start + LANES], (LANES, LANES))
        parts.append(jnp.sum(jnp.where(here == there, wide, 0.0), axis=0, keepdims=True))
    return jnp.concatenate(parts, axis=1)


CHUNK = 64


def chunks_of(rows):
    return [pl.ds(start, CHUNK) for start in range(0, rows, CHUNK)]


def row_sweep(score_of, blocks, rows, found_of, columns=None, others=None, kept=None):
    tops = []
    for at in chunks_of(rows):
        top = None if others is None else others[at, :]
        for p in blocks:
            score = score_of(at, p)
            if columns is not None:
                score = score + columns[p]
                kept[at, p * LANES : (p + 1) * LANES] = score
            top = score if top is None else jnp.maximum(top, score)
        tops.append(jnp.max(top, axis=1, keepdims=True))
    for at, top in zip(chunks_of(rows), tops):
        total = None
        for p in blocks:
            if columns is None:
                score = score_of(at, p)
            else:
                score = kept[at, p * LANES : (p + 1) * LANES]
            term = jnp.exp2(score - top)
            total = term if total is None else total + term
        total = jnp.sum(total, axis=1, keepdims=True)
        if others is not None:
            total = total + jnp.exp2(others[at, :] - top)
        found_of(at, top + jnp.log2(total))


def column_sweep(score_of, blocks, rows, row_pot, found_of):
    folds = (CHUNK // SUBLANES, SUBLANES, LANES)
    found = [[] for _ in blocks]
    for at in chunks_of(rows):
        addend = row_pot[at, :]
        for p in blocks:
            score = (score_of(at, p) + addend).reshape(folds)
            top = jnp.max(score, axis=0)
            found[p].append((top, jnp.sum(jnp.exp2(score - top[None]), axis=0)))
    for p in blocks:
        top = functools.reduce(jnp.maximum, [each for each, _ in found[p]])
        top = jnp.max(top, axis=0, keepdims=True)
        total = sum(each * jnp.exp2(at_top - top) for at_top, each in found[p])
        found_of(p, top + jnp.log2(jnp.sum(total, axis=0, keepdims=True)))


def products(source, targets, factor, smalls, scaled, table):
    for p, small in enumerate(smalls):
        table[0, p : p + 1, :] = small[1:2] * LOG2E
        table[1, p : p + 1, :] = small[0:1] * (inverse_eps * LOG2E)
    for p in range(0, len(smalls), 2):
        end = min(p + 2, len(smalls))
        lanes = slice(p * LANES, end * LANES)
        product = lax.dot_general(
            source[...], targets[lanes, :], (((1,), (1,)), ((), ())),
            preferred_element_type=jnp.float32,
        )
        shift = jnp.concatenate([table[1, q : q + 1, :] for q in range(p, end)], axis=1)
        scaled[:, lanes] = product * factor + shift


def head_kernel(
    own, init, target_logw, first, second, whole, small, first_plain, second_plain, init_row,
    logw_row, sems,
):
    rows, half = own.shape[0], first_plain.shape[0]
    copies = [
        pltpu.make_async_copy(own, whole.at[0:rows], sems.at[0]),
        pltpu.make_async_copy(init, init_row, sems.at[1]),
        pltpu.make_async_copy(target_logw, logw_row, sems.at[2]),
    ]
    for copy in copies:
        copy.start()
    for copy in copies:
        copy.wait()
    for out in (first, first_plain):
        out[0:half, :] = whole[0:half, :]
    for out in (second, second_plain):
        out[0:half, :] = whole[half:rows, :]
    small[0:1, :] = init_row[...]
    small[1:2, :] = logw_row[...]
    filler = jnp.zeros((SPARE - 2, LANES), jnp.float32)
    rest = jnp.concatenate([init_row[...], logw_row[...], filler], axis=0)
    for k in range(whole.shape[1] // LANES):
        lanes = slice(k * LANES, (k + 1) * LANES)
        part = (rest if k < 3 else jnp.zeros_like(rest)).astype(whole.dtype)
        first[half:, lanes] = part
        second[half:, lanes] = part
        whole[rows:, lanes] = part
        rest = rest - part.astype(jnp.float32)


def source_kernel(source, logw, whole, held, row_logw, passed, rows_row, sems):
    copies = [
        pltpu.make_async_copy(source, held, sems.at[0]),
        pltpu.make_async_copy(logw, rows_row, sems.at[1]),
    ]
    for copy in copies:
        copy.start()
    passed[...] = whole[...]
    for copy in copies:
        copy.wait()
    row_logw[...] = jnp.broadcast_to(as_column(rows_row[...] * LOG2E), row_logw.shape)


def sibling_kernel(whole, a_first, a_second, b_first, b_second, out):
    half = a_second.shape[0]
    block = 2 * half + SPARE
    out[0:block, :] = whole[...]
    out[block : block + half, :] = a_first[0:half, :]
    out[block + half : block + 2 * half, :] = a_second[...]
    out[block + 2 * half : 2 * block, :] = a_first[half:, :]
    out[2 * block : 2 * block + half, :] = b_first[...]
    out[2 * block + half : 3 * block, :] = b_second[...]


def unpack(message, end=None):
    end = message.shape[0] if end is None else end
    parts = [
        message[end - SPARE : end, k * LANES : (k + 1) * LANES].astype(jnp.float32)[0:2]
        for k in range(3)
    ]
    return (parts[0] + parts[1]) + parts[2]


def own_kernel(
    factor, source, whole, a_first, a_second, b_first, b_second, scaled, table, targets
):
    half = a_second.shape[0]
    pieces = (whole, whole, a_first, a_second, b_first, b_second)
    targets[0 : 2 * half, :] = whole[0 : 2 * half, :]
    for k in range(2, 6):
        targets[k * half : (k + 1) * half, :] = pieces[k][0:half, :]
    smalls = [unpack(whole), unpack(a_first), unpack(b_second)]
    products(source, targets, factor, smalls, scaled, table)


def sibling_scores_kernel(factor, source, sibling, own, scaled, table, found, targets):
    width = targets.shape[0] // 3
    block = width + SPARE
    smalls = []
    for k in range(3):
        targets[k * width : (k + 1) * width, :] = sibling[k * block : k * block + width, :]
        smalls.append(unpack(sibling, (k + 1) * block))
    products(source, targets, factor, smalls, scaled, table)

    def score_of(at, p):
        part = (own, scaled)[p % 2]
        return part[at, p // 2 * LANES : (p // 2 + 1) * LANES]

    def found_of(at, value):
        found[at, :] = jnp.broadcast_to(value, (CHUNK, LANES))

    row_sweep(score_of, range(6), scaled.shape[0], found_of)


def pass_kernel(message, tie, out):
    out[...] = message[...]


def far_kernel(
    factor, source, far_a, far_b, sibling_a, sibling_b, near, scaled, table, targets
):
    half = targets.shape[0] // 4
    for k, piece in enumerate((far_a, far_b, sibling_a, sibling_b)):
        targets[k * half : (k + 1) * half, :] = piece[0:half, :]
    smalls = [unpack(far_a), unpack(sibling_a)]
    products(source, targets, factor, smalls, scaled, table)


def neighbour_step(me, turn):
    step = 2 + 2 * (me % 2)
    return step if turn == 0 else 6 - step


def positions(me):
    sibling = me ^ 1
    own = [me, me ^ neighbour_step(me, 0), me ^ neighbour_step(me, 1), me ^ 6]
    other = [
        sibling,
        sibling ^ neighbour_step(sibling, 0),
        sibling ^ neighbour_step(sibling, 1),
        sibling ^ 6,
    ]
    return [block for pair in zip(own, other) for block in pair]


class Held:

    def __init__(self, own, own_table, sibling, sibling_table, far, far_table):
        self.near = own.shape[1] // LANES * 2
        self.total = self.near + far.shape[1] // LANES
        self.scores, self.tables = (own, sibling, far), (own_table, sibling_table, far_table)

    def place(self, p):
        return (p % 2, p // 2) if p < self.near else (2, p - self.near)

    def score(self, at, p):
        part, k = self.place(p)
        return self.scores[part][at, k * LANES : (k + 1) * LANES]

    def row(self, kind, p):
        part, k = self.place(p)
        return self.tables[part][kind, k : k + 1, :]


def first_kernel(
    own, own_table, sibling, sibling_table, far, far_table, found, logw, message, row_pot, ordered
):
    order = positions(lax.axis_index("blk"))
    held = Held(own, own_table, sibling, sibling_table, far, far_table)
    rows = own.shape[0]

    def row_found(at, value):
        row_pot[at, :] = logw[at, :] - value

    def column_found(p, value):
        ordered[pl.ds(order[p], 1), :] = value - held.row(1, p)

    row_sweep(held.score, range(held.near, held.total), rows, row_found, others=found)
    column_sweep(held.score, range(held.total), rows, row_pot, column_found)
    message[...] = jnp.broadcast_to(ordered[...][None], message.shape)


def second_kernel(
    copies, own, own_table, sibling, sibling_table, far, far_table, got, logw, row, message,
    row_pot, ordered, kept,
):
    order = positions(lax.axis_index("blk"))
    held = Held(own, own_table, sibling, sibling_table, far, far_table)
    rows = own.shape[0]
    values = got[...]
    top = jnp.max(values, axis=0)
    ordered[...] = top + jnp.log2(jnp.sum(jnp.exp2(values - top[None]), axis=0))
    columns = []
    for p in range(held.total):
        columns.append(held.row(0, p) - ordered[pl.ds(order[p], 1), :] - held.row(1, p))

    def row_found(at, value):
        row_pot[at, :] = logw[at, :] - value

    def column_found(p, value):
        at = pl.ds((held.total - 1 - order[p]) * copies, copies)
        message[at, :] = jnp.broadcast_to(value - held.row(1, p), (copies, LANES))

    row_sweep(held.score, range(held.total), rows, row_found, columns=columns, kept=kept)
    column_sweep(held.score, range(held.total), rows, row_pot, column_found)
    row[...] = as_row(row_pot[:, 0:1]) * (epsilon * LN2)


def last_kernel(got, small, row, row_out, column_out):
    values = got[...]
    top = jnp.max(values, axis=0, keepdims=True)
    total = top + jnp.log2(jnp.sum(jnp.exp2(values - top), axis=0, keepdims=True))
    column_out[...] = epsilon * small[1:2, :] - (epsilon * LN2) * total
    row_out[...] = row[...]


def lse(values):
    top = jnp.max(values, axis=0)
    return top + jnp.log(jnp.sum(jnp.exp(values - top[None]), axis=0))


def solution(mesh):
    blk, grp = mesh.shape["blk"], mesh.shape["grp"]
    chips = blk // 2
    everyone = ("chip", "core", "grp")

    def shards_square(source_embed, target_embed, target_init, source_logw, target_logw):
        rows, depth = source_embed.shape
        width = target_embed.shape[0]
        half = width // 2
        factor = inverse_eps * LOG2E / math.sqrt(depth)
        vmem, hbm = pl.BlockSpec(memory_space=pltpu.VMEM), pl.BlockSpec(memory_space=pltpu.HBM)
        params = pltpu.CompilerParams(vmem_limit_bytes=16 * 1024 * 1024)

        def values(*shape):
            return jax.ShapeDtypeStruct(shape, jnp.float32)

        def cost(targets, sweeps):
            return pl.CostEstimate(
                flops=2 * rows * targets * depth + 16 * sweeps * rows * blk * width,
                transcendentals=2 * sweeps * rows * blk * width,
                bytes_accessed=2 * (rows + targets) * depth,
            )

        def along(array, turn):
            return lax.ppermute(
                array, "blk", [(i ^ neighbour_step(i, turn), i) for i in range(blk)]
            )

        def to_sibling(array):
            return fetch(array, "blk", 1, blk)

        def exchange(message):
            order = list(range(blk * grp))[::-1]
            return lax.all_to_all(message, ("blk", "grp"), 0, 0, axis_index_groups=[order])

        def block_of(size):
            return jax.ShapeDtypeStruct((size, depth), target_embed.dtype)

        def in_hbm(*arrays):
            return [pltpu.with_memory_space_constraint(each, pltpu.HBM) for each in arrays]

        first, second, whole, small, first_plain, second_plain = pl.pallas_call(
            head_kernel,
            out_shape=(
                block_of(half + SPARE),
                block_of(half + SPARE),
                block_of(width + SPARE),
                values(2, width),
                block_of(half),
                block_of(half),
            ),
            in_specs=[hbm] * 3,
            out_specs=(vmem,) * 6,
            scratch_shapes=[
                pltpu.VMEM((1, width), jnp.float32),
                pltpu.VMEM((1, width), jnp.float32),
                pltpu.SemaphoreType.DMA((3,)),
            ],
            compiler_params=params,
        )(*in_hbm(target_embed, target_init.reshape(1, width), target_logw.reshape(1, width)))
        a_first = along(first, 0)
        b_second = along(second, 1)
        a_second = along(second_plain, 0)
        b_first = along(first_plain, 1)
        far_a = along(a_first, 1)
        far_b = along(b_second[:half], 0)
        source, logw, passed = pl.pallas_call(
            source_kernel,
            out_shape=(
                jax.ShapeDtypeStruct((rows, depth), source_embed.dtype),
                values(rows, LANES),
                block_of(width + SPARE),
            ),
            in_specs=[hbm] * 2 + [vmem],
            out_specs=(vmem,) * 3,
            scratch_shapes=[pltpu.VMEM((1, rows), jnp.float32), pltpu.SemaphoreType.DMA((2,))],
            compiler_params=params,
        )(*in_hbm(source_embed, source_logw.reshape(1, rows)), whole)
        near = (a_first, a_second, b_first, b_second)
        sibling = pl.pallas_call(
            sibling_kernel,
            out_shape=block_of(3 * (width + SPARE)),
            in_specs=[vmem] * 5,
            out_specs=vmem,
            compiler_params=params,
            cost_estimate=cost(0, 0),
        )(passed, *near)
        sibling = to_sibling(sibling)

        def table():
            return values(2, SUBLANES, width)

        def scores_of(kernel, blocks, pieces, extra=()):
            return pl.pallas_call(
                functools.partial(kernel, factor),
                out_shape=(values(rows, blocks * width), table(), *extra),
                in_specs=[vmem] * (1 + len(pieces)),
                out_specs=(vmem,) * (2 + len(extra)),
                scratch_shapes=[pltpu.VMEM((blocks * width, depth), target_embed.dtype)],
                compiler_params=params,
                cost_estimate=cost(0, 0),
            )(source, *pieces)

        own = scores_of(own_kernel, 3, (whole, *near))

        def passed_on(message, tie, weight):
            return pl.pallas_call(
                pass_kernel,
                out_shape=jax.ShapeDtypeStruct(message.shape, message.dtype),
                in_specs=[vmem] * 2,
                out_specs=vmem,
                compiler_params=params,
                cost_estimate=cost(weight * width, 0),
            )(message, tie)

        sibling_a = to_sibling(passed_on(far_a, own[1], 0))
        sibling_b = to_sibling(passed_on(far_b, own[1], 50))
        *other, found = scores_of(
            sibling_scores_kernel, 3, (sibling, own[0]), (values(rows, LANES),)
        )
        far = scores_of(far_kernel, 2, (far_a, far_b, sibling_a, sibling_b, other[0]))
        scores = (*own, *other, *far)
        row_scratch = pltpu.VMEM((rows, LANES), jnp.float32)
        block_scratch = pltpu.VMEM((blk, width), jnp.float32)
        message = pl.pallas_call(
            first_kernel,
            out_shape=values(blk * grp, blk, width),
            in_specs=[vmem] * 8,
            out_specs=vmem,
            scratch_shapes=[row_scratch, block_scratch],
            compiler_params=params,
            cost_estimate=cost(0, 1),
        )(*scores, found, logw)
        got = exchange(message)
        row, message = pl.pallas_call(
            functools.partial(second_kernel, grp),
            out_shape=(values(1, rows), values(blk * grp, width)),
            in_specs=[vmem] * 8,
            out_specs=(vmem, vmem),
            scratch_shapes=[
                row_scratch,
                block_scratch,
                pltpu.VMEM((rows, blk * width), jnp.float32),
            ],
            compiler_params=params,
            cost_estimate=cost(0, 1),
        )(*scores, got, logw)
        got = exchange(message)
        row_pot, column_pot = pl.pallas_call(
            last_kernel,
            out_shape=(values(1, rows), values(1, width)),
            in_specs=[vmem] * 3,
            out_specs=(vmem, vmem),
            compiler_params=params,
        )(got, small, row)
        return row_pot.reshape(rows), column_pot.reshape(width)

    def shards_any(source_embed, target_embed, target_init, source_logw, target_logw):
        width, depth = target_embed.shape
        factor = -1.0 / math.sqrt(depth)
        me = lax.axis_index("chip") * 2 + lax.axis_index("core")

        def swap_order(values):
            parts = values.reshape(blk, width)
            step = 1
            while step < blk:
                pairs = parts.reshape(blk // (2 * step), 2, step, width)
                pairs = jnp.where(me & step, pairs[:, ::-1], pairs)
                parts = pairs.reshape(blk, width)
                step *= 2
            return parts

        small = jnp.stack([target_init, target_logw])
        targets, smalls = gather_any(target_embed, small, chips)
        cost = (
            lax.dot_general(
                source_embed, targets, (((1,), (1,)), ((), ())), preferred_element_type=jnp.float32
            )
            * factor
        )
        column_pot, logw_all = smalls[:, 0].reshape(-1), smalls[:, 1].reshape(-1)
        for iteration in range(ITERS):
            scores = (column_pot[None, :] - cost) * inverse_eps
            row_top = jnp.max(scores, axis=1)
            row_sum = jnp.sum(jnp.exp(scores - row_top[:, None]), axis=1)
            row_pot = epsilon * source_logw - epsilon * (row_top + jnp.log(row_sum))
            part = swap_order(lse((row_pot[:, None] - cost) * inverse_eps))
            if iteration < ITERS - 1:
                copies = jnp.broadcast_to(part[None], (blk * grp, blk, width))
                got = lax.all_to_all(copies, everyone, 0, 0)
                total = swap_order(lse(got)).reshape(-1)
                column_pot = epsilon * logw_all - epsilon * total
            else:
                copies = jnp.broadcast_to(part[:, None], (blk, grp, width)).reshape(blk * grp, width)
                got = lax.all_to_all(copies, everyone, 0, 0)
                own_column = epsilon * target_logw - epsilon * lse(got)
        return row_pot, own_column

    if chips == 4:
        shards = shards_square
        rows_spec, blk_spec = P(("blk", "grp")), P("blk")
    else:
        shards = shards_any
        rows_spec, blk_spec = P(everyone), P(("chip", "core"))
        mesh = Mesh(mesh.devices.reshape(chips, 2, grp), everyone)
    in_specs = (rows_spec, blk_spec, blk_spec, rows_spec, blk_spec)
    out_specs = (rows_spec, blk_spec)
    return jax.shard_map(shards, mesh=mesh, in_specs=in_specs, out_specs=out_specs, check_vma=False)
```

```python
import functools
import math

import jax
import jax.numpy as jnp
from jax import lax
from jax.experimental import pallas as pl
from jax.experimental.pallas import tpu as pltpu
from jax.sharding import Mesh, PartitionSpec as P

ITERS = 2
epsilon = 0.1
inverse_eps = 10.0
LOG2E = math.log2(math.e)
LN2 = math.log(2.0)
LANES = 128
SPARE = 8
SUBLANES = 8


def fetch(array, axis, step, size):
    return lax.ppermute(array, axis, [(i ^ step, i) for i in range(size)])


def doubled(held, step, chips):
    return jnp.concatenate([held, fetch(held, "chip", step, chips)])


def gather_any(array, small, chips):
    pair = jnp.stack([array, fetch(array, "core", 1, 2)])[None]
    smalls = jnp.stack([small, fetch(small, "core", 1, 2)])[None]
    step = 1
    while step < chips:
        pair = doubled(pair, step, chips)
        smalls = doubled(smalls, step, chips)
        step *= 2
    return pair.reshape(-1, array.shape[1]), smalls.reshape(-1, *small.shape)


def as_column(row):
    size = row.shape[1]
    here = lax.broadcasted_iota(jnp.int32, (LANES, LANES), 0)
    there = lax.broadcasted_iota(jnp.int32, (LANES, LANES), 1)
    parts = []
    for start in range(0, size, LANES):
        wide = jnp.broadcast_to(row[:, start : start + LANES], (LANES, LANES))
        parts.append(jnp.sum(jnp.where(here == there, wide, 0.0), axis=1, keepdims=True))
    return jnp.concatenate(parts, axis=0)


def as_row(column):
    size = column.shape[0]
    here = lax.broadcasted_iota(jnp.int32, (LANES, LANES), 0)
    there = lax.broadcasted_iota(jnp.int32, (LANES, LANES), 1)
    parts = []
    for start in range(0, size, LANES):
        wide = jnp.broadcast_to(column[start : start + LANES], (LANES, LANES))
        parts.append(jnp.sum(jnp.where(here == there, wide, 0.0), axis=0, keepdims=True))
    return jnp.concatenate(parts, axis=1)


CHUNK = 64


def chunks_of(rows):
    return [pl.ds(start, CHUNK) for start in range(0, rows, CHUNK)]


def row_sweep(score_of, blocks, rows, found_of, columns=None, others=None):
    tops = []
    for at in chunks_of(rows):
        top = None if others is None else others[at, :]
        for p in blocks:
            score = score_of(at, p)
            score = score if columns is None else score + columns[p]
            top = score if top is None else jnp.maximum(top, score)
        tops.append(jnp.max(top, axis=1, keepdims=True))
    for at, top in zip(chunks_of(rows), tops):
        total = None
        for p in blocks:
            shift = -top if columns is None else columns[p] - top
            term = jnp.exp2(score_of(at, p) + shift)
            total = term if total is None else total + term
        total = jnp.sum(total, axis=1, keepdims=True)
        if others is not None:
            total = total + jnp.exp2(others[at, :] - top)
        found_of(at, top + jnp.log2(total))


def column_sweep(score_of, blocks, rows, row_pot, found_of):
    folds = (CHUNK // SUBLANES, SUBLANES, LANES)
    for start in range(0, len(blocks), 2):
        pair = blocks[start : start + 2]
        found = {p: [] for p in pair}
        for at in chunks_of(rows):
            addend = row_pot[at, :]
            for p in pair:
                score = (score_of(at, p) + addend).reshape(folds)
                top = jnp.max(score, axis=0)
                found[p].append((top, jnp.sum(jnp.exp2(score - top[None]), axis=0)))
        for p in pair:
            top = functools.reduce(jnp.maximum, [each for each, _ in found[p]])
            top = jnp.max(top, axis=0, keepdims=True)
            total = sum(each * jnp.exp2(at_top - top) for at_top, each in found[p])
            found_of(p, top + jnp.log2(jnp.sum(total, axis=0, keepdims=True)))


def products(source, targets, factor, smalls, scaled, table):
    for p, small in enumerate(smalls):
        table[0, p : p + 1, :] = small[1:2] * LOG2E
        table[1, p : p + 1, :] = small[0:1] * (inverse_eps * LOG2E)
    for p in range(0, len(smalls), 2):
        end = min(p + 2, len(smalls))
        lanes = slice(p * LANES, end * LANES)
        product = lax.dot_general(
            source[...], targets[lanes, :], (((1,), (1,)), ((), ())),
            preferred_element_type=jnp.float32,
        )
        shift = jnp.concatenate([table[1, q : q + 1, :] for q in range(p, end)], axis=1)
        scaled[:, lanes] = product * factor + shift


def head_kernel(
    own, init, target_logw, first, second, whole, small, first_plain, second_plain, init_row,
    logw_row, sems,
):
    rows, cut, rest_rows = own.shape[0], first_plain.shape[0], second_plain.shape[0]
    copies = [
        pltpu.make_async_copy(own, whole.at[0:rows], sems.at[0]),
        pltpu.make_async_copy(init, init_row, sems.at[1]),
        pltpu.make_async_copy(target_logw, logw_row, sems.at[2]),
    ]
    for copy in copies:
        copy.start()
    for copy in copies:
        copy.wait()
    for out in (first, first_plain):
        out[0:cut, :] = whole[0:cut, :]
    for out in (second, second_plain):
        out[0:rest_rows, :] = whole[cut:rows, :]
    small[0:1, :] = init_row[...]
    small[1:2, :] = logw_row[...]
    filler = jnp.zeros((SPARE - 2, LANES), jnp.float32)
    rest = jnp.concatenate([init_row[...], logw_row[...], filler], axis=0)
    for k in range(whole.shape[1] // LANES):
        lanes = slice(k * LANES, (k + 1) * LANES)
        part = (rest if k < 3 else jnp.zeros_like(rest)).astype(whole.dtype)
        first[cut:, lanes] = part
        second[rest_rows:, lanes] = part
        whole[rows:, lanes] = part
        rest = rest - part.astype(jnp.float32)


def source_kernel(source, logw, whole, held, row_logw, passed, rows_row, sems):
    copies = [
        pltpu.make_async_copy(source, held, sems.at[0]),
        pltpu.make_async_copy(logw, rows_row, sems.at[1]),
    ]
    for copy in copies:
        copy.start()
    passed[...] = whole[...]
    for copy in copies:
        copy.wait()
    row_logw[...] = jnp.broadcast_to(as_column(rows_row[...] * LOG2E), row_logw.shape)


def fill(out, start, *halves):
    cut, rest_rows = halves[0][1], halves[1][1]
    out[start : start + cut, :] = halves[0][0][0:cut, :]
    out[start + cut : start + cut + rest_rows, :] = halves[1][0][0:rest_rows, :]


def sibling_kernel(whole, a_first, a_second, b_first, b_second, out):
    cut, rest_rows = b_first.shape[0], a_second.shape[0]
    block = cut + rest_rows + SPARE
    out[0:block, :] = whole[...]
    fill(out, block, (a_first, cut), (a_second, rest_rows))
    out[2 * block - SPARE : 2 * block, :] = a_first[cut:, :]
    fill(out, 2 * block, (b_first, cut), (b_second, rest_rows))
    out[3 * block - SPARE : 3 * block, :] = b_second[rest_rows:, :]


def unpack(message, end=None):
    end = message.shape[0] if end is None else end
    parts = [
        message[end - SPARE : end, k * LANES : (k + 1) * LANES].astype(jnp.float32)[0:2]
        for k in range(3)
    ]
    return (parts[0] + parts[1]) + parts[2]


def own_kernel(
    factor, source, whole, a_first, a_second, b_first, b_second, scaled, table, targets
):
    cut, rest_rows = b_first.shape[0], a_second.shape[0]
    width = cut + rest_rows
    targets[0:width, :] = whole[0:width, :]
    fill(targets, width, (a_first, cut), (a_second, rest_rows))
    fill(targets, 2 * width, (b_first, cut), (b_second, rest_rows))
    smalls = [unpack(whole), unpack(a_first), unpack(b_second)]
    products(source, targets, factor, smalls, scaled, table)


def sibling_scores_kernel(factor, source, sibling, own, scaled, table, found, targets):
    width = targets.shape[0] // 3
    block = width + SPARE
    smalls = []
    for k in range(3):
        targets[k * width : (k + 1) * width, :] = sibling[k * block : k * block + width, :]
        smalls.append(unpack(sibling, (k + 1) * block))
    products(source, targets, factor, smalls, scaled, table)

    def score_of(at, p):
        part = (own, scaled)[p % 2]
        return part[at, p // 2 * LANES : (p // 2 + 1) * LANES]

    def found_of(at, value):
        found[at, :] = jnp.broadcast_to(value, (CHUNK, LANES))

    row_sweep(score_of, range(6), scaled.shape[0], found_of)


def pass_kernel(message, tie, out):
    out[...] = message[...]


def far_kernel(
    factor, source, far_a, far_b, sibling_a, sibling_b, near, scaled, table, targets
):
    width = targets.shape[0] // 2
    rest_rows = far_b.shape[0]
    cut = width - rest_rows
    fill(targets, 0, (far_a, cut), (far_b, rest_rows))
    fill(targets, width, (sibling_a, cut), (sibling_b, rest_rows))
    smalls = [unpack(far_a), unpack(sibling_a)]
    products(source, targets, factor, smalls, scaled, table)


def neighbour_step(me, turn):
    step = 2 + 2 * (me % 2)
    return step if turn == 0 else 6 - step


def positions(me):
    sibling = me ^ 1
    own = [me, me ^ neighbour_step(me, 0), me ^ neighbour_step(me, 1), me ^ 6]
    other = [
        sibling,
        sibling ^ neighbour_step(sibling, 0),
        sibling ^ neighbour_step(sibling, 1),
        sibling ^ 6,
    ]
    return [block for pair in zip(own, other) for block in pair]


class Held:

    def __init__(self, own, own_table, sibling, sibling_table, far, far_table):
        self.near = own.shape[1] // LANES * 2
        self.total = self.near + far.shape[1] // LANES
        self.scores, self.tables = (own, sibling, far), (own_table, sibling_table, far_table)

    def place(self, p):
        return (p % 2, p // 2) if p < self.near else (2, p - self.near)

    def score(self, at, p):
        part, k = self.place(p)
        return self.scores[part][at, k * LANES : (k + 1) * LANES]

    def row(self, kind, p):
        part, k = self.place(p)
        return self.tables[part][kind, k : k + 1, :]


def first_kernel(
    own, own_table, sibling, sibling_table, far, far_table, found, logw, message, row_pot, ordered
):
    order = positions(lax.axis_index("blk"))
    held = Held(own, own_table, sibling, sibling_table, far, far_table)
    rows = own.shape[0]

    def row_found(at, value):
        row_pot[at, :] = logw[at, :] - value

    def column_found(p, value):
        ordered[pl.ds(order[p], 1), :] = value - held.row(1, p)

    row_sweep(held.score, range(held.near, held.total), rows, row_found, others=found)
    column_sweep(held.score, range(held.total), rows, row_pot, column_found)
    message[...] = jnp.broadcast_to(ordered[...][None], message.shape)


def second_kernel(
    copies, own, own_table, sibling, sibling_table, far, far_table, got, logw, row, message,
    row_pot, ordered,
):
    order = positions(lax.axis_index("blk"))
    held = Held(own, own_table, sibling, sibling_table, far, far_table)
    rows = own.shape[0]
    values = got[...]
    top = jnp.max(values, axis=0)
    ordered[...] = top + jnp.log2(jnp.sum(jnp.exp2(values - top[None]), axis=0))
    columns = []
    for p in range(held.total):
        columns.append(held.row(0, p) - ordered[pl.ds(order[p], 1), :] - held.row(1, p))

    def row_found(at, value):
        row_pot[at, :] = logw[at, :] - value

    def column_found(p, value):
        at = pl.ds((held.total - 1 - order[p]) * copies, copies)
        message[at, :] = jnp.broadcast_to(value - held.row(1, p), (copies, LANES))

    row_sweep(held.score, range(held.total), rows, row_found, columns=columns)
    column_sweep(held.score, range(held.total), rows, row_pot, column_found)
    row[...] = as_row(row_pot[:, 0:1]) * (epsilon * LN2)


def last_kernel(got, small, row, row_out, column_out):
    values = got[...]
    top = jnp.max(values, axis=0, keepdims=True)
    total = top + jnp.log2(jnp.sum(jnp.exp2(values - top), axis=0, keepdims=True))
    column_out[...] = epsilon * small[1:2, :] - (epsilon * LN2) * total
    row_out[...] = row[...]


def lse(values):
    top = jnp.max(values, axis=0)
    return top + jnp.log(jnp.sum(jnp.exp(values - top[None]), axis=0))


def solution(mesh):
    blk, grp = mesh.shape["blk"], mesh.shape["grp"]
    chips = blk // 2
    everyone = ("chip", "core", "grp")

    def shards_square(source_embed, target_embed, target_init, source_logw, target_logw):
        rows, depth = source_embed.shape
        width = target_embed.shape[0]
        cut = width // 2
        factor = inverse_eps * LOG2E / math.sqrt(depth)
        vmem, hbm = pl.BlockSpec(memory_space=pltpu.VMEM), pl.BlockSpec(memory_space=pltpu.HBM)
        params = pltpu.CompilerParams(vmem_limit_bytes=16 * 1024 * 1024)

        def values(*shape):
            return jax.ShapeDtypeStruct(shape, jnp.float32)

        def cost(targets, sweeps):
            return pl.CostEstimate(
                flops=2 * rows * targets * depth + 16 * sweeps * rows * blk * width,
                transcendentals=2 * sweeps * rows * blk * width,
                bytes_accessed=2 * (rows + targets) * depth,
            )

        def along(array, turn):
            return lax.ppermute(
                array, "blk", [(i ^ neighbour_step(i, turn), i) for i in range(blk)]
            )

        def to_sibling(array):
            return fetch(array, "blk", 1, blk)

        def exchange(message):
            order = list(range(blk * grp))[::-1]
            return lax.all_to_all(message, ("blk", "grp"), 0, 0, axis_index_groups=[order])

        def block_of(size):
            return jax.ShapeDtypeStruct((size, depth), target_embed.dtype)

        def in_hbm(*arrays):
            return [pltpu.with_memory_space_constraint(each, pltpu.HBM) for each in arrays]

        first, second, whole, small, first_plain, second_plain = pl.pallas_call(
            head_kernel,
            out_shape=(
                block_of(cut + SPARE),
                block_of(width - cut + SPARE),
                block_of(width + SPARE),
                values(2, width),
                block_of(cut),
                block_of(width - cut),
            ),
            in_specs=[hbm] * 3,
            out_specs=(vmem,) * 6,
            scratch_shapes=[
                pltpu.VMEM((1, width), jnp.float32),
                pltpu.VMEM((1, width), jnp.float32),
                pltpu.SemaphoreType.DMA((3,)),
            ],
            compiler_params=params,
        )(*in_hbm(target_embed, target_init.reshape(1, width), target_logw.reshape(1, width)))
        a_first = along(first, 0)
        b_second = along(second, 1)
        a_second = along(second_plain, 0)
        b_first = along(first_plain, 1)
        far_a = along(a_first, 1)
        far_b = along(b_second[: width - cut], 0)
        source, logw, passed = pl.pallas_call(
            source_kernel,
            out_shape=(
                jax.ShapeDtypeStruct((rows, depth), source_embed.dtype),
                values(rows, LANES),
                block_of(width + SPARE),
            ),
            in_specs=[hbm] * 2 + [vmem],
            out_specs=(vmem,) * 3,
            scratch_shapes=[pltpu.VMEM((1, rows), jnp.float32), pltpu.SemaphoreType.DMA((2,))],
            compiler_params=params,
        )(*in_hbm(source_embed, source_logw.reshape(1, rows)), whole)
        near = (a_first, a_second, b_first, b_second)
        sibling = pl.pallas_call(
            sibling_kernel,
            out_shape=block_of(3 * (width + SPARE)),
            in_specs=[vmem] * 5,
            out_specs=vmem,
            compiler_params=params,
            cost_estimate=cost(0, 0),
        )(passed, *near)
        sibling = to_sibling(sibling)

        def table():
            return values(2, SUBLANES, width)

        def scores_of(kernel, blocks, pieces, extra=()):
            return pl.pallas_call(
                functools.partial(kernel, factor),
                out_shape=(values(rows, blocks * width), table(), *extra),
                in_specs=[vmem] * (1 + len(pieces)),
                out_specs=(vmem,) * (2 + len(extra)),
                scratch_shapes=[pltpu.VMEM((blocks * width, depth), target_embed.dtype)],
                compiler_params=params,
                cost_estimate=cost(0, 0),
            )(source, *pieces)

        own = scores_of(own_kernel, 3, (whole, *near))

        def passed_on(message, tie, weight):
            return pl.pallas_call(
                pass_kernel,
                out_shape=jax.ShapeDtypeStruct(message.shape, message.dtype),
                in_specs=[vmem] * 2,
                out_specs=vmem,
                compiler_params=params,
                cost_estimate=cost(weight * width, 0),
            )(message, tie)

        sibling_a = to_sibling(passed_on(far_a, own[1], 0))
        sibling_b = to_sibling(passed_on(far_b, own[1], 50))
        *other, found = scores_of(
            sibling_scores_kernel, 3, (sibling, own[0]), (values(rows, LANES),)
        )
        far = scores_of(far_kernel, 2, (far_a, far_b, sibling_a, sibling_b, other[0]))
        scores = (*own, *other, *far)
        row_scratch = pltpu.VMEM((rows, LANES), jnp.float32)
        block_scratch = pltpu.VMEM((blk, width), jnp.float32)
        message = pl.pallas_call(
            first_kernel,
            out_shape=values(blk * grp, blk, width),
            in_specs=[vmem] * 8,
            out_specs=vmem,
            scratch_shapes=[row_scratch, block_scratch],
            compiler_params=params,
            cost_estimate=cost(0, 1),
        )(*scores, found, logw)
        got = exchange(message)
        row, message = pl.pallas_call(
            functools.partial(second_kernel, grp),
            out_shape=(values(1, rows), values(blk * grp, width)),
            in_specs=[vmem] * 8,
            out_specs=(vmem, vmem),
            scratch_shapes=[row_scratch, block_scratch],
            compiler_params=params,
            cost_estimate=cost(0, 1),
        )(*scores, got, logw)
        got = exchange(message)
        row_pot, column_pot = pl.pallas_call(
            last_kernel,
            out_shape=(values(1, rows), values(1, width)),
            in_specs=[vmem] * 3,
            out_specs=(vmem, vmem),
            compiler_params=params,
        )(got, small, row)
        return row_pot.reshape(rows), column_pot.reshape(width)

    def shards_any(source_embed, target_embed, target_init, source_logw, target_logw):
        width, depth = target_embed.shape
        factor = -1.0 / math.sqrt(depth)
        me = lax.axis_index("chip") * 2 + lax.axis_index("core")

        def swap_order(values):
            parts = values.reshape(blk, width)
            step = 1
            while step < blk:
                pairs = parts.reshape(blk // (2 * step), 2, step, width)
                pairs = jnp.where(me & step, pairs[:, ::-1], pairs)
                parts = pairs.reshape(blk, width)
                step *= 2
            return parts

        small = jnp.stack([target_init, target_logw])
        targets, smalls = gather_any(target_embed, small, chips)
        cost = (
            lax.dot_general(
                source_embed, targets, (((1,), (1,)), ((), ())), preferred_element_type=jnp.float32
            )
            * factor
        )
        column_pot, logw_all = smalls[:, 0].reshape(-1), smalls[:, 1].reshape(-1)
        for iteration in range(ITERS):
            scores = (column_pot[None, :] - cost) * inverse_eps
            row_top = jnp.max(scores, axis=1)
            row_sum = jnp.sum(jnp.exp(scores - row_top[:, None]), axis=1)
            row_pot = epsilon * source_logw - epsilon * (row_top + jnp.log(row_sum))
            part = swap_order(lse((row_pot[:, None] - cost) * inverse_eps))
            if iteration < ITERS - 1:
                copies = jnp.broadcast_to(part[None], (blk * grp, blk, width))
                got = lax.all_to_all(copies, everyone, 0, 0)
                total = swap_order(lse(got)).reshape(-1)
                column_pot = epsilon * logw_all - epsilon * total
            else:
                copies = jnp.broadcast_to(part[:, None], (blk, grp, width)).reshape(blk * grp, width)
                got = lax.all_to_all(copies, everyone, 0, 0)
                own_column = epsilon * target_logw - epsilon * lse(got)
        return row_pot, own_column

    if chips == 4:
        shards = shards_square
        rows_spec, blk_spec = P(("blk", "grp")), P("blk")
    else:
        shards = shards_any
        rows_spec, blk_spec = P(everyone), P(("chip", "core"))
        mesh = Mesh(mesh.devices.reshape(chips, 2, grp), everyone)
    in_specs = (rows_spec, blk_spec, blk_spec, rows_spec, blk_spec)
    out_specs = (rows_spec, blk_spec)
    return jax.shard_map(shards, mesh=mesh, in_specs=in_specs, out_specs=out_specs, check_vma=False)
```

```python
import functools
import math

import jax
import jax.numpy as jnp
from jax import lax
from jax.experimental import pallas as pl
from jax.experimental.pallas import tpu as pltpu
from jax.sharding import Mesh, PartitionSpec as P

ITERS = 2
epsilon = 0.1
inverse_eps = 10.0
LOG2E = math.log2(math.e)
LN2 = math.log(2.0)
LANES = 128
SPARE = 8
SUBLANES = 8


def fetch(array, axis, step, size):
    return lax.ppermute(array, axis, [(i ^ step, i) for i in range(size)])


def doubled(held, step, chips):
    return jnp.concatenate([held, fetch(held, "chip", step, chips)])


def gather_any(array, small, chips):
    pair = jnp.stack([array, fetch(array, "core", 1, 2)])[None]
    smalls = jnp.stack([small, fetch(small, "core", 1, 2)])[None]
    step = 1
    while step < chips:
        pair = doubled(pair, step, chips)
        smalls = doubled(smalls, step, chips)
        step *= 2
    return pair.reshape(-1, array.shape[1]), smalls.reshape(-1, *small.shape)


def as_column(row):
    size = row.shape[1]
    here = lax.broadcasted_iota(jnp.int32, (LANES, LANES), 0)
    there = lax.broadcasted_iota(jnp.int32, (LANES, LANES), 1)
    parts = []
    for start in range(0, size, LANES):
        wide = jnp.broadcast_to(row[:, start : start + LANES], (LANES, LANES))
        parts.append(jnp.sum(jnp.where(here == there, wide, 0.0), axis=1, keepdims=True))
    return jnp.concatenate(parts, axis=0)


def as_row(column):
    size = column.shape[0]
    here = lax.broadcasted_iota(jnp.int32, (LANES, LANES), 0)
    there = lax.broadcasted_iota(jnp.int32, (LANES, LANES), 1)
    parts = []
    for start in range(0, size, LANES):
        wide = jnp.broadcast_to(column[start : start + LANES], (LANES, LANES))
        parts.append(jnp.sum(jnp.where(here == there, wide, 0.0), axis=0, keepdims=True))
    return jnp.concatenate(parts, axis=1)


CHUNK = 64


def chunks_of(rows):
    return [pl.ds(start, CHUNK) for start in range(0, rows, CHUNK)]


def row_sweep(score_of, blocks, rows, found_of, columns=None, others=None):
    tops = []
    for at in chunks_of(rows):
        top = None if others is None else others[at, :]
        for p in blocks:
            score = score_of(at, p)
            score = score if columns is None else score + columns[p]
            top = score if top is None else jnp.maximum(top, score)
        tops.append(jnp.max(top, axis=1, keepdims=True))
    for at, top in zip(chunks_of(rows), tops):
        total = None
        for p in blocks:
            shift = -top if columns is None else columns[p] - top
            term = jnp.exp2(score_of(at, p) + shift)
            total = term if total is None else total + term
        total = jnp.sum(total, axis=1, keepdims=True)
        if others is not None:
            total = total + jnp.exp2(others[at, :] - top)
        found_of(at, top + jnp.log2(total))


def column_sweep(score_of, blocks, rows, row_pot, found_of):
    folds = (CHUNK // SUBLANES, SUBLANES, LANES)
    found = [[] for _ in blocks]
    for at in chunks_of(rows):
        addend = row_pot[at, :]
        for p in blocks:
            score = (score_of(at, p) + addend).reshape(folds)
            top = jnp.max(score, axis=0)
            found[p].append((top, jnp.sum(jnp.exp2(score - top[None]), axis=0)))
    for p in blocks:
        top = functools.reduce(jnp.maximum, [each for each, _ in found[p]])
        top = jnp.max(top, axis=0, keepdims=True)
        total = sum(each * jnp.exp2(at_top - top) for at_top, each in found[p])
        found_of(p, top + jnp.log2(jnp.sum(total, axis=0, keepdims=True)))


def products(source, targets, factor, smalls, scaled, table):
    for p, small in enumerate(smalls):
        table[0, p : p + 1, :] = small[1:2] * LOG2E
        table[1, p : p + 1, :] = small[0:1] * (inverse_eps * LOG2E)
    for p in range(0, len(smalls), 2):
        end = min(p + 2, len(smalls))
        lanes = slice(p * LANES, end * LANES)
        product = lax.dot_general(
            source[...], targets[lanes, :], (((1,), (1,)), ((), ())),
            preferred_element_type=jnp.float32,
        )
        shift = jnp.concatenate([table[1, q : q + 1, :] for q in range(p, end)], axis=1)
        scaled[:, lanes] = product * factor + shift


def head_kernel(
    own, init, target_logw, first, second, whole, small, first_plain, second_plain, init_row,
    logw_row, sems,
):
    rows, half = own.shape[0], first_plain.shape[0]
    copies = [
        pltpu.make_async_copy(own, whole.at[0:rows], sems.at[0]),
        pltpu.make_async_copy(init, init_row, sems.at[1]),
        pltpu.make_async_copy(target_logw, logw_row, sems.at[2]),
    ]
    for copy in copies:
        copy.start()
    for copy in copies:
        copy.wait()
    for out in (first, first_plain):
        out[0:half, :] = whole[0:half, :]
    for out in (second, second_plain):
        out[0:half, :] = whole[half:rows, :]
    small[0:1, :] = init_row[...]
    small[1:2, :] = logw_row[...]
    filler = jnp.zeros((SPARE - 2, LANES), jnp.float32)
    rest = jnp.concatenate([init_row[...], logw_row[...], filler], axis=0)
    for k in range(whole.shape[1] // LANES):
        lanes = slice(k * LANES, (k + 1) * LANES)
        part = (rest if k < 3 else jnp.zeros_like(rest)).astype(whole.dtype)
        first[half:, lanes] = part
        second[half:, lanes] = part
        whole[rows:, lanes] = part
        rest = rest - part.astype(jnp.float32)


def source_kernel(source, logw, whole, held, row_logw, passed, rows_row, sems):
    copies = [
        pltpu.make_async_copy(source, held, sems.at[0]),
        pltpu.make_async_copy(logw, rows_row, sems.at[1]),
    ]
    for copy in copies:
        copy.start()
    passed[...] = whole[...]
    for copy in copies:
        copy.wait()
    row_logw[...] = jnp.broadcast_to(as_column(rows_row[...] * LOG2E), row_logw.shape)


def sibling_kernel(whole, a_first, a_second, b_first, b_second, out):
    half = a_second.shape[0]
    block = 2 * half + SPARE
    out[0:block, :] = whole[...]
    out[block : block + half, :] = a_first[0:half, :]
    out[block + half : block + 2 * half, :] = a_second[...]
    out[block + 2 * half : 2 * block, :] = a_first[half:, :]
    out[2 * block : 2 * block + half, :] = b_first[...]
    out[2 * block + half : 3 * block, :] = b_second[...]


def unpack(message, end=None):
    end = message.shape[0] if end is None else end
    parts = [
        message[end - SPARE : end, k * LANES : (k + 1) * LANES].astype(jnp.float32)[0:2]
        for k in range(3)
    ]
    return (parts[0] + parts[1]) + parts[2]


def own_kernel(
    factor, source, whole, a_first, a_second, b_first, b_second, scaled, table, targets
):
    half = a_second.shape[0]
    pieces = (whole, whole, a_first, a_second, b_first, b_second)
    targets[0 : 2 * half, :] = whole[0 : 2 * half, :]
    for k in range(2, 6):
        targets[k * half : (k + 1) * half, :] = pieces[k][0:half, :]
    smalls = [unpack(whole), unpack(a_first), unpack(b_second)]
    products(source, targets, factor, smalls, scaled, table)


def sibling_scores_kernel(factor, source, sibling, own, scaled, table, found, targets):
    width = targets.shape[0] // 3
    block = width + SPARE
    smalls = []
    for k in range(3):
        targets[k * width : (k + 1) * width, :] = sibling[k * block : k * block + width, :]
        smalls.append(unpack(sibling, (k + 1) * block))
    products(source, targets, factor, smalls, scaled, table)

    def score_of(at, p):
        part = (own, scaled)[p % 2]
        return part[at, p // 2 * LANES : (p // 2 + 1) * LANES]

    def found_of(at, value):
        found[at, :] = jnp.broadcast_to(value, (CHUNK, LANES))

    row_sweep(score_of, range(6), scaled.shape[0], found_of)


def pass_kernel(message, tie, out):
    out[...] = message[...]


def far_kernel(
    factor, source, far_a, far_b, sibling_a, sibling_b, near, scaled, table, targets
):
    half = targets.shape[0] // 4
    for k, piece in enumerate((far_a, far_b, sibling_a, sibling_b)):
        targets[k * half : (k + 1) * half, :] = piece[0:half, :]
    smalls = [unpack(far_a), unpack(sibling_a)]
    products(source, targets, factor, smalls, scaled, table)


def neighbour_step(me, turn):
    step = 2 + 2 * (me % 2)
    return step if turn == 0 else 6 - step


def positions(me):
    sibling = me ^ 1
    own = [me, me ^ neighbour_step(me, 0), me ^ neighbour_step(me, 1), me ^ 6]
    other = [
        sibling,
        sibling ^ neighbour_step(sibling, 0),
        sibling ^ neighbour_step(sibling, 1),
        sibling ^ 6,
    ]
    return [block for pair in zip(own, other) for block in pair]


class Held:

    def __init__(self, own, own_table, sibling, sibling_table, far, far_table):
        self.near = own.shape[1] // LANES * 2
        self.total = self.near + far.shape[1] // LANES
        self.scores, self.tables = (own, sibling, far), (own_table, sibling_table, far_table)

    def place(self, p):
        return (p % 2, p // 2) if p < self.near else (2, p - self.near)

    def score(self, at, p):
        part, k = self.place(p)
        return self.scores[part][at, k * LANES : (k + 1) * LANES]

    def row(self, kind, p):
        part, k = self.place(p)
        return self.tables[part][kind, k : k + 1, :]


def first_kernel(
    own, own_table, sibling, sibling_table, far, far_table, found, logw, message, row_pot, ordered
):
    order = positions(lax.axis_index("blk"))
    held = Held(own, own_table, sibling, sibling_table, far, far_table)
    rows = own.shape[0]

    def row_found(at, value):
        row_pot[at, :] = logw[at, :] - value

    def column_found(p, value):
        ordered[pl.ds(order[p], 1), :] = value - held.row(1, p)

    row_sweep(held.score, range(held.near, held.total), rows, row_found, others=found)
    column_sweep(held.score, range(held.total), rows, row_pot, column_found)
    message[...] = jnp.broadcast_to(ordered[...][None], message.shape)


def second_kernel(
    copies, own, own_table, sibling, sibling_table, far, far_table, got, logw, row, message,
    row_pot, ordered,
):
    order = positions(lax.axis_index("blk"))
    held = Held(own, own_table, sibling, sibling_table, far, far_table)
    rows = own.shape[0]
    values = got[...]
    top = jnp.max(values, axis=0)
    ordered[...] = top + jnp.log2(jnp.sum(jnp.exp2(values - top[None]), axis=0))
    columns = []
    for p in range(held.total):
        columns.append(held.row(0, p) - ordered[pl.ds(order[p], 1), :] - held.row(1, p))

    def row_found(at, value):
        row_pot[at, :] = logw[at, :] - value

    def column_found(p, value):
        at = pl.ds((held.total - 1 - order[p]) * copies, copies)
        message[at, :] = jnp.broadcast_to(value - held.row(1, p), (copies, LANES))

    row_sweep(held.score, range(held.total), rows, row_found, columns=columns)
    column_sweep(held.score, range(held.total), rows, row_pot, column_found)
    row[...] = as_row(row_pot[:, 0:1]) * (epsilon * LN2)


def last_kernel(got, small, row, row_out, column_out):
    values = got[...]
    top = jnp.max(values, axis=0, keepdims=True)
    total = top + jnp.log2(jnp.sum(jnp.exp2(values - top), axis=0, keepdims=True))
    column_out[...] = epsilon * small[1:2, :] - (epsilon * LN2) * total
    row_out[...] = row[...]


def lse(values):
    top = jnp.max(values, axis=0)
    return top + jnp.log(jnp.sum(jnp.exp(values - top[None]), axis=0))


def solution(mesh):
    blk, grp = mesh.shape["blk"], mesh.shape["grp"]
    chips = blk // 2
    everyone = ("chip", "core", "grp")

    def shards_square(source_embed, target_embed, target_init, source_logw, target_logw):
        rows, depth = source_embed.shape
        width = target_embed.shape[0]
        half = width // 2
        factor = inverse_eps * LOG2E / math.sqrt(depth)
        vmem, hbm = pl.BlockSpec(memory_space=pltpu.VMEM), pl.BlockSpec(memory_space=pltpu.HBM)
        params = pltpu.CompilerParams(vmem_limit_bytes=16 * 1024 * 1024)

        def values(*shape):
            return jax.ShapeDtypeStruct(shape, jnp.float32)

        def cost(targets, sweeps):
            return pl.CostEstimate(
                flops=2 * rows * targets * depth + 16 * sweeps * rows * blk * width,
                transcendentals=2 * sweeps * rows * blk * width,
                bytes_accessed=2 * (rows + targets) * depth,
            )

        def along(array, turn):
            return lax.ppermute(
                array, "blk", [(i ^ neighbour_step(i, turn), i) for i in range(blk)]
            )

        def to_sibling(array):
            return fetch(array, "blk", 1, blk)

        def exchange(message):
            order = list(range(blk * grp))[::-1]
            flat = message.reshape(blk * grp, 1, -1)
            got = lax.all_to_all(flat, ("blk", "grp"), 0, 0, axis_index_groups=[order])
            return got.reshape(message.shape)

        def block_of(size):
            return jax.ShapeDtypeStruct((size, depth), target_embed.dtype)

        def in_hbm(*arrays):
            return [pltpu.with_memory_space_constraint(each, pltpu.HBM) for each in arrays]

        first, second, whole, small, first_plain, second_plain = pl.pallas_call(
            head_kernel,
            out_shape=(
                block_of(half + SPARE),
                block_of(half + SPARE),
                block_of(width + SPARE),
                values(2, width),
                block_of(half),
                block_of(half),
            ),
            in_specs=[hbm] * 3,
            out_specs=(vmem,) * 6,
            scratch_shapes=[
                pltpu.VMEM((1, width), jnp.float32),
                pltpu.VMEM((1, width), jnp.float32),
                pltpu.SemaphoreType.DMA((3,)),
            ],
            compiler_params=params,
        )(*in_hbm(target_embed, target_init.reshape(1, width), target_logw.reshape(1, width)))
        a_first = along(first, 0)
        b_second = along(second, 1)
        a_second = along(second_plain, 0)
        b_first = along(first_plain, 1)
        far_a = along(a_first, 1)
        far_b = along(b_second[:half], 0)
        source, logw, passed = pl.pallas_call(
            source_kernel,
            out_shape=(
                jax.ShapeDtypeStruct((rows, depth), source_embed.dtype),
                values(rows, LANES),
                block_of(width + SPARE),
            ),
            in_specs=[hbm] * 2 + [vmem],
            out_specs=(vmem,) * 3,
            scratch_shapes=[pltpu.VMEM((1, rows), jnp.float32), pltpu.SemaphoreType.DMA((2,))],
            compiler_params=params,
        )(*in_hbm(source_embed, source_logw.reshape(1, rows)), whole)
        near = (a_first, a_second, b_first, b_second)
        sibling = pl.pallas_call(
            sibling_kernel,
            out_shape=block_of(3 * (width + SPARE)),
            in_specs=[vmem] * 5,
            out_specs=vmem,
            compiler_params=params,
            cost_estimate=cost(0, 0),
        )(passed, *near)
        sibling = to_sibling(sibling)

        def table():
            return values(2, SUBLANES, width)

        def scores_of(kernel, blocks, pieces, extra=()):
            return pl.pallas_call(
                functools.partial(kernel, factor),
                out_shape=(values(rows, blocks * width), table(), *extra),
                in_specs=[vmem] * (1 + len(pieces)),
                out_specs=(vmem,) * (2 + len(extra)),
                scratch_shapes=[pltpu.VMEM((blocks * width, depth), target_embed.dtype)],
                compiler_params=params,
                cost_estimate=cost(0, 0),
            )(source, *pieces)

        own = scores_of(own_kernel, 3, (whole, *near))

        def passed_on(message, tie, weight):
            return pl.pallas_call(
                pass_kernel,
                out_shape=jax.ShapeDtypeStruct(message.shape, message.dtype),
                in_specs=[vmem] * 2,
                out_specs=vmem,
                compiler_params=params,
                cost_estimate=cost(weight * width, 0),
            )(message, tie)

        sibling_a = to_sibling(passed_on(far_a, own[1], 0))
        sibling_b = to_sibling(passed_on(far_b, own[1], 50))
        *other, found = scores_of(
            sibling_scores_kernel, 3, (sibling, own[0]), (values(rows, LANES),)
        )
        far = scores_of(far_kernel, 2, (far_a, far_b, sibling_a, sibling_b, other[0]))
        scores = (*own, *other, *far)
        row_scratch = pltpu.VMEM((rows, LANES), jnp.float32)
        block_scratch = pltpu.VMEM((blk, width), jnp.float32)
        message = pl.pallas_call(
            first_kernel,
            out_shape=values(blk * grp, blk, width),
            in_specs=[vmem] * 8,
            out_specs=vmem,
            scratch_shapes=[row_scratch, block_scratch],
            compiler_params=params,
            cost_estimate=cost(0, 1),
        )(*scores, found, logw)
        got = exchange(message)
        row, message = pl.pallas_call(
            functools.partial(second_kernel, grp),
            out_shape=(values(1, rows), values(blk * grp, width)),
            in_specs=[vmem] * 8,
            out_specs=(vmem, vmem),
            scratch_shapes=[row_scratch, block_scratch],
            compiler_params=params,
            cost_estimate=cost(0, 1),
        )(*scores, got, logw)
        got = exchange(message)
        row_pot, column_pot = pl.pallas_call(
            last_kernel,
            out_shape=(values(1, rows), values(1, width)),
            in_specs=[vmem] * 3,
            out_specs=(vmem, vmem),
            compiler_params=params,
        )(got, small, row)
        return row_pot.reshape(rows), column_pot.reshape(width)

    def shards_any(source_embed, target_embed, target_init, source_logw, target_logw):
        width, depth = target_embed.shape
        factor = -1.0 / math.sqrt(depth)
        me = lax.axis_index("chip") * 2 + lax.axis_index("core")

        def swap_order(values):
            parts = values.reshape(blk, width)
            step = 1
            while step < blk:
                pairs = parts.reshape(blk // (2 * step), 2, step, width)
                pairs = jnp.where(me & step, pairs[:, ::-1], pairs)
                parts = pairs.reshape(blk, width)
                step *= 2
            return parts

        small = jnp.stack([target_init, target_logw])
        targets, smalls = gather_any(target_embed, small, chips)
        cost = (
            lax.dot_general(
                source_embed, targets, (((1,), (1,)), ((), ())), preferred_element_type=jnp.float32
            )
            * factor
        )
        column_pot, logw_all = smalls[:, 0].reshape(-1), smalls[:, 1].reshape(-1)
        for iteration in range(ITERS):
            scores = (column_pot[None, :] - cost) * inverse_eps
            row_top = jnp.max(scores, axis=1)
            row_sum = jnp.sum(jnp.exp(scores - row_top[:, None]), axis=1)
            row_pot = epsilon * source_logw - epsilon * (row_top + jnp.log(row_sum))
            part = swap_order(lse((row_pot[:, None] - cost) * inverse_eps))
            if iteration < ITERS - 1:
                copies = jnp.broadcast_to(part[None], (blk * grp, blk, width))
                got = lax.all_to_all(copies, everyone, 0, 0)
                total = swap_order(lse(got)).reshape(-1)
                column_pot = epsilon * logw_all - epsilon * total
            else:
                copies = jnp.broadcast_to(part[:, None], (blk, grp, width)).reshape(blk * grp, width)
                got = lax.all_to_all(copies, everyone, 0, 0)
                own_column = epsilon * target_logw - epsilon * lse(got)
        return row_pot, own_column

    if chips == 4:
        shards = shards_square
        rows_spec, blk_spec = P(("blk", "grp")), P("blk")
    else:
        shards = shards_any
        rows_spec, blk_spec = P(everyone), P(("chip", "core"))
        mesh = Mesh(mesh.devices.reshape(chips, 2, grp), everyone)
    in_specs = (rows_spec, blk_spec, blk_spec, rows_spec, blk_spec)
    out_specs = (rows_spec, blk_spec)
    return jax.shard_map(shards, mesh=mesh, in_specs=in_specs, out_specs=out_specs, check_vma=False)
```

```python
import functools
import math

import jax
import jax.numpy as jnp
from jax import lax
from jax.experimental import pallas as pl
from jax.experimental.pallas import tpu as pltpu
from jax.sharding import Mesh, PartitionSpec as P

ITERS = 2
epsilon = 0.1
inverse_eps = 10.0
LOG2E = math.log2(math.e)
LN2 = math.log(2.0)
LANES = 128
SPARE = 8
SUBLANES = 8


def fetch(array, axis, step, size):
    return lax.ppermute(array, axis, [(i ^ step, i) for i in range(size)])


def doubled(held, step, chips):
    return jnp.concatenate([held, fetch(held, "chip", step, chips)])


def gather_any(array, small, chips):
    pair = jnp.stack([array, fetch(array, "core", 1, 2)])[None]
    smalls = jnp.stack([small, fetch(small, "core", 1, 2)])[None]
    step = 1
    while step < chips:
        pair = doubled(pair, step, chips)
        smalls = doubled(smalls, step, chips)
        step *= 2
    return pair.reshape(-1, array.shape[1]), smalls.reshape(-1, *small.shape)


def as_column(row):
    size = row.shape[1]
    here = lax.broadcasted_iota(jnp.int32, (LANES, LANES), 0)
    there = lax.broadcasted_iota(jnp.int32, (LANES, LANES), 1)
    parts = []
    for start in range(0, size, LANES):
        wide = jnp.broadcast_to(row[:, start : start + LANES], (LANES, LANES))
        parts.append(jnp.sum(jnp.where(here == there, wide, 0.0), axis=1, keepdims=True))
    return jnp.concatenate(parts, axis=0)


def as_row(column):
    size = column.shape[0]
    here = lax.broadcasted_iota(jnp.int32, (LANES, LANES), 0)
    there = lax.broadcasted_iota(jnp.int32, (LANES, LANES), 1)
    parts = []
    for start in range(0, size, LANES):
        wide = jnp.broadcast_to(column[start : start + LANES], (LANES, LANES))
        parts.append(jnp.sum(jnp.where(here == there, wide, 0.0), axis=0, keepdims=True))
    return jnp.concatenate(parts, axis=1)


CHUNK = 64


def chunks_of(rows):
    return [pl.ds(start, CHUNK) for start in range(0, rows, CHUNK)]


def row_sweep(score_of, blocks, rows, found_of, columns=None, others=None):
    tops = []
    for at in chunks_of(rows):
        top = None if others is None else others[at, :]
        for p in blocks:
            score = score_of(at, p)
            score = score if columns is None else score + columns[p]
            top = score if top is None else jnp.maximum(top, score)
        tops.append(jnp.max(top, axis=1, keepdims=True))
    for at, top in zip(chunks_of(rows), tops):
        total = None
        for p in blocks:
            shift = -top if columns is None else columns[p] - top
            term = jnp.exp2(score_of(at, p) + shift)
            total = term if total is None else total + term
        total = jnp.sum(total, axis=1, keepdims=True)
        if others is not None:
            total = total + jnp.exp2(others[at, :] - top)
        found_of(at, top + jnp.log2(total))


def column_sweep(score_of, blocks, rows, row_pot, found_of):
    folds = (CHUNK // SUBLANES, SUBLANES, LANES)
    found = [[] for _ in blocks]
    for at in chunks_of(rows):
        addend = row_pot[at, :]
        for p in blocks:
            score = (score_of(at, p) + addend).reshape(folds)
            top = jnp.max(score, axis=0)
            found[p].append((top, jnp.sum(jnp.exp2(score - top[None]), axis=0)))
    for p in blocks:
        top = functools.reduce(jnp.maximum, [each for each, _ in found[p]])
        top = jnp.max(top, axis=0, keepdims=True)
        total = sum(each * jnp.exp2(at_top - top) for at_top, each in found[p])
        found_of(p, top + jnp.log2(jnp.sum(total, axis=0, keepdims=True)))


def products(source, targets, factor, smalls, scaled, table):
    for p, small in enumerate(smalls):
        table[0, p : p + 1, :] = small[1:2] * LOG2E
        table[1, p : p + 1, :] = small[0:1] * (inverse_eps * LOG2E)
    for p in range(0, len(smalls), 2):
        end = min(p + 2, len(smalls))
        lanes = slice(p * LANES, end * LANES)
        product = lax.dot_general(
            source[...], targets[lanes, :], (((1,), (1,)), ((), ())),
            preferred_element_type=jnp.float32,
        )
        shift = jnp.concatenate([table[1, q : q + 1, :] for q in range(p, end)], axis=1)
        scaled[:, lanes] = product * factor + shift


def head_kernel(
    own, init, target_logw, first, second, whole, small, first_plain, second_plain, init_row,
    logw_row, sems,
):
    rows, half = own.shape[0], first_plain.shape[0]
    vectors = [
        pltpu.make_async_copy(init, init_row, sems.at[0]),
        pltpu.make_async_copy(target_logw, logw_row, sems.at[1]),
    ]
    upper, lower = own.at[0:half], own.at[half:rows]
    blocks = [
        pltpu.make_async_copy(upper, first.at[0:half], sems.at[2]),
        pltpu.make_async_copy(lower, second.at[0:half], sems.at[3]),
        pltpu.make_async_copy(upper, first_plain, sems.at[4]),
        pltpu.make_async_copy(lower, second_plain, sems.at[5]),
        pltpu.make_async_copy(own, whole.at[0:rows], sems.at[6]),
    ]
    for copy in vectors + blocks:
        copy.start()
    for copy in vectors:
        copy.wait()
    small[0:1, :] = init_row[...]
    small[1:2, :] = logw_row[...]
    filler = jnp.zeros((SPARE - 2, LANES), jnp.float32)
    rest = jnp.concatenate([init_row[...], logw_row[...], filler], axis=0)
    for k in range(whole.shape[1] // LANES):
        lanes = slice(k * LANES, (k + 1) * LANES)
        part = (rest if k < 3 else jnp.zeros_like(rest)).astype(whole.dtype)
        first[half:, lanes] = part
        second[half:, lanes] = part
        whole[rows:, lanes] = part
        rest = rest - part.astype(jnp.float32)
    for copy in blocks:
        copy.wait()


def source_kernel(source, logw, whole, held, row_logw, passed, rows_row, sems):
    copies = [
        pltpu.make_async_copy(source, held, sems.at[0]),
        pltpu.make_async_copy(logw, rows_row, sems.at[1]),
    ]
    for copy in copies:
        copy.start()
    passed[...] = whole[...]
    for copy in copies:
        copy.wait()
    row_logw[...] = jnp.broadcast_to(as_column(rows_row[...] * LOG2E), row_logw.shape)


def sibling_kernel(whole, a_first, a_second, b_first, b_second, out):
    half = a_second.shape[0]
    block = 2 * half + SPARE
    out[0:block, :] = whole[...]
    out[block : block + half, :] = a_first[0:half, :]
    out[block + half : block + 2 * half, :] = a_second[...]
    out[block + 2 * half : 2 * block, :] = a_first[half:, :]
    out[2 * block : 2 * block + half, :] = b_first[...]
    out[2 * block + half : 3 * block, :] = b_second[...]


def unpack(message, end=None):
    end = message.shape[0] if end is None else end
    parts = [
        message[end - SPARE : end, k * LANES : (k + 1) * LANES].astype(jnp.float32)[0:2]
        for k in range(3)
    ]
    return (parts[0] + parts[1]) + parts[2]


def own_kernel(
    factor, source, whole, a_first, a_second, b_first, b_second, scaled, table, targets
):
    half = a_second.shape[0]
    pieces = (whole, whole, a_first, a_second, b_first, b_second)
    targets[0 : 2 * half, :] = whole[0 : 2 * half, :]
    for k in range(2, 6):
        targets[k * half : (k + 1) * half, :] = pieces[k][0:half, :]
    smalls = [unpack(whole), unpack(a_first), unpack(b_second)]
    products(source, targets, factor, smalls, scaled, table)


def sibling_scores_kernel(factor, source, sibling, own, scaled, table, found, targets):
    width = targets.shape[0] // 3
    block = width + SPARE
    smalls = []
    for k in range(3):
        targets[k * width : (k + 1) * width, :] = sibling[k * block : k * block + width, :]
        smalls.append(unpack(sibling, (k + 1) * block))
    products(source, targets, factor, smalls, scaled, table)

    def score_of(at, p):
        part = (own, scaled)[p % 2]
        return part[at, p // 2 * LANES : (p // 2 + 1) * LANES]

    def found_of(at, value):
        found[at, :] = jnp.broadcast_to(value, (CHUNK, LANES))

    row_sweep(score_of, range(6), scaled.shape[0], found_of)


def pass_kernel(message, tie, out):
    out[...] = message[...]


def far_kernel(
    factor, source, far_a, far_b, sibling_a, sibling_b, near, scaled, table, targets
):
    half = targets.shape[0] // 4
    for k, piece in enumerate((far_a, far_b, sibling_a, sibling_b)):
        targets[k * half : (k + 1) * half, :] = piece[0:half, :]
    smalls = [unpack(far_a), unpack(sibling_a)]
    products(source, targets, factor, smalls, scaled, table)


def neighbour_step(me, turn):
    step = 2 + 2 * (me % 2)
    return step if turn == 0 else 6 - step


def positions(me):
    sibling = me ^ 1
    own = [me, me ^ neighbour_step(me, 0), me ^ neighbour_step(me, 1), me ^ 6]
    other = [
        sibling,
        sibling ^ neighbour_step(sibling, 0),
        sibling ^ neighbour_step(sibling, 1),
        sibling ^ 6,
    ]
    return [block for pair in zip(own, other) for block in pair]


class Held:

    def __init__(self, own, own_table, sibling, sibling_table, far, far_table):
        self.near = own.shape[1] // LANES * 2
        self.total = self.near + far.shape[1] // LANES
        self.scores, self.tables = (own, sibling, far), (own_table, sibling_table, far_table)

    def place(self, p):
        return (p % 2, p // 2) if p < self.near else (2, p - self.near)

    def score(self, at, p):
        part, k = self.place(p)
        return self.scores[part][at, k * LANES : (k + 1) * LANES]

    def row(self, kind, p):
        part, k = self.place(p)
        return self.tables[part][kind, k : k + 1, :]


def first_kernel(
    own, own_table, sibling, sibling_table, far, far_table, found, logw, message, row_pot, ordered
):
    order = positions(lax.axis_index("blk"))
    held = Held(own, own_table, sibling, sibling_table, far, far_table)
    rows = own.shape[0]

    def row_found(at, value):
        row_pot[at, :] = logw[at, :] - value

    def column_found(p, value):
        ordered[pl.ds(order[p], 1), :] = value - held.row(1, p)

    row_sweep(held.score, range(held.near, held.total), rows, row_found, others=found)
    column_sweep(held.score, range(held.total), rows, row_pot, column_found)
    message[...] = jnp.broadcast_to(ordered[...][None], message.shape)


def second_kernel(
    copies, own, own_table, sibling, sibling_table, far, far_table, got, logw, row, message,
    row_pot, ordered,
):
    order = positions(lax.axis_index("blk"))
    held = Held(own, own_table, sibling, sibling_table, far, far_table)
    rows = own.shape[0]
    values = got[...]
    top = jnp.max(values, axis=0)
    ordered[...] = top + jnp.log2(jnp.sum(jnp.exp2(values - top[None]), axis=0))
    columns = []
    for p in range(held.total):
        columns.append(held.row(0, p) - ordered[pl.ds(order[p], 1), :] - held.row(1, p))

    def row_found(at, value):
        row_pot[at, :] = logw[at, :] - value

    def column_found(p, value):
        at = pl.ds((held.total - 1 - order[p]) * copies, copies)
        message[at, :] = jnp.broadcast_to(value - held.row(1, p), (copies, LANES))

    row_sweep(held.score, range(held.total), rows, row_found, columns=columns)
    column_sweep(held.score, range(held.total), rows, row_pot, column_found)
    row[...] = as_row(row_pot[:, 0:1]) * (epsilon * LN2)


def last_kernel(got, small, row, row_out, column_out):
    values = got[...]
    top = jnp.max(values, axis=0, keepdims=True)
    total = top + jnp.log2(jnp.sum(jnp.exp2(values - top), axis=0, keepdims=True))
    column_out[...] = epsilon * small[1:2, :] - (epsilon * LN2) * total
    row_out[...] = row[...]


def lse(values):
    top = jnp.max(values, axis=0)
    return top + jnp.log(jnp.sum(jnp.exp(values - top[None]), axis=0))


def solution(mesh):
    blk, grp = mesh.shape["blk"], mesh.shape["grp"]
    chips = blk // 2
    everyone = ("chip", "core", "grp")

    def shards_square(source_embed, target_embed, target_init, source_logw, target_logw):
        rows, depth = source_embed.shape
        width = target_embed.shape[0]
        half = width // 2
        factor = inverse_eps * LOG2E / math.sqrt(depth)
        vmem, hbm = pl.BlockSpec(memory_space=pltpu.VMEM), pl.BlockSpec(memory_space=pltpu.HBM)
        params = pltpu.CompilerParams(vmem_limit_bytes=16 * 1024 * 1024)

        def values(*shape):
            return jax.ShapeDtypeStruct(shape, jnp.float32)

        def cost(targets, sweeps):
            return pl.CostEstimate(
                flops=2 * rows * targets * depth + 16 * sweeps * rows * blk * width,
                transcendentals=2 * sweeps * rows * blk * width,
                bytes_accessed=2 * (rows + targets) * depth,
            )

        def along(array, turn):
            return lax.ppermute(
                array, "blk", [(i ^ neighbour_step(i, turn), i) for i in range(blk)]
            )

        def to_sibling(array):
            return fetch(array, "blk", 1, blk)

        def exchange(message):
            order = list(range(blk * grp))[::-1]
            return lax.all_to_all(message, ("blk", "grp"), 0, 0, axis_index_groups=[order])

        def block_of(size):
            return jax.ShapeDtypeStruct((size, depth), target_embed.dtype)

        def in_hbm(*arrays):
            return [pltpu.with_memory_space_constraint(each, pltpu.HBM) for each in arrays]

        first, second, whole, small, first_plain, second_plain = pl.pallas_call(
            head_kernel,
            out_shape=(
                block_of(half + SPARE),
                block_of(half + SPARE),
                block_of(width + SPARE),
                values(2, width),
                block_of(half),
                block_of(half),
            ),
            in_specs=[hbm] * 3,
            out_specs=(vmem,) * 6,
            scratch_shapes=[
                pltpu.VMEM((1, width), jnp.float32),
                pltpu.VMEM((1, width), jnp.float32),
                pltpu.SemaphoreType.DMA((7,)),
            ],
            compiler_params=params,
        )(*in_hbm(target_embed, target_init.reshape(1, width), target_logw.reshape(1, width)))
        a_first = along(first, 0)
        b_second = along(second, 1)
        a_second = along(second_plain, 0)
        b_first = along(first_plain, 1)
        far_a = along(a_first, 1)
        far_b = along(b_second[:half], 0)
        source, logw, passed = pl.pallas_call(
            source_kernel,
            out_shape=(
                jax.ShapeDtypeStruct((rows, depth), source_embed.dtype),
                values(rows, LANES),
                block_of(width + SPARE),
            ),
            in_specs=[hbm] * 2 + [vmem],
            out_specs=(vmem,) * 3,
            scratch_shapes=[pltpu.VMEM((1, rows), jnp.float32), pltpu.SemaphoreType.DMA((2,))],
            compiler_params=params,
        )(*in_hbm(source_embed, source_logw.reshape(1, rows)), whole)
        near = (a_first, a_second, b_first, b_second)
        sibling = pl.pallas_call(
            sibling_kernel,
            out_shape=block_of(3 * (width + SPARE)),
            in_specs=[vmem] * 5,
            out_specs=vmem,
            compiler_params=params,
            cost_estimate=cost(0, 0),
        )(passed, *near)
        sibling = to_sibling(sibling)

        def table():
            return values(2, SUBLANES, width)

        def scores_of(kernel, blocks, pieces, extra=()):
            return pl.pallas_call(
                functools.partial(kernel, factor),
                out_shape=(values(rows, blocks * width), table(), *extra),
                in_specs=[vmem] * (1 + len(pieces)),
                out_specs=(vmem,) * (2 + len(extra)),
                scratch_shapes=[pltpu.VMEM((blocks * width, depth), target_embed.dtype)],
                compiler_params=params,
                cost_estimate=cost(0, 0),
            )(source, *pieces)

        own = scores_of(own_kernel, 3, (whole, *near))

        def passed_on(message, tie, weight):
            return pl.pallas_call(
                pass_kernel,
                out_shape=jax.ShapeDtypeStruct(message.shape, message.dtype),
                in_specs=[vmem] * 2,
                out_specs=vmem,
                compiler_params=params,
                cost_estimate=cost(weight * width, 0),
            )(message, tie)

        sibling_a = to_sibling(passed_on(far_a, own[1], 0))
        sibling_b = to_sibling(passed_on(far_b, own[1], 50))
        *other, found = scores_of(
            sibling_scores_kernel, 3, (sibling, own[0]), (values(rows, LANES),)
        )
        far = scores_of(far_kernel, 2, (far_a, far_b, sibling_a, sibling_b, other[0]))
        scores = (*own, *other, *far)
        row_scratch = pltpu.VMEM((rows, LANES), jnp.float32)
        block_scratch = pltpu.VMEM((blk, width), jnp.float32)
        message = pl.pallas_call(
            first_kernel,
            out_shape=values(blk * grp, blk, width),
            in_specs=[vmem] * 8,
            out_specs=vmem,
            scratch_shapes=[row_scratch, block_scratch],
            compiler_params=params,
            cost_estimate=cost(0, 1),
        )(*scores, found, logw)
        got = exchange(message)
        row, message = pl.pallas_call(
            functools.partial(second_kernel, grp),
            out_shape=(values(1, rows), values(blk * grp, width)),
            in_specs=[vmem] * 8,
            out_specs=(vmem, vmem),
            scratch_shapes=[row_scratch, block_scratch],
            compiler_params=params,
            cost_estimate=cost(0, 1),
        )(*scores, got, logw)
        got = exchange(message)
        row_pot, column_pot = pl.pallas_call(
            last_kernel,
            out_shape=(values(1, rows), values(1, width)),
            in_specs=[vmem] * 3,
            out_specs=(vmem, vmem),
            compiler_params=params,
        )(got, small, row)
        return row_pot.reshape(rows), column_pot.reshape(width)

    def shards_any(source_embed, target_embed, target_init, source_logw, target_logw):
        width, depth = target_embed.shape
        factor = -1.0 / math.sqrt(depth)
        me = lax.axis_index("chip") * 2 + lax.axis_index("core")

        def swap_order(values):
            parts = values.reshape(blk, width)
            step = 1
            while step < blk:
                pairs = parts.reshape(blk // (2 * step), 2, step, width)
                pairs = jnp.where(me & step, pairs[:, ::-1], pairs)
                parts = pairs.reshape(blk, width)
                step *= 2
            return parts

        small = jnp.stack([target_init, target_logw])
        targets, smalls = gather_any(target_embed, small, chips)
        cost = (
            lax.dot_general(
                source_embed, targets, (((1,), (1,)), ((), ())), preferred_element_type=jnp.float32
            )
            * factor
        )
        column_pot, logw_all = smalls[:, 0].reshape(-1), smalls[:, 1].reshape(-1)
        for iteration in range(ITERS):
            scores = (column_pot[None, :] - cost) * inverse_eps
            row_top = jnp.max(scores, axis=1)
            row_sum = jnp.sum(jnp.exp(scores - row_top[:, None]), axis=1)
            row_pot = epsilon * source_logw - epsilon * (row_top + jnp.log(row_sum))
            part = swap_order(lse((row_pot[:, None] - cost) * inverse_eps))
            if iteration < ITERS - 1:
                copies = jnp.broadcast_to(part[None], (blk * grp, blk, width))
                got = lax.all_to_all(copies, everyone, 0, 0)
                total = swap_order(lse(got)).reshape(-1)
                column_pot = epsilon * logw_all - epsilon * total
            else:
                copies = jnp.broadcast_to(part[:, None], (blk, grp, width)).reshape(blk * grp, width)
                got = lax.all_to_all(copies, everyone, 0, 0)
                own_column = epsilon * target_logw - epsilon * lse(got)
        return row_pot, own_column

    if chips == 4:
        shards = shards_square
        rows_spec, blk_spec = P(("blk", "grp")), P("blk")
    else:
        shards = shards_any
        rows_spec, blk_spec = P(everyone), P(("chip", "core"))
        mesh = Mesh(mesh.devices.reshape(chips, 2, grp), everyone)
    in_specs = (rows_spec, blk_spec, blk_spec, rows_spec, blk_spec)
    out_specs = (rows_spec, blk_spec)
    return jax.shard_map(shards, mesh=mesh, in_specs=in_specs, out_specs=out_specs, check_vma=False)
```

```python
import functools
import math

import jax
import jax.numpy as jnp
from jax import lax
from jax.experimental import pallas as pl
from jax.experimental.pallas import tpu as pltpu
from jax.sharding import Mesh, PartitionSpec as P

ITERS = 2
epsilon = 0.1
inverse_eps = 10.0
LOG2E = math.log2(math.e)
LN2 = math.log(2.0)
LANES = 128
SPARE = 8
SUBLANES = 8


def fetch(array, axis, step, size):
    return lax.ppermute(array, axis, [(i ^ step, i) for i in range(size)])


def doubled(held, step, chips):
    return jnp.concatenate([held, fetch(held, "chip", step, chips)])


def gather_any(array, small, chips):
    pair = jnp.stack([array, fetch(array, "core", 1, 2)])[None]
    smalls = jnp.stack([small, fetch(small, "core", 1, 2)])[None]
    step = 1
    while step < chips:
        pair = doubled(pair, step, chips)
        smalls = doubled(smalls, step, chips)
        step *= 2
    return pair.reshape(-1, array.shape[1]), smalls.reshape(-1, *small.shape)


def as_column(row):
    size = row.shape[1]
    here = lax.broadcasted_iota(jnp.int32, (LANES, LANES), 0)
    there = lax.broadcasted_iota(jnp.int32, (LANES, LANES), 1)
    parts = []
    for start in range(0, size, LANES):
        wide = jnp.broadcast_to(row[:, start : start + LANES], (LANES, LANES))
        parts.append(jnp.sum(jnp.where(here == there, wide, 0.0), axis=1, keepdims=True))
    return jnp.concatenate(parts, axis=0)


def as_row(column):
    size = column.shape[0]
    here = lax.broadcasted_iota(jnp.int32, (LANES, LANES), 0)
    there = lax.broadcasted_iota(jnp.int32, (LANES, LANES), 1)
    parts = []
    for start in range(0, size, LANES):
        wide = jnp.broadcast_to(column[start : start + LANES], (LANES, LANES))
        parts.append(jnp.sum(jnp.where(here == there, wide, 0.0), axis=0, keepdims=True))
    return jnp.concatenate(parts, axis=1)


CHUNK = 64
TALL = 128


def chunks_of(rows, size=CHUNK):
    return [pl.ds(start, size) for start in range(0, rows, size)]


def row_sweep(score_of, blocks, rows, found_of, columns=None, others=None):
    tops = []
    for at in chunks_of(rows):
        top = None if others is None else others[at, :]
        for p in blocks:
            score = score_of(at, p)
            score = score if columns is None else score + columns[p]
            top = score if top is None else jnp.maximum(top, score)
        tops.append(jnp.max(top, axis=1, keepdims=True))
    for at, top in zip(chunks_of(rows), tops):
        total = None
        for p in blocks:
            shift = -top if columns is None else columns[p] - top
            term = jnp.exp2(score_of(at, p) + shift)
            total = term if total is None else total + term
        total = jnp.sum(total, axis=1, keepdims=True)
        if others is not None:
            total = total + jnp.exp2(others[at, :] - top)
        found_of(at, top + jnp.log2(total))


def column_sweep(score_of, blocks, rows, row_pot, found_of):
    folds = (TALL // SUBLANES, SUBLANES, LANES)
    found = [[] for _ in blocks]
    for at in chunks_of(rows, TALL):
        addend = row_pot[at, :]
        for p in blocks:
            score = (score_of(at, p) + addend).reshape(folds)
            top = jnp.max(score, axis=0)
            found[p].append((top, jnp.sum(jnp.exp2(score - top[None]), axis=0)))
    for p in blocks:
        top = functools.reduce(jnp.maximum, [each for each, _ in found[p]])
        top = jnp.max(top, axis=0, keepdims=True)
        total = sum(each * jnp.exp2(at_top - top) for at_top, each in found[p])
        found_of(p, top + jnp.log2(jnp.sum(total, axis=0, keepdims=True)))


def products(source, targets, factor, smalls, scaled, table):
    for p, small in enumerate(smalls):
        table[0, p : p + 1, :] = small[1:2] * LOG2E
        table[1, p : p + 1, :] = small[0:1] * (inverse_eps * LOG2E)
    for p in range(0, len(smalls), 2):
        end = min(p + 2, len(smalls))
        lanes = slice(p * LANES, end * LANES)
        product = lax.dot_general(
            source[...], targets[lanes, :], (((1,), (1,)), ((), ())),
            preferred_element_type=jnp.float32,
        )
        shift = jnp.concatenate([table[1, q : q + 1, :] for q in range(p, end)], axis=1)
        scaled[:, lanes] = product * factor + shift


def head_kernel(
    own, init, target_logw, first, second, whole, small, first_plain, second_plain, init_row,
    logw_row, sems,
):
    rows, half = own.shape[0], first_plain.shape[0]
    copies = [
        pltpu.make_async_copy(own, whole.at[0:rows], sems.at[0]),
        pltpu.make_async_copy(init, init_row, sems.at[1]),
        pltpu.make_async_copy(target_logw, logw_row, sems.at[2]),
    ]
    for copy in copies:
        copy.start()
    for copy in copies:
        copy.wait()
    for out in (first, first_plain):
        out[0:half, :] = whole[0:half, :]
    for out in (second, second_plain):
        out[0:half, :] = whole[half:rows, :]
    small[0:1, :] = init_row[...]
    small[1:2, :] = logw_row[...]
    filler = jnp.zeros((SPARE - 2, LANES), jnp.float32)
    rest = jnp.concatenate([init_row[...], logw_row[...], filler], axis=0)
    for k in range(whole.shape[1] // LANES):
        lanes = slice(k * LANES, (k + 1) * LANES)
        part = (rest if k < 3 else jnp.zeros_like(rest)).astype(whole.dtype)
        first[half:, lanes] = part
        second[half:, lanes] = part
        whole[rows:, lanes] = part
        rest = rest - part.astype(jnp.float32)


def source_kernel(source, logw, whole, held, row_logw, passed, rows_row, sems):
    copies = [
        pltpu.make_async_copy(source, held, sems.at[0]),
        pltpu.make_async_copy(logw, rows_row, sems.at[1]),
    ]
    for copy in copies:
        copy.start()
    passed[...] = whole[...]
    for copy in copies:
        copy.wait()
    row_logw[...] = jnp.broadcast_to(as_column(rows_row[...] * LOG2E), row_logw.shape)


def sibling_kernel(whole, a_first, a_second, b_first, b_second, out):
    half = a_second.shape[0]
    block = 2 * half + SPARE
    out[0:block, :] = whole[...]
    out[block : block + half, :] = a_first[0:half, :]
    out[block + half : block + 2 * half, :] = a_second[...]
    out[block + 2 * half : 2 * block, :] = a_first[half:, :]
    out[2 * block : 2 * block + half, :] = b_first[...]
    out[2 * block + half : 3 * block, :] = b_second[...]


def unpack(message, end=None):
    end = message.shape[0] if end is None else end
    parts = [
        message[end - SPARE : end, k * LANES : (k + 1) * LANES].astype(jnp.float32)[0:2]
        for k in range(3)
    ]
    return (parts[0] + parts[1]) + parts[2]


def own_kernel(
    factor, source, whole, a_first, a_second, b_first, b_second, scaled, table, targets
):
    half = a_second.shape[0]
    pieces = (whole, whole, a_first, a_second, b_first, b_second)
    targets[0 : 2 * half, :] = whole[0 : 2 * half, :]
    for k in range(2, 6):
        targets[k * half : (k + 1) * half, :] = pieces[k][0:half, :]
    smalls = [unpack(whole), unpack(a_first), unpack(b_second)]
    products(source, targets, factor, smalls, scaled, table)


def sibling_scores_kernel(factor, source, sibling, own, scaled, table, found, targets):
    width = targets.shape[0] // 3
    block = width + SPARE
    smalls = []
    for k in range(3):
        targets[k * width : (k + 1) * width, :] = sibling[k * block : k * block + width, :]
        smalls.append(unpack(sibling, (k + 1) * block))
    products(source, targets, factor, smalls, scaled, table)

    def score_of(at, p):
        part = (own, scaled)[p % 2]
        return part[at, p // 2 * LANES : (p // 2 + 1) * LANES]

    def found_of(at, value):
        found[at, :] = jnp.broadcast_to(value, (CHUNK, LANES))

    row_sweep(score_of, range(6), scaled.shape[0], found_of)


def pass_kernel(message, tie, out):
    out[...] = message[...]


def far_kernel(
    factor, source, far_a, far_b, sibling_a, sibling_b, near, scaled, table, targets
):
    half = targets.shape[0] // 4
    for k, piece in enumerate((far_a, far_b, sibling_a, sibling_b)):
        targets[k * half : (k + 1) * half, :] = piece[0:half, :]
    smalls = [unpack(far_a), unpack(sibling_a)]
    products(source, targets, factor, smalls, scaled, table)


def neighbour_step(me, turn):
    step = 2 + 2 * (me % 2)
    return step if turn == 0 else 6 - step


def positions(me):
    sibling = me ^ 1
    own = [me, me ^ neighbour_step(me, 0), me ^ neighbour_step(me, 1), me ^ 6]
    other = [
        sibling,
        sibling ^ neighbour_step(sibling, 0),
        sibling ^ neighbour_step(sibling, 1),
        sibling ^ 6,
    ]
    return [block for pair in zip(own, other) for block in pair]


class Held:

    def __init__(self, own, own_table, sibling, sibling_table, far, far_table):
        self.near = own.shape[1] // LANES * 2
        self.total = self.near + far.shape[1] // LANES
        self.scores, self.tables = (own, sibling, far), (own_table, sibling_table, far_table)

    def place(self, p):
        return (p % 2, p // 2) if p < self.near else (2, p - self.near)

    def score(self, at, p):
        part, k = self.place(p)
        return self.scores[part][at, k * LANES : (k + 1) * LANES]

    def row(self, kind, p):
        part, k = self.place(p)
        return self.tables[part][kind, k : k + 1, :]


def first_kernel(
    own, own_table, sibling, sibling_table, far, far_table, found, logw, message, row_pot, ordered
):
    order = positions(lax.axis_index("blk"))
    held = Held(own, own_table, sibling, sibling_table, far, far_table)
    rows = own.shape[0]

    def row_found(at, value):
        row_pot[at, :] = logw[at, :] - value

    def column_found(p, value):
        ordered[pl.ds(order[p], 1), :] = value - held.row(1, p)

    row_sweep(held.score, range(held.near, held.total), rows, row_found, others=found)
    column_sweep(held.score, range(held.total), rows, row_pot, column_found)
    message[...] = jnp.broadcast_to(ordered[...][None], message.shape)


def second_kernel(
    copies, own, own_table, sibling, sibling_table, far, far_table, got, logw, row, message,
    row_pot, ordered,
):
    order = positions(lax.axis_index("blk"))
    held = Held(own, own_table, sibling, sibling_table, far, far_table)
    rows = own.shape[0]
    values = got[...]
    top = jnp.max(values, axis=0)
    ordered[...] = top + jnp.log2(jnp.sum(jnp.exp2(values - top[None]), axis=0))
    columns = []
    for p in range(held.total):
        columns.append(held.row(0, p) - ordered[pl.ds(order[p], 1), :] - held.row(1, p))

    def row_found(at, value):
        row_pot[at, :] = logw[at, :] - value

    def column_found(p, value):
        at = pl.ds((held.total - 1 - order[p]) * copies, copies)
        message[at, :] = jnp.broadcast_to(value - held.row(1, p), (copies, LANES))

    row_sweep(held.score, range(held.total), rows, row_found, columns=columns)
    column_sweep(held.score, range(held.total), rows, row_pot, column_found)
    row[...] = as_row(row_pot[:, 0:1]) * (epsilon * LN2)


def last_kernel(got, small, row, row_out, column_out):
    values = got[...]
    top = jnp.max(values, axis=0, keepdims=True)
    total = top + jnp.log2(jnp.sum(jnp.exp2(values - top), axis=0, keepdims=True))
    column_out[...] = epsilon * small[1:2, :] - (epsilon * LN2) * total
    row_out[...] = row[...]


def lse(values):
    top = jnp.max(values, axis=0)
    return top + jnp.log(jnp.sum(jnp.exp(values - top[None]), axis=0))


def solution(mesh):
    blk, grp = mesh.shape["blk"], mesh.shape["grp"]
    chips = blk // 2
    everyone = ("chip", "core", "grp")

    def shards_square(source_embed, target_embed, target_init, source_logw, target_logw):
        rows, depth = source_embed.shape
        width = target_embed.shape[0]
        half = width // 2
        factor = inverse_eps * LOG2E / math.sqrt(depth)
        vmem, hbm = pl.BlockSpec(memory_space=pltpu.VMEM), pl.BlockSpec(memory_space=pltpu.HBM)
        params = pltpu.CompilerParams(vmem_limit_bytes=16 * 1024 * 1024)

        def values(*shape):
            return jax.ShapeDtypeStruct(shape, jnp.float32)

        def cost(targets, sweeps):
            return pl.CostEstimate(
                flops=2 * rows * targets * depth + 16 * sweeps * rows * blk * width,
                transcendentals=2 * sweeps * rows * blk * width,
                bytes_accessed=2 * (rows + targets) * depth,
            )

        def along(array, turn):
            return lax.ppermute(
                array, "blk", [(i ^ neighbour_step(i, turn), i) for i in range(blk)]
            )

        def to_sibling(array):
            return fetch(array, "blk", 1, blk)

        def exchange(message):
            order = list(range(blk * grp))[::-1]
            return lax.all_to_all(message, ("blk", "grp"), 0, 0, axis_index_groups=[order])

        def block_of(size):
            return jax.ShapeDtypeStruct((size, depth), target_embed.dtype)

        def in_hbm(*arrays):
            return [pltpu.with_memory_space_constraint(each, pltpu.HBM) for each in arrays]

        first, second, whole, small, first_plain, second_plain = pl.pallas_call(
            head_kernel,
            out_shape=(
                block_of(half + SPARE),
                block_of(half + SPARE),
                block_of(width + SPARE),
                values(2, width),
                block_of(half),
                block_of(half),
            ),
            in_specs=[hbm] * 3,
            out_specs=(vmem,) * 6,
            scratch_shapes=[
                pltpu.VMEM((1, width), jnp.float32),
                pltpu.VMEM((1, width), jnp.float32),
                pltpu.SemaphoreType.DMA((3,)),
            ],
            compiler_params=params,
        )(*in_hbm(target_embed, target_init.reshape(1, width), target_logw.reshape(1, width)))
        a_first = along(first, 0)
        b_second = along(second, 1)
        a_second = along(second_plain, 0)
        b_first = along(first_plain, 1)
        far_a = along(a_first, 1)
        far_b = along(b_second[:half], 0)
        source, logw, passed = pl.pallas_call(
            source_kernel,
            out_shape=(
                jax.ShapeDtypeStruct((rows, depth), source_embed.dtype),
                values(rows, LANES),
                block_of(width + SPARE),
            ),
            in_specs=[hbm] * 2 + [vmem],
            out_specs=(vmem,) * 3,
            scratch_shapes=[pltpu.VMEM((1, rows), jnp.float32), pltpu.SemaphoreType.DMA((2,))],
            compiler_params=params,
        )(*in_hbm(source_embed, source_logw.reshape(1, rows)), whole)
        near = (a_first, a_second, b_first, b_second)
        sibling = pl.pallas_call(
            sibling_kernel,
            out_shape=block_of(3 * (width + SPARE)),
            in_specs=[vmem] * 5,
            out_specs=vmem,
            compiler_params=params,
            cost_estimate=cost(0, 0),
        )(passed, *near)
        sibling = to_sibling(sibling)

        def table():
            return values(2, SUBLANES, width)

        def scores_of(kernel, blocks, pieces, extra=()):
            return pl.pallas_call(
                functools.partial(kernel, factor),
                out_shape=(values(rows, blocks * width), table(), *extra),
                in_specs=[vmem] * (1 + len(pieces)),
                out_specs=(vmem,) * (2 + len(extra)),
                scratch_shapes=[pltpu.VMEM((blocks * width, depth), target_embed.dtype)],
                compiler_params=params,
                cost_estimate=cost(0, 0),
            )(source, *pieces)

        own = scores_of(own_kernel, 3, (whole, *near))

        def passed_on(message, tie, weight):
            return pl.pallas_call(
                pass_kernel,
                out_shape=jax.ShapeDtypeStruct(message.shape, message.dtype),
                in_specs=[vmem] * 2,
                out_specs=vmem,
                compiler_params=params,
                cost_estimate=cost(weight * width, 0),
            )(message, tie)

        sibling_a = to_sibling(passed_on(far_a, own[1], 0))
        sibling_b = to_sibling(passed_on(far_b, own[1], 50))
        *other, found = scores_of(
            sibling_scores_kernel, 3, (sibling, own[0]), (values(rows, LANES),)
        )
        far = scores_of(far_kernel, 2, (far_a, far_b, sibling_a, sibling_b, other[0]))
        scores = (*own, *other, *far)
        row_scratch = pltpu.VMEM((rows, LANES), jnp.float32)
        block_scratch = pltpu.VMEM((blk, width), jnp.float32)
        message = pl.pallas_call(
            first_kernel,
            out_shape=values(blk * grp, blk, width),
            in_specs=[vmem] * 8,
            out_specs=vmem,
            scratch_shapes=[row_scratch, block_scratch],
            compiler_params=params,
            cost_estimate=cost(0, 1),
        )(*scores, found, logw)
        got = exchange(message)
        row, message = pl.pallas_call(
            functools.partial(second_kernel, grp),
            out_shape=(values(1, rows), values(blk * grp, width)),
            in_specs=[vmem] * 8,
            out_specs=(vmem, vmem),
            scratch_shapes=[row_scratch, block_scratch],
            compiler_params=params,
            cost_estimate=cost(0, 1),
        )(*scores, got, logw)
        got = exchange(message)
        row_pot, column_pot = pl.pallas_call(
            last_kernel,
            out_shape=(values(1, rows), values(1, width)),
            in_specs=[vmem] * 3,
            out_specs=(vmem, vmem),
            compiler_params=params,
        )(got, small, row)
        return row_pot.reshape(rows), column_pot.reshape(width)

    def shards_any(source_embed, target_embed, target_init, source_logw, target_logw):
        width, depth = target_embed.shape
        factor = -1.0 / math.sqrt(depth)
        me = lax.axis_index("chip") * 2 + lax.axis_index("core")

        def swap_order(values):
            parts = values.reshape(blk, width)
            step = 1
            while step < blk:
                pairs = parts.reshape(blk // (2 * step), 2, step, width)
                pairs = jnp.where(me & step, pairs[:, ::-1], pairs)
                parts = pairs.reshape(blk, width)
                step *= 2
            return parts

        small = jnp.stack([target_init, target_logw])
        targets, smalls = gather_any(target_embed, small, chips)
        cost = (
            lax.dot_general(
                source_embed, targets, (((1,), (1,)), ((), ())), preferred_element_type=jnp.float32
            )
            * factor
        )
        column_pot, logw_all = smalls[:, 0].reshape(-1), smalls[:, 1].reshape(-1)
        for iteration in range(ITERS):
            scores = (column_pot[None, :] - cost) * inverse_eps
            row_top = jnp.max(scores, axis=1)
            row_sum = jnp.sum(jnp.exp(scores - row_top[:, None]), axis=1)
            row_pot = epsilon * source_logw - epsilon * (row_top + jnp.log(row_sum))
            part = swap_order(lse((row_pot[:, None] - cost) * inverse_eps))
            if iteration < ITERS - 1:
                copies = jnp.broadcast_to(part[None], (blk * grp, blk, width))
                got = lax.all_to_all(copies, everyone, 0, 0)
                total = swap_order(lse(got)).reshape(-1)
                column_pot = epsilon * logw_all - epsilon * total
            else:
                copies = jnp.broadcast_to(part[:, None], (blk, grp, width)).reshape(blk * grp, width)
                got = lax.all_to_all(copies, everyone, 0, 0)
                own_column = epsilon * target_logw - epsilon * lse(got)
        return row_pot, own_column

    if chips == 4:
        shards = shards_square
        rows_spec, blk_spec = P(("blk", "grp")), P("blk")
    else:
        shards = shards_any
        rows_spec, blk_spec = P(everyone), P(("chip", "core"))
        mesh = Mesh(mesh.devices.reshape(chips, 2, grp), everyone)
    in_specs = (rows_spec, blk_spec, blk_spec, rows_spec, blk_spec)
    out_specs = (rows_spec, blk_spec)
    return jax.shard_map(shards, mesh=mesh, in_specs=in_specs, out_specs=out_specs, check_vma=False)
```

```python
import functools
import math

import jax
import jax.numpy as jnp
from jax import lax
from jax.experimental import pallas as pl
from jax.experimental.pallas import tpu as pltpu
from jax.sharding import Mesh, PartitionSpec as P

ITERS = 2
epsilon = 0.1
inverse_eps = 10.0
LOG2E = math.log2(math.e)
LN2 = math.log(2.0)
LANES = 128
SPARE = 8
SUBLANES = 8


def fetch(array, axis, step, size):
    return lax.ppermute(array, axis, [(i ^ step, i) for i in range(size)])


def doubled(held, step, chips):
    return jnp.concatenate([held, fetch(held, "chip", step, chips)])


def gather_any(array, small, chips):
    pair = jnp.stack([array, fetch(array, "core", 1, 2)])[None]
    smalls = jnp.stack([small, fetch(small, "core", 1, 2)])[None]
    step = 1
    while step < chips:
        pair = doubled(pair, step, chips)
        smalls = doubled(smalls, step, chips)
        step *= 2
    return pair.reshape(-1, array.shape[1]), smalls.reshape(-1, *small.shape)


def as_column(row):
    size = row.shape[1]
    here = lax.broadcasted_iota(jnp.int32, (LANES, LANES), 0)
    there = lax.broadcasted_iota(jnp.int32, (LANES, LANES), 1)
    parts = []
    for start in range(0, size, LANES):
        wide = jnp.broadcast_to(row[:, start : start + LANES], (LANES, LANES))
        parts.append(jnp.sum(jnp.where(here == there, wide, 0.0), axis=1, keepdims=True))
    return jnp.concatenate(parts, axis=0)


def as_row(column):
    size = column.shape[0]
    here = lax.broadcasted_iota(jnp.int32, (LANES, LANES), 0)
    there = lax.broadcasted_iota(jnp.int32, (LANES, LANES), 1)
    parts = []
    for start in range(0, size, LANES):
        wide = jnp.broadcast_to(column[start : start + LANES], (LANES, LANES))
        parts.append(jnp.sum(jnp.where(here == there, wide, 0.0), axis=0, keepdims=True))
    return jnp.concatenate(parts, axis=1)


CHUNK = 64


def chunks_of(rows):
    return [pl.ds(start, CHUNK) for start in range(0, rows, CHUNK)]


def row_sweep(score_of, blocks, rows, found_of, columns=None, others=None):
    tops = []
    for at in chunks_of(rows):
        top = None if others is None else others[at, :]
        for p in blocks:
            score = score_of(at, p)
            score = score if columns is None else score + columns[p]
            top = score if top is None else jnp.maximum(top, score)
        tops.append(jnp.max(top, axis=1, keepdims=True))
    for at, top in zip(chunks_of(rows), tops):
        total = None
        for p in blocks:
            shift = -top if columns is None else columns[p] - top
            term = jnp.exp2(score_of(at, p) + shift)
            total = term if total is None else total + term
        total = jnp.sum(total, axis=1, keepdims=True)
        if others is not None:
            total = total + jnp.exp2(others[at, :] - top)
        found_of(at, top + jnp.log2(total))


def column_sweep(score_of, blocks, rows, row_pot, found_of):
    folds = (CHUNK // SUBLANES, SUBLANES, LANES)
    found = [[] for _ in blocks]
    for at in chunks_of(rows):
        addend = row_pot[at, :]
        for p in blocks:
            score = (score_of(at, p) + addend).reshape(folds)
            top = jnp.max(score, axis=0)
            found[p].append((top, jnp.sum(jnp.exp2(score - top[None]), axis=0)))
    for p in blocks:
        top = functools.reduce(jnp.maximum, [each for each, _ in found[p]])
        top = jnp.max(top, axis=0, keepdims=True)
        total = sum(each * jnp.exp2(at_top - top) for at_top, each in found[p])
        found_of(p, top + jnp.log2(jnp.sum(total, axis=0, keepdims=True)))


def products(source, targets, factor, smalls, scaled, table):
    for p, small in enumerate(smalls):
        table[0, p : p + 1, :] = small[1:2] * LOG2E
        table[1, p : p + 1, :] = small[0:1] * (inverse_eps * LOG2E)
    for p in range(0, len(smalls), 2):
        end = min(p + 2, len(smalls))
        lanes = slice(p * LANES, end * LANES)
        product = lax.dot_general(
            source[...], targets[lanes, :], (((1,), (1,)), ((), ())),
            preferred_element_type=jnp.float32,
        )
        shift = jnp.concatenate([table[1, q : q + 1, :] for q in range(p, end)], axis=1)
        scaled[:, lanes] = product * factor + shift


def head_kernel(
    own, init, target_logw, first, second, whole, small, init_row, logw_row, sems
):
    rows, half = own.shape[0], second.shape[0]
    copies = [
        pltpu.make_async_copy(own, whole.at[0:rows], sems.at[0]),
        pltpu.make_async_copy(init, init_row, sems.at[1]),
        pltpu.make_async_copy(target_logw, logw_row, sems.at[2]),
    ]
    for copy in copies:
        copy.start()
    for copy in copies:
        copy.wait()
    first[0:half, :] = whole[0:half, :]
    second[...] = whole[half:rows, :]
    small[0:1, :] = init_row[...]
    small[1:2, :] = logw_row[...]
    filler = jnp.zeros((SPARE - 2, LANES), jnp.float32)
    rest = jnp.concatenate([init_row[...], logw_row[...], filler], axis=0)
    for k in range(whole.shape[1] // LANES):
        lanes = slice(k * LANES, (k + 1) * LANES)
        part = (rest if k < 3 else jnp.zeros_like(rest)).astype(whole.dtype)
        first[half:, lanes] = part
        whole[rows:, lanes] = part
        rest = rest - part.astype(jnp.float32)


def source_kernel(source, logw, whole, held, row_logw, passed, rows_row, sems):
    copies = [
        pltpu.make_async_copy(source, held, sems.at[0]),
        pltpu.make_async_copy(logw, rows_row, sems.at[1]),
    ]
    for copy in copies:
        copy.start()
    passed[...] = whole[...]
    for copy in copies:
        copy.wait()
    row_logw[...] = jnp.broadcast_to(as_column(rows_row[...] * LOG2E), row_logw.shape)


def sibling_kernel(whole, a_first, a_second, b_first, b_second, out):
    half = a_second.shape[0]
    block = 2 * half + SPARE
    out[0:block, :] = whole[...]
    out[block : block + half, :] = a_first[0:half, :]
    out[block + half : block + 2 * half, :] = a_second[...]
    out[block + 2 * half : 2 * block, :] = a_first[half:, :]
    out[2 * block : 2 * block + half, :] = b_first[0:half, :]
    out[2 * block + half : 2 * block + 2 * half, :] = b_second[...]
    out[2 * block + 2 * half : 3 * block, :] = b_first[half:, :]


def unpack(message, end=None):
    end = message.shape[0] if end is None else end
    parts = [
        message[end - SPARE : end, k * LANES : (k + 1) * LANES].astype(jnp.float32)[0:2]
        for k in range(3)
    ]
    return (parts[0] + parts[1]) + parts[2]


def own_kernel(
    factor, source, whole, a_first, a_second, b_first, b_second, scaled, table, targets
):
    half = a_second.shape[0]
    pieces = (whole, whole, a_first, a_second, b_first, b_second)
    targets[0 : 2 * half, :] = whole[0 : 2 * half, :]
    for k in range(2, 6):
        targets[k * half : (k + 1) * half, :] = pieces[k][0:half, :]
    smalls = [unpack(whole), unpack(a_first), unpack(b_first)]
    products(source, targets, factor, smalls, scaled, table)


def sibling_scores_kernel(factor, source, sibling, own, scaled, table, found, targets):
    width = targets.shape[0] // 3
    block = width + SPARE
    smalls = []
    for k in range(3):
        targets[k * width : (k + 1) * width, :] = sibling[k * block : k * block + width, :]
        smalls.append(unpack(sibling, (k + 1) * block))
    products(source, targets, factor, smalls, scaled, table)

    def score_of(at, p):
        part = (own, scaled)[p % 2]
        return part[at, p // 2 * LANES : (p // 2 + 1) * LANES]

    def found_of(at, value):
        found[at, :] = jnp.broadcast_to(value, (CHUNK, LANES))

    row_sweep(score_of, range(6), scaled.shape[0], found_of)


def pass_kernel(message, tie, out):
    out[...] = message[...]


def far_kernel(
    factor, source, far_a, far_b, sibling_a, sibling_b, near, scaled, table, targets
):
    half = targets.shape[0] // 4
    for k, piece in enumerate((far_a, far_b, sibling_a, sibling_b)):
        targets[k * half : (k + 1) * half, :] = piece[0:half, :]
    smalls = [unpack(far_a), unpack(sibling_a)]
    products(source, targets, factor, smalls, scaled, table)


def neighbour_step(me, turn):
    step = 2 + 2 * (me % 2)
    return step if turn == 0 else 6 - step


def positions(me):
    sibling = me ^ 1
    own = [me, me ^ neighbour_step(me, 0), me ^ neighbour_step(me, 1), me ^ 6]
    other = [
        sibling,
        sibling ^ neighbour_step(sibling, 0),
        sibling ^ neighbour_step(sibling, 1),
        sibling ^ 6,
    ]
    return [block for pair in zip(own, other) for block in pair]


class Held:

    def __init__(self, own, own_table, sibling, sibling_table, far, far_table):
        self.near = own.shape[1] // LANES * 2
        self.total = self.near + far.shape[1] // LANES
        self.scores, self.tables = (own, sibling, far), (own_table, sibling_table, far_table)

    def place(self, p):
        return (p % 2, p // 2) if p < self.near else (2, p - self.near)

    def score(self, at, p):
        part, k = self.place(p)
        return self.scores[part][at, k * LANES : (k + 1) * LANES]

    def row(self, kind, p):
        part, k = self.place(p)
        return self.tables[part][kind, k : k + 1, :]


def first_kernel(
    own, own_table, sibling, sibling_table, far, far_table, found, logw, message, row_pot, ordered
):
    order = positions(lax.axis_index("blk"))
    held = Held(own, own_table, sibling, sibling_table, far, far_table)
    rows = own.shape[0]

    def row_found(at, value):
        row_pot[at, :] = logw[at, :] - value

    def column_found(p, value):
        ordered[pl.ds(order[p], 1), :] = value - held.row(1, p)

    row_sweep(held.score, range(held.near, held.total), rows, row_found, others=found)
    column_sweep(held.score, range(held.total), rows, row_pot, column_found)
    message[...] = jnp.broadcast_to(ordered[...][None], message.shape)


def second_kernel(
    copies, own, own_table, sibling, sibling_table, far, far_table, got, logw, row, message,
    row_pot, ordered,
):
    order = positions(lax.axis_index("blk"))
    held = Held(own, own_table, sibling, sibling_table, far, far_table)
    rows = own.shape[0]
    values = got[...]
    top = jnp.max(values, axis=0)
    ordered[...] = top + jnp.log2(jnp.sum(jnp.exp2(values - top[None]), axis=0))
    columns = []
    for p in range(held.total):
        columns.append(held.row(0, p) - ordered[pl.ds(order[p], 1), :] - held.row(1, p))

    def row_found(at, value):
        row_pot[at, :] = logw[at, :] - value

    def column_found(p, value):
        at = pl.ds((held.total - 1 - order[p]) * copies, copies)
        message[at, :] = jnp.broadcast_to(value - held.row(1, p), (copies, LANES))

    row_sweep(held.score, range(held.total), rows, row_found, columns=columns)
    column_sweep(held.score, range(held.total), rows, row_pot, column_found)
    row[...] = as_row(row_pot[:, 0:1]) * (epsilon * LN2)


def last_kernel(got, small, row, row_out, column_out):
    values = got[...]
    top = jnp.max(values, axis=0, keepdims=True)
    total = top + jnp.log2(jnp.sum(jnp.exp2(values - top), axis=0, keepdims=True))
    column_out[...] = epsilon * small[1:2, :] - (epsilon * LN2) * total
    row_out[...] = row[...]


def lse(values):
    top = jnp.max(values, axis=0)
    return top + jnp.log(jnp.sum(jnp.exp(values - top[None]), axis=0))


def solution(mesh):
    blk, grp = mesh.shape["blk"], mesh.shape["grp"]
    chips = blk // 2
    everyone = ("chip", "core", "grp")

    def shards_square(source_embed, target_embed, target_init, source_logw, target_logw):
        rows, depth = source_embed.shape
        width = target_embed.shape[0]
        half = width // 2
        factor = inverse_eps * LOG2E / math.sqrt(depth)
        vmem, hbm = pl.BlockSpec(memory_space=pltpu.VMEM), pl.BlockSpec(memory_space=pltpu.HBM)
        params = pltpu.CompilerParams(vmem_limit_bytes=16 * 1024 * 1024)

        def values(*shape):
            return jax.ShapeDtypeStruct(shape, jnp.float32)

        def cost(targets, sweeps):
            return pl.CostEstimate(
                flops=2 * rows * targets * depth + 16 * sweeps * rows * blk * width,
                transcendentals=2 * sweeps * rows * blk * width,
                bytes_accessed=2 * (rows + targets) * depth,
            )

        def along(array, turn):
            return lax.ppermute(
                array, "blk", [(i ^ neighbour_step(i, turn), i) for i in range(blk)]
            )

        def to_sibling(array):
            return fetch(array, "blk", 1, blk)

        def exchange(message):
            order = list(range(blk * grp))[::-1]
            return lax.all_to_all(message, ("blk", "grp"), 0, 0, axis_index_groups=[order])

        def block_of(size):
            return jax.ShapeDtypeStruct((size, depth), target_embed.dtype)

        def in_hbm(*arrays):
            return [pltpu.with_memory_space_constraint(each, pltpu.HBM) for each in arrays]

        first, second, whole, small = pl.pallas_call(
            head_kernel,
            out_shape=(
                block_of(half + SPARE),
                block_of(half),
                block_of(width + SPARE),
                values(2, width),
            ),
            in_specs=[hbm] * 3,
            out_specs=(vmem,) * 4,
            scratch_shapes=[
                pltpu.VMEM((1, width), jnp.float32),
                pltpu.VMEM((1, width), jnp.float32),
                pltpu.SemaphoreType.DMA((3,)),
            ],
            compiler_params=params,
        )(*in_hbm(target_embed, target_init.reshape(1, width), target_logw.reshape(1, width)))
        a_first = along(first, 0)
        b_second = along(second, 1)
        a_second = along(second, 0)
        b_first = along(first, 1)
        far_a = along(a_first, 1)
        far_b = along(b_second, 0)
        source, logw, passed = pl.pallas_call(
            source_kernel,
            out_shape=(
                jax.ShapeDtypeStruct((rows, depth), source_embed.dtype),
                values(rows, LANES),
                block_of(width + SPARE),
            ),
            in_specs=[hbm] * 2 + [vmem],
            out_specs=(vmem,) * 3,
            scratch_shapes=[pltpu.VMEM((1, rows), jnp.float32), pltpu.SemaphoreType.DMA((2,))],
            compiler_params=params,
        )(*in_hbm(source_embed, source_logw.reshape(1, rows)), whole)
        near = (a_first, a_second, b_first, b_second)
        sibling = pl.pallas_call(
            sibling_kernel,
            out_shape=block_of(3 * (width + SPARE)),
            in_specs=[vmem] * 5,
            out_specs=vmem,
            compiler_params=params,
            cost_estimate=cost(0, 0),
        )(passed, *near)
        sibling = to_sibling(sibling)

        def table():
            return values(2, SUBLANES, width)

        def scores_of(kernel, blocks, pieces, extra=()):
            return pl.pallas_call(
                functools.partial(kernel, factor),
                out_shape=(values(rows, blocks * width), table(), *extra),
                in_specs=[vmem] * (1 + len(pieces)),
                out_specs=(vmem,) * (2 + len(extra)),
                scratch_shapes=[pltpu.VMEM((blocks * width, depth), target_embed.dtype)],
                compiler_params=params,
                cost_estimate=cost(0, 0),
            )(source, *pieces)

        own = scores_of(own_kernel, 3, (whole, *near))

        def passed_on(message, tie, weight):
            return pl.pallas_call(
                pass_kernel,
                out_shape=jax.ShapeDtypeStruct(message.shape, message.dtype),
                in_specs=[vmem] * 2,
                out_specs=vmem,
                compiler_params=params,
                cost_estimate=cost(weight * width, 0),
            )(message, tie)

        sibling_a = to_sibling(passed_on(far_a, own[1], 0))
        sibling_b = to_sibling(passed_on(far_b, own[1], 50))
        *other, found = scores_of(
            sibling_scores_kernel, 3, (sibling, own[0]), (values(rows, LANES),)
        )
        far = scores_of(far_kernel, 2, (far_a, far_b, sibling_a, sibling_b, other[0]))
        scores = (*own, *other, *far)
        row_scratch = pltpu.VMEM((rows, LANES), jnp.float32)
        block_scratch = pltpu.VMEM((blk, width), jnp.float32)
        message = pl.pallas_call(
            first_kernel,
            out_shape=values(blk * grp, blk, width),
            in_specs=[vmem] * 8,
            out_specs=vmem,
            scratch_shapes=[row_scratch, block_scratch],
            compiler_params=params,
            cost_estimate=cost(0, 1),
        )(*scores, found, logw)
        got = exchange(message)
        row, message = pl.pallas_call(
            functools.partial(second_kernel, grp),
            out_shape=(values(1, rows), values(blk * grp, width)),
            in_specs=[vmem] * 8,
            out_specs=(vmem, vmem),
            scratch_shapes=[row_scratch, block_scratch],
            compiler_params=params,
            cost_estimate=cost(0, 1),
        )(*scores, got, logw)
        got = exchange(message)
        row_pot, column_pot = pl.pallas_call(
            last_kernel,
            out_shape=(values(1, rows), values(1, width)),
            in_specs=[vmem] * 3,
            out_specs=(vmem, vmem),
            compiler_params=params,
        )(got, small, row)
        return row_pot.reshape(rows), column_pot.reshape(width)

    def shards_any(source_embed, target_embed, target_init, source_logw, target_logw):
        width, depth = target_embed.shape
        factor = -1.0 / math.sqrt(depth)
        me = lax.axis_index("chip") * 2 + lax.axis_index("core")

        def swap_order(values):
            parts = values.reshape(blk, width)
            step = 1
            while step < blk:
                pairs = parts.reshape(blk // (2 * step), 2, step, width)
                pairs = jnp.where(me & step, pairs[:, ::-1], pairs)
                parts = pairs.reshape(blk, width)
                step *= 2
            return parts

        small = jnp.stack([target_init, target_logw])
        targets, smalls = gather_any(target_embed, small, chips)
        cost = (
            lax.dot_general(
                source_embed, targets, (((1,), (1,)), ((), ())), preferred_element_type=jnp.float32
            )
            * factor
        )
        column_pot, logw_all = smalls[:, 0].reshape(-1), smalls[:, 1].reshape(-1)
        for iteration in range(ITERS):
            scores = (column_pot[None, :] - cost) * inverse_eps
            row_top = jnp.max(scores, axis=1)
            row_sum = jnp.sum(jnp.exp(scores - row_top[:, None]), axis=1)
            row_pot = epsilon * source_logw - epsilon * (row_top + jnp.log(row_sum))
            part = swap_order(lse((row_pot[:, None] - cost) * inverse_eps))
            if iteration < ITERS - 1:
                copies = jnp.broadcast_to(part[None], (blk * grp, blk, width))
                got = lax.all_to_all(copies, everyone, 0, 0)
                total = swap_order(lse(got)).reshape(-1)
                column_pot = epsilon * logw_all - epsilon * total
            else:
                copies = jnp.broadcast_to(part[:, None], (blk, grp, width)).reshape(blk * grp, width)
                got = lax.all_to_all(copies, everyone, 0, 0)
                own_column = epsilon * target_logw - epsilon * lse(got)
        return row_pot, own_column

    if chips == 4:
        shards = shards_square
        rows_spec, blk_spec = P(("blk", "grp")), P("blk")
    else:
        shards = shards_any
        rows_spec, blk_spec = P(everyone), P(("chip", "core"))
        mesh = Mesh(mesh.devices.reshape(chips, 2, grp), everyone)
    in_specs = (rows_spec, blk_spec, blk_spec, rows_spec, blk_spec)
    out_specs = (rows_spec, blk_spec)
    return jax.shard_map(shards, mesh=mesh, in_specs=in_specs, out_specs=out_specs, check_vma=False)
```

```python
import functools
import math

import jax
import jax.numpy as jnp
from jax import lax
from jax.experimental import pallas as pl
from jax.experimental.pallas import tpu as pltpu
from jax.sharding import Mesh, PartitionSpec as P

ITERS = 2
epsilon = 0.1
inverse_eps = 10.0
LOG2E = math.log2(math.e)
LN2 = math.log(2.0)
LANES = 128
SPARE = 8
SUBLANES = 8


def fetch(array, axis, step, size):
    return lax.ppermute(array, axis, [(i ^ step, i) for i in range(size)])


def doubled(held, step, chips):
    return jnp.concatenate([held, fetch(held, "chip", step, chips)])


def gather_any(array, small, chips):
    pair = jnp.stack([array, fetch(array, "core", 1, 2)])[None]
    smalls = jnp.stack([small, fetch(small, "core", 1, 2)])[None]
    step = 1
    while step < chips:
        pair = doubled(pair, step, chips)
        smalls = doubled(smalls, step, chips)
        step *= 2
    return pair.reshape(-1, array.shape[1]), smalls.reshape(-1, *small.shape)


def as_column(row):
    size = row.shape[1]
    here = lax.broadcasted_iota(jnp.int32, (LANES, LANES), 0)
    there = lax.broadcasted_iota(jnp.int32, (LANES, LANES), 1)
    parts = []
    for start in range(0, size, LANES):
        wide = jnp.broadcast_to(row[:, start : start + LANES], (LANES, LANES))
        parts.append(jnp.sum(jnp.where(here == there, wide, 0.0), axis=1, keepdims=True))
    return jnp.concatenate(parts, axis=0)


def as_row(column):
    size = column.shape[0]
    here = lax.broadcasted_iota(jnp.int32, (LANES, LANES), 0)
    there = lax.broadcasted_iota(jnp.int32, (LANES, LANES), 1)
    parts = []
    for start in range(0, size, LANES):
        wide = jnp.broadcast_to(column[start : start + LANES], (LANES, LANES))
        parts.append(jnp.sum(jnp.where(here == there, wide, 0.0), axis=0, keepdims=True))
    return jnp.concatenate(parts, axis=1)


CHUNK = 64


def chunks_of(rows):
    return [pl.ds(start, CHUNK) for start in range(0, rows, CHUNK)]


def row_sweep(score_of, blocks, rows, found_of, columns=None, others=None):
    tops = []
    for at in chunks_of(rows):
        top = None if others is None else others[at, :]
        for p in blocks:
            score = score_of(at, p)
            score = score if columns is None else score + columns[p]
            top = score if top is None else jnp.maximum(top, score)
        tops.append(jnp.max(top, axis=1, keepdims=True))
    for at, top in zip(chunks_of(rows), tops):
        total = None
        for p in blocks:
            shift = -top if columns is None else columns[p] - top
            term = jnp.exp2(score_of(at, p) + shift)
            total = term if total is None else total + term
        total = jnp.sum(total, axis=1, keepdims=True)
        if others is not None:
            total = total + jnp.exp2(others[at, :] - top)
        found_of(at, top + jnp.log2(total))


def column_sweep(score_of, blocks, rows, row_pot, found_of):
    folds = (CHUNK // SUBLANES, SUBLANES, LANES)
    found = [[] for _ in blocks]
    for at in chunks_of(rows):
        addend = row_pot[at, :]
        for p in blocks:
            score = (score_of(at, p) + addend).reshape(folds)
            top = jnp.max(score, axis=0)
            found[p].append((top, jnp.sum(jnp.exp2(score - top[None]), axis=0)))
    for p in blocks:
        top = functools.reduce(jnp.maximum, [each for each, _ in found[p]])
        top = jnp.max(top, axis=0, keepdims=True)
        total = sum(each * jnp.exp2(at_top - top) for at_top, each in found[p])
        found_of(p, top + jnp.log2(jnp.sum(total, axis=0, keepdims=True)))


def products(source, targets, factor, smalls, scaled, table):
    for p, small in enumerate(smalls):
        table[0, p : p + 1, :] = small[1:2] * LOG2E
        table[1, p : p + 1, :] = small[0:1] * (inverse_eps * LOG2E)
    for p in range(0, len(smalls), 2):
        end = min(p + 2, len(smalls))
        lanes = slice(p * LANES, end * LANES)
        product = lax.dot_general(
            source[...], targets[lanes, :], (((1,), (1,)), ((), ())),
            preferred_element_type=jnp.float32,
        )
        shift = jnp.concatenate([table[1, q : q + 1, :] for q in range(p, end)], axis=1)
        scaled[:, lanes] = product * factor + shift


def head_kernel(
    own, init, target_logw, first, second, whole, small, init_row, logw_row, sems
):
    rows, half = own.shape[0], second.shape[0]
    copies = [
        pltpu.make_async_copy(own, whole.at[0:rows], sems.at[0]),
        pltpu.make_async_copy(init, init_row, sems.at[1]),
        pltpu.make_async_copy(target_logw, logw_row, sems.at[2]),
    ]
    for copy in copies:
        copy.start()
    for copy in copies:
        copy.wait()
    first[0:half, :] = whole[0:half, :]
    second[...] = whole[half:rows, :]
    small[0:1, :] = init_row[...]
    small[1:2, :] = logw_row[...]
    filler = jnp.zeros((SPARE - 2, LANES), jnp.float32)
    rest = jnp.concatenate([init_row[...], logw_row[...], filler], axis=0)
    for k in range(whole.shape[1] // LANES):
        lanes = slice(k * LANES, (k + 1) * LANES)
        part = (rest if k < 3 else jnp.zeros_like(rest)).astype(whole.dtype)
        first[half:, lanes] = part
        whole[rows:, lanes] = part
        rest = rest - part.astype(jnp.float32)


def source_kernel(source, logw, whole, held, row_logw, passed, rows_row, sems):
    copies = [
        pltpu.make_async_copy(source, held, sems.at[0]),
        pltpu.make_async_copy(logw, rows_row, sems.at[1]),
    ]
    for copy in copies:
        copy.start()
    passed[...] = whole[...]
    for copy in copies:
        copy.wait()
    row_logw[...] = jnp.broadcast_to(as_column(rows_row[...] * LOG2E), row_logw.shape)


def sibling_kernel(whole, a_first, a_second, b_first, b_second, out):
    half = a_second.shape[0]
    block = 2 * half + SPARE
    out[0:block, :] = whole[...]
    out[block : block + half, :] = a_first[0:half, :]
    out[block + half : block + 2 * half, :] = a_second[...]
    out[block + 2 * half : 2 * block, :] = a_first[half:, :]
    out[2 * block : 2 * block + half, :] = b_first[0:half, :]
    out[2 * block + half : 2 * block + 2 * half, :] = b_second[...]
    out[2 * block + 2 * half : 3 * block, :] = b_first[half:, :]


def unpack(message, end=None):
    end = message.shape[0] if end is None else end
    parts = [
        message[end - SPARE : end, k * LANES : (k + 1) * LANES].astype(jnp.float32)[0:2]
        for k in range(3)
    ]
    return (parts[0] + parts[1]) + parts[2]


def own_kernel(
    factor, source, whole, a_first, a_second, b_first, b_second, scaled, table, targets
):
    half = a_second.shape[0]
    pieces = (whole, whole, a_first, a_second, b_first, b_second)
    targets[0 : 2 * half, :] = whole[0 : 2 * half, :]
    for k in range(2, 6):
        targets[k * half : (k + 1) * half, :] = pieces[k][0:half, :]
    smalls = [unpack(whole), unpack(a_first), unpack(b_first)]
    products(source, targets, factor, smalls, scaled, table)


def sibling_scores_kernel(factor, source, sibling, own, scaled, table, found, targets):
    width = targets.shape[0] // 3
    block = width + SPARE
    smalls = []
    for k in range(3):
        targets[k * width : (k + 1) * width, :] = sibling[k * block : k * block + width, :]
        smalls.append(unpack(sibling, (k + 1) * block))
    products(source, targets, factor, smalls, scaled, table)

    def score_of(at, p):
        part = (own, scaled)[p % 2]
        return part[at, p // 2 * LANES : (p // 2 + 1) * LANES]

    def found_of(at, value):
        found[at, :] = jnp.broadcast_to(value, (CHUNK, LANES))

    row_sweep(score_of, range(6), scaled.shape[0], found_of)


def pass_kernel(message, tie, out):
    out[...] = message[...]


def far_kernel(
    factor, source, far_a, far_b, sibling_a, sibling_b, near, scaled, table, targets
):
    half = targets.shape[0] // 4
    for k, piece in enumerate((far_a, far_b, sibling_a, sibling_b)):
        targets[k * half : (k + 1) * half, :] = piece[0:half, :]
    smalls = [unpack(far_a), unpack(sibling_a)]
    products(source, targets, factor, smalls, scaled, table)


def neighbour_step(me, turn):
    step = 4 - 2 * (me % 2)
    return step if turn == 0 else 6 - step


def positions(me):
    sibling = me ^ 1
    own = [me, me ^ neighbour_step(me, 0), me ^ neighbour_step(me, 1), me ^ 6]
    other = [
        sibling,
        sibling ^ neighbour_step(sibling, 0),
        sibling ^ neighbour_step(sibling, 1),
        sibling ^ 6,
    ]
    return [block for pair in zip(own, other) for block in pair]


class Held:

    def __init__(self, own, own_table, sibling, sibling_table, far, far_table):
        self.near = own.shape[1] // LANES * 2
        self.total = self.near + far.shape[1] // LANES
        self.scores, self.tables = (own, sibling, far), (own_table, sibling_table, far_table)

    def place(self, p):
        return (p % 2, p // 2) if p < self.near else (2, p - self.near)

    def score(self, at, p):
        part, k = self.place(p)
        return self.scores[part][at, k * LANES : (k + 1) * LANES]

    def row(self, kind, p):
        part, k = self.place(p)
        return self.tables[part][kind, k : k + 1, :]


def first_kernel(
    own, own_table, sibling, sibling_table, far, far_table, found, logw, message, row_pot, ordered
):
    order = positions(lax.axis_index("blk"))
    held = Held(own, own_table, sibling, sibling_table, far, far_table)
    rows = own.shape[0]

    def row_found(at, value):
        row_pot[at, :] = logw[at, :] - value

    def column_found(p, value):
        ordered[pl.ds(order[p], 1), :] = value - held.row(1, p)

    row_sweep(held.score, range(held.near, held.total), rows, row_found, others=found)
    column_sweep(held.score, range(held.total), rows, row_pot, column_found)
    message[...] = jnp.broadcast_to(ordered[...][None], message.shape)


def second_kernel(
    copies, own, own_table, sibling, sibling_table, far, far_table, got, logw, row, message,
    row_pot, ordered,
):
    order = positions(lax.axis_index("blk"))
    held = Held(own, own_table, sibling, sibling_table, far, far_table)
    rows = own.shape[0]
    values = got[...]
    top = jnp.max(values, axis=0)
    ordered[...] = top + jnp.log2(jnp.sum(jnp.exp2(values - top[None]), axis=0))
    columns = []
    for p in range(held.total):
        columns.append(held.row(0, p) - ordered[pl.ds(order[p], 1), :] - held.row(1, p))

    def row_found(at, value):
        row_pot[at, :] = logw[at, :] - value

    def column_found(p, value):
        at = pl.ds((held.total - 1 - order[p]) * copies, copies)
        message[at, :] = jnp.broadcast_to(value - held.row(1, p), (copies, LANES))

    row_sweep(held.score, range(held.total), rows, row_found, columns=columns)
    column_sweep(held.score, range(held.total), rows, row_pot, column_found)
    row[...] = as_row(row_pot[:, 0:1]) * (epsilon * LN2)


def last_kernel(got, small, row, row_out, column_out):
    values = got[...]
    top = jnp.max(values, axis=0, keepdims=True)
    total = top + jnp.log2(jnp.sum(jnp.exp2(values - top), axis=0, keepdims=True))
    column_out[...] = epsilon * small[1:2, :] - (epsilon * LN2) * total
    row_out[...] = row[...]


def lse(values):
    top = jnp.max(values, axis=0)
    return top + jnp.log(jnp.sum(jnp.exp(values - top[None]), axis=0))


def solution(mesh):
    blk, grp = mesh.shape["blk"], mesh.shape["grp"]
    chips = blk // 2
    everyone = ("chip", "core", "grp")

    def shards_square(source_embed, target_embed, target_init, source_logw, target_logw):
        rows, depth = source_embed.shape
        width = target_embed.shape[0]
        half = width // 2
        factor = inverse_eps * LOG2E / math.sqrt(depth)
        vmem, hbm = pl.BlockSpec(memory_space=pltpu.VMEM), pl.BlockSpec(memory_space=pltpu.HBM)
        params = pltpu.CompilerParams(vmem_limit_bytes=16 * 1024 * 1024)

        def values(*shape):
            return jax.ShapeDtypeStruct(shape, jnp.float32)

        def cost(targets, sweeps):
            return pl.CostEstimate(
                flops=2 * rows * targets * depth + 16 * sweeps * rows * blk * width,
                transcendentals=2 * sweeps * rows * blk * width,
                bytes_accessed=2 * (rows + targets) * depth,
            )

        def along(array, turn):
            return lax.ppermute(
                array, "blk", [(i ^ neighbour_step(i, turn), i) for i in range(blk)]
            )

        def to_sibling(array):
            return fetch(array, "blk", 1, blk)

        def exchange(message):
            order = list(range(blk * grp))[::-1]
            return lax.all_to_all(message, ("blk", "grp"), 0, 0, axis_index_groups=[order])

        def block_of(size):
            return jax.ShapeDtypeStruct((size, depth), target_embed.dtype)

        def in_hbm(*arrays):
            return [pltpu.with_memory_space_constraint(each, pltpu.HBM) for each in arrays]

        first, second, whole, small = pl.pallas_call(
            head_kernel,
            out_shape=(
                block_of(half + SPARE),
                block_of(half),
                block_of(width + SPARE),
                values(2, width),
            ),
            in_specs=[hbm] * 3,
            out_specs=(vmem,) * 4,
            scratch_shapes=[
                pltpu.VMEM((1, width), jnp.float32),
                pltpu.VMEM((1, width), jnp.float32),
                pltpu.SemaphoreType.DMA((3,)),
            ],
            compiler_params=params,
        )(*in_hbm(target_embed, target_init.reshape(1, width), target_logw.reshape(1, width)))
        a_first = along(first, 0)
        b_second = along(second, 1)
        a_second = along(second, 0)
        b_first = along(first, 1)
        far_a = along(a_first, 1)
        far_b = along(b_second, 0)
        source, logw, passed = pl.pallas_call(
            source_kernel,
            out_shape=(
                jax.ShapeDtypeStruct((rows, depth), source_embed.dtype),
                values(rows, LANES),
                block_of(width + SPARE),
            ),
            in_specs=[hbm] * 2 + [vmem],
            out_specs=(vmem,) * 3,
            scratch_shapes=[pltpu.VMEM((1, rows), jnp.float32), pltpu.SemaphoreType.DMA((2,))],
            compiler_params=params,
        )(*in_hbm(source_embed, source_logw.reshape(1, rows)), whole)
        near = (a_first, a_second, b_first, b_second)
        sibling = pl.pallas_call(
            sibling_kernel,
            out_shape=block_of(3 * (width + SPARE)),
            in_specs=[vmem] * 5,
            out_specs=vmem,
            compiler_params=params,
            cost_estimate=cost(0, 0),
        )(passed, *near)
        sibling = to_sibling(sibling)

        def table():
            return values(2, SUBLANES, width)

        def scores_of(kernel, blocks, pieces, extra=()):
            return pl.pallas_call(
                functools.partial(kernel, factor),
                out_shape=(values(rows, blocks * width), table(), *extra),
                in_specs=[vmem] * (1 + len(pieces)),
                out_specs=(vmem,) * (2 + len(extra)),
                scratch_shapes=[pltpu.VMEM((blocks * width, depth), target_embed.dtype)],
                compiler_params=params,
                cost_estimate=cost(0, 0),
            )(source, *pieces)

        own = scores_of(own_kernel, 3, (whole, *near))

        def passed_on(message, tie, weight):
            return pl.pallas_call(
                pass_kernel,
                out_shape=jax.ShapeDtypeStruct(message.shape, message.dtype),
                in_specs=[vmem] * 2,
                out_specs=vmem,
                compiler_params=params,
                cost_estimate=cost(weight * width, 0),
            )(message, tie)

        sibling_a = to_sibling(passed_on(far_a, own[1], 0))
        sibling_b = to_sibling(passed_on(far_b, own[1], 50))
        *other, found = scores_of(
            sibling_scores_kernel, 3, (sibling, own[0]), (values(rows, LANES),)
        )
        far = scores_of(far_kernel, 2, (far_a, far_b, sibling_a, sibling_b, other[0]))
        scores = (*own, *other, *far)
        row_scratch = pltpu.VMEM((rows, LANES), jnp.float32)
        block_scratch = pltpu.VMEM((blk, width), jnp.float32)
        message = pl.pallas_call(
            first_kernel,
            out_shape=values(blk * grp, blk, width),
            in_specs=[vmem] * 8,
            out_specs=vmem,
            scratch_shapes=[row_scratch, block_scratch],
            compiler_params=params,
            cost_estimate=cost(0, 1),
        )(*scores, found, logw)
        got = exchange(message)
        row, message = pl.pallas_call(
            functools.partial(second_kernel, grp),
            out_shape=(values(1, rows), values(blk * grp, width)),
            in_specs=[vmem] * 8,
            out_specs=(vmem, vmem),
            scratch_shapes=[row_scratch, block_scratch],
            compiler_params=params,
            cost_estimate=cost(0, 1),
        )(*scores, got, logw)
        got = exchange(message)
        row_pot, column_pot = pl.pallas_call(
            last_kernel,
            out_shape=(values(1, rows), values(1, width)),
            in_specs=[vmem] * 3,
            out_specs=(vmem, vmem),
            compiler_params=params,
        )(got, small, row)
        return row_pot.reshape(rows), column_pot.reshape(width)

    def shards_any(source_embed, target_embed, target_init, source_logw, target_logw):
        width, depth = target_embed.shape
        factor = -1.0 / math.sqrt(depth)
        me = lax.axis_index("chip") * 2 + lax.axis_index("core")

        def swap_order(values):
            parts = values.reshape(blk, width)
            step = 1
            while step < blk:
                pairs = parts.reshape(blk // (2 * step), 2, step, width)
                pairs = jnp.where(me & step, pairs[:, ::-1], pairs)
                parts = pairs.reshape(blk, width)
                step *= 2
            return parts

        small = jnp.stack([target_init, target_logw])
        targets, smalls = gather_any(target_embed, small, chips)
        cost = (
            lax.dot_general(
                source_embed, targets, (((1,), (1,)), ((), ())), preferred_element_type=jnp.float32
            )
            * factor
        )
        column_pot, logw_all = smalls[:, 0].reshape(-1), smalls[:, 1].reshape(-1)
        for iteration in range(ITERS):
            scores = (column_pot[None, :] - cost) * inverse_eps
            row_top = jnp.max(scores, axis=1)
            row_sum = jnp.sum(jnp.exp(scores - row_top[:, None]), axis=1)
            row_pot = epsilon * source_logw - epsilon * (row_top + jnp.log(row_sum))
            part = swap_order(lse((row_pot[:, None] - cost) * inverse_eps))
            if iteration < ITERS - 1:
                copies = jnp.broadcast_to(part[None], (blk * grp, blk, width))
                got = lax.all_to_all(copies, everyone, 0, 0)
                total = swap_order(lse(got)).reshape(-1)
                column_pot = epsilon * logw_all - epsilon * total
            else:
                copies = jnp.broadcast_to(part[:, None], (blk, grp, width)).reshape(blk * grp, width)
                got = lax.all_to_all(copies, everyone, 0, 0)
                own_column = epsilon * target_logw - epsilon * lse(got)
        return row_pot, own_column

    if chips == 4:
        shards = shards_square
        rows_spec, blk_spec = P(("blk", "grp")), P("blk")
    else:
        shards = shards_any
        rows_spec, blk_spec = P(everyone), P(("chip", "core"))
        mesh = Mesh(mesh.devices.reshape(chips, 2, grp), everyone)
    in_specs = (rows_spec, blk_spec, blk_spec, rows_spec, blk_spec)
    out_specs = (rows_spec, blk_spec)
    return jax.shard_map(shards, mesh=mesh, in_specs=in_specs, out_specs=out_specs, check_vma=False)
```
